32 devices in a mesh: dp: 4 (over z), expert: 4 (over y, x), tensor: 2 (over core).
Axes of the slice: x: 2, y: 2, z: 4, core: 2. Of those that a mesh axis runs over, the one named last changes fastest.
Arguments:
- tokens: bfloat16 [4096, 2048], P(('dp', 'expert')), may hold values from -6 to 6
- segments: int32 [4096], P(('dp', 'expert')), may hold values from 0 to 2, as said below
- routes: int32 [4096, 4], P(('dp', 'expert')), may hold values from 0 to 7, all different within a row; in each aligned block of 256 rows (0 to 255, 256 to 511, ...) at most 192 rows name the same one
- attn_gain: bfloat16 [2048], replicated, may hold values from 0.5 to 1.5
- query_weight: bfloat16 [2048, 2048], P(None, 'tensor'), may hold values from -0.125 to 0.125
- query_bias: bfloat16 [16, 128], P('tensor'), may hold values from -1 to 1
- key_weight: bfloat16 [2048, 2048], P(None, 'tensor'), may hold values from -0.125 to 0.125
- key_bias: bfloat16 [16, 128], P('tensor'), may hold values from -1 to 1
- value_weight: bfloat16 [2048, 2048], P(None, 'tensor'), may hold values from -0.125 to 0.125
- value_bias: bfloat16 [16, 128], P('tensor'), may hold values from -1 to 1
- out_weight: bfloat16 [2048, 2048], P('tensor'), may hold values from -0.5 to 0.5
- mlp_gain: bfloat16 [2048], replicated, may hold values from 0.5 to 1.5
- router_weight: bfloat16 [2048, 8], replicated, may hold values from -0.0625 to 0.0625
- shared_router: bfloat16 [2048], replicated, may hold values from -0.125 to 0.125
- shared_gate: bfloat16 [2048, 5632], P(None, 'tensor'), may hold values from -0.125 to 0.125
- shared_up: bfloat16 [2048, 5632], P(None, 'tensor'), may hold values from -0.125 to 0.125
- shared_down: bfloat16 [5632, 2048], P('tensor'), may hold values from -0.15625 to 0.15625
- expert_gate: bfloat16 [8, 2048, 1408], P('expert', None, 'tensor'), may hold values from -0.125 to 0.125
- expert_up: bfloat16 [8, 2048, 1408], P('expert', None, 'tensor'), may hold values from -0.125 to 0.125
- expert_down: bfloat16 [8, 1408, 2048], P('expert', 'tensor'), may hold values from -0.625 to 0.625
- grad_out: bfloat16 [4096, 2048], P(('dp', 'expert')), may hold values from -6 to 6
Outputs:
- out: bfloat16 [4096, 2048], P(('dp', 'expert'))
- grad_tokens: float32 [4096, 2048], P(('dp', 'expert'))
- grad_attn_gain: float32 [2048], P(('dp', 'expert'))
- grad_query_weight: float32 [2048, 2048], P(('dp', 'expert'), 'tensor')
- grad_query_bias: float32 [16, 128], P('tensor', ('dp', 'expert'))
- grad_key_weight: float32 [2048, 2048], P(('dp', 'expert'), 'tensor')
- grad_key_bias: float32 [16, 128], P('tensor', ('dp', 'expert'))
- grad_value_weight: float32 [2048, 2048], P(('dp', 'expert'), 'tensor')
- grad_value_bias: float32 [16, 128], P('tensor', ('dp', 'expert'))
- grad_out_weight: float32 [2048, 2048], P('tensor', ('dp', 'expert'))
- grad_mlp_gain: float32 [2048], P(('dp', 'expert'))
- grad_router_weight: float32 [2048, 8], P(('dp', 'expert'))
- grad_shared_router: float32 [2048], P(('dp', 'expert'))
- grad_shared_gate: float32 [2048, 5632], P(('dp', 'expert'), 'tensor')
- grad_shared_up: float32 [2048, 5632], P(('dp', 'expert'), 'tensor')
- grad_shared_down: float32 [5632, 2048], P('tensor', ('dp', 'expert'))
- grad_expert_gate: float32 [8, 2048, 1408], P('expert', 'dp', 'tensor')
- grad_expert_up: float32 [8, 2048, 1408], P('expert', 'dp', 'tensor')
- grad_expert_down: float32 [8, 1408, 2048], P('expert', 'tensor', 'dp')
The draws below stay inside these ranges and needn't reach their ends.
Inputs may be any that keep to these rules, and one draw needn't show every extreme that they name: `segments`: segment numbers never fall; every aligned run of 4096 tokens holds three whole documents of its own, and the middle one covers at least three quarters of the run. `routes`: each token names 4 different experts; among the tokens of one device (aligned blocks of 256 rows) no expert is named more than 192 times, a bound that some block reaches.
All inputs are finite; a program needn't handle non-finite values.
Results may differ from the reference program's by a relative error of at most 0.023.
Values may be sent and summed in bfloat16 or wider, within the bound.
No kernel may reach another device: no remote copies, remote signals or barrier semaphores. Data moves between devices by JAX's collectives and lax.ppermute only.
A program may use at most 384 MiB of HBM per device.

```python
import math
import jax
import jax.numpy as jnp
import numpy as np
from jax import lax

D = 2048
HD = 128
HEADS = 16
H = 1408
FS = 5632
TOPK = 4
E = 8
TOK_DEV = 256
SEQ_LEN = 4096
WINDOW = 1024
TOKENS = 4096
CAP = 192


def draw_segments(key, part):
    key = jax.random.fold_in(key, 11)
    seq_count = TOKENS // SEQ_LEN
    first_key, second_key = jax.random.split(key)
    tail_len = SEQ_LEN // 8
    first_cut = jax.random.randint(first_key, (seq_count, 1), 1, tail_len + 1)
    second_cut = SEQ_LEN - jax.random.randint(second_key, (seq_count, 1), 1, tail_len + 1)
    places = jnp.arange(SEQ_LEN, dtype=jnp.int32)[None, :]
    numbers = 3 * jnp.arange(seq_count, dtype=jnp.int32)[:, None] + (places >= first_cut).astype(jnp.int32) + (places >= second_cut).astype(jnp.int32)
    return numbers.reshape(TOKENS)


def levels(stream_key, extent, pieces, smallest, high):
    gain, own = 1.0, jax.random.fold_in(stream_key, 6)
    for axis_at, shards_of in pieces:
        steps = jnp.exp(jax.random.uniform(jax.random.fold_in(own, axis_at), (shards_of,), jnp.float32, smallest / len(pieces), high / len(pieces)))
        gain = gain * jnp.repeat(steps, extent[axis_at] // shards_of).reshape([-1 if axis == axis_at else 1 for axis in range(len(extent))])
    return gain


def assign_block(rng, own, number, rows, count, top, bound, slope):
    order = jax.random.permutation(rng, count)
    heavy_load, ordinary = load_shares(count, rows * top, bound, slope, True), load_shares(count, rows * top, bound, slope, False)
    places = jnp.arange(count)

    def named(tallies, turn):
        used = int((tallies > 0).sum())
        fixed = max(1, used // 4)
        moved = fixed + (places - fixed + turn * (used - fixed)) % max(1, count - fixed)
        return jnp.zeros((count,), jnp.int32).at[order[jnp.where(places < fixed, places, moved)]].set(jnp.asarray(tallies, jnp.int32))

    tallies = jnp.where(number % 4 == 0, named(heavy_load, number // 4), named(ordinary, number - number // 4 - 1))
    mixed = jax.random.permutation(jax.random.fold_in(own, 3), count)
    source_of, taker = mixed[0:count // 2 * 2:2], mixed[1:count // 2 * 2:2]
    margin = jnp.minimum(tallies[source_of] - 1, bound - tallies[taker]) // 2
    margin = jnp.where((source_of == order[0]) | (taker == order[0]) | (tallies[taker] == 0), 0, jnp.maximum(margin, 0))
    moved = jax.random.randint(jax.random.fold_in(own, 4), (count // 2,), 0, 1 << 20) % (margin + 1)
    tallies = tallies.at[source_of].add(-moved).at[taker].add(moved)
    members = jnp.searchsorted(jnp.cumsum(tallies), jnp.arange(rows * top), side="right").astype(jnp.int32)
    grid = members.reshape(top, rows).T
    grid = grid[jax.random.permutation(jax.random.fold_in(own, 1), rows)]
    turn = jax.random.randint(jax.random.fold_in(own, 2), (rows, 1), 0, top)
    return jnp.take_along_axis(grid, (jnp.arange(top)[None, :] + turn) % top, axis=1)


def load_shares(count, total, most, slope, full):
    loads = [(1 << 20) // math.isqrt(standing ** slope) + 1 for standing in range(1, count + 1)]
    largest = most if full else min(most, max(-(-total // count), total * loads[0] // sum(loads)))
    least = 1 if total - largest >= count - 1 else 0
    counts, spare = [largest] + [least] * (count - 1), total - largest - least * (count - 1)
    while spare > 0:
        candidates = [i for i in range(1, count) if counts[i] < largest] or [i for i in range(1, count) if counts[i] < most]
        whole, left = sum([loads[i] for i in candidates]), spare
        for i in candidates:
            extra = min(most - counts[i], max(1, left * loads[i] // whole), spare)
            counts[i] = counts[i] + extra
            spare = spare - extra
    return np.array(counts)


def noise(key, shape, scale, limit, pieces=(), kind=jnp.bfloat16):
    array = jax.random.normal(key, shape, jnp.float32) * scale
    if len(pieces) > 0:
        array = levels(key, shape, pieces, -0.22, 0.18) * array
    return jnp.clip(array, min=-limit, max=limit).astype(kind)


def setup_inputs(seed: int = 0) -> dict:
    seeds = jax.random.split(jax.random.key(seed), 22)
    tokens = noise(seeds[0], (TOKENS, D), 1.0, 6.0, ((0, 16),))
    segments = draw_segments(jax.random.fold_in(seeds[21], 71), 0)
    routes_keys = jax.random.split(jax.random.fold_in(seeds[2], 1), TOKENS // TOK_DEV)
    routes_turns = jax.random.permutation(jax.random.fold_in(seeds[2], 3), TOKENS // TOK_DEV)
    routes = jax.vmap(lambda own, number: assign_block(jax.random.fold_in(seeds[2], 2), own, number, TOK_DEV, E, TOPK, CAP, 1))(routes_keys, routes_turns).reshape((TOKENS, TOPK))
    attn_gain = jnp.clip(1.0 + 0.1 * jax.random.normal(seeds[3], (D,), jnp.float32), 0.5, 1.5).astype(jnp.bfloat16)
    query_weight = noise(seeds[4], (D, D), D ** -0.5, 0.125, ((1, 2),))
    query_bias = noise(seeds[5], (HEADS, HD), 0.2, 1.0, ((0, 2),))
    key_weight = noise(seeds[6], (D, D), D ** -0.5, 0.125, ((1, 2),))
    key_bias = noise(seeds[7], (HEADS, HD), 0.2, 1.0, ((0, 2),))
    value_weight = noise(seeds[8], (D, D), D ** -0.5, 0.125, ((1, 2),))
    value_bias = noise(seeds[9], (HEADS, HD), 0.2, 1.0, ((0, 2),))
    out_weight = noise(seeds[10], (D, D), (D // 16) ** -0.5, 0.5, ((0, 2),))
    mlp_gain = jnp.clip(1.0 + 0.1 * jax.random.normal(seeds[11], (D,), jnp.float32), 0.5, 1.5).astype(jnp.bfloat16)
    router_weight = noise(seeds[12], (D, E), (4 * D) ** -0.5, 0.0625)
    shared_router = noise(seeds[13], (D,), D ** -0.5, 0.125)
    shared_gate = noise(seeds[14], (D, FS), D ** -0.5, 0.125, ((1, 2),))
    shared_up = noise(seeds[15], (D, FS), D ** -0.5, 0.125, ((1, 2),))
    shared_down = noise(seeds[16], (FS, D), (FS // 4) ** -0.5, 0.15625, ((0, 2),))
    expert_gate = noise(seeds[17], (E, D, H), D ** -0.5, 0.125, ((0, 4), (2, 2)))
    expert_up = noise(seeds[18], (E, D, H), D ** -0.5, 0.125, ((0, 4), (2, 2)))
    expert_down = noise(seeds[19], (E, H, D), (H // 16) ** -0.5, 0.625, ((0, 4), (1, 2)))
    grad_out = noise(seeds[20], (TOKENS, D), 1.0, 6.0, ((0, 16),))
    return dict(tokens=tokens, segments=segments, routes=routes, attn_gain=attn_gain, query_weight=query_weight, query_bias=query_bias, key_weight=key_weight, key_bias=key_bias, value_weight=value_weight, value_bias=value_bias, out_weight=out_weight, mlp_gain=mlp_gain, router_weight=router_weight, shared_router=shared_router, shared_gate=shared_gate, shared_up=shared_up, shared_down=shared_down, expert_gate=expert_gate, expert_up=expert_up, expert_down=expert_down, grad_out=grad_out)


EPS = 1e-06
THETA = 1000000.0
HIGHEST = lax.Precision.HIGHEST

@jax.custom_vjp
def low(v):
    return lax.optimization_barrier(v.astype(jnp.bfloat16)).astype(jnp.float32)

@jax.custom_vjp
def low_back(v):
    return v

def low_keep(v):
    return (low(v), None)

def low_pass(kept, grad):
    return (grad,)

def back_keep(v):
    return (v, None)

def back_low(kept, grad):
    return (low(grad),)
low.defvjp(low_keep, low_pass)
low_back.defvjp(back_keep, back_low)

def matmul(left, right):
    return jnp.dot(left, right, precision=HIGHEST, preferred_element_type=jnp.float32)

def rms_norm(values, gain_vec):
    return values * lax.rsqrt(lax.optimization_barrier(jnp.mean(values * values, axis=-1, keepdims=True)) + EPS) * gain_vec

def rotate(values, cosine, sine_table):
    half_dim = HD // 2
    first_half = values[..., :half_dim]
    second_half = values[..., half_dim:]
    cosine = cosine[:, None, :]
    sine_table = sine_table[:, None, :]
    return jnp.concatenate([first_half * cosine - second_half * sine_table, second_half * cosine + first_half * sine_table], axis=-1)

def rope_tables():
    places = jnp.arange(SEQ_LEN, dtype=jnp.float32)
    frequency = THETA ** (-2.0 * jnp.arange(HD // 2, dtype=jnp.float32) / HD)
    angles = places[:, None] * frequency[None, :]
    return (jnp.cos(angles), jnp.sin(angles))

def attend(query_rot, key_rot, value_low, seg_ids):
    block_rows = min(512, SEQ_LEN)
    score_scale = HD ** (-0.5)
    key_padded = jnp.pad(key_rot, ((WINDOW, 0), (0, 0), (0, 0)))
    value_padded = jnp.pad(value_low, ((WINDOW, 0), (0, 0), (0, 0)))
    seg_padded = jnp.pad(seg_ids, (WINDOW, 0), constant_values=-1)

    def one_block(start_row):
        query_block = lax.dynamic_slice_in_dim(query_rot, start_row, block_rows, 0)
        seg_query = lax.dynamic_slice_in_dim(seg_ids, start_row, block_rows, 0)
        key_block = lax.dynamic_slice_in_dim(key_padded, start_row, block_rows + WINDOW, 0)
        value_block = lax.dynamic_slice_in_dim(value_padded, start_row, block_rows + WINDOW, 0)
        seg_key = lax.dynamic_slice_in_dim(seg_padded, start_row, block_rows + WINDOW, 0)
        query_index = start_row + jnp.arange(block_rows, dtype=jnp.int32)
        key_index = start_row - WINDOW + jnp.arange(block_rows + WINDOW, dtype=jnp.int32)
        offsets = query_index[:, None] - key_index[None, :]
        allowed = (seg_query[:, None] == seg_key[None, :]) & (offsets >= 0) & (offsets < WINDOW)
        scores = low_back(jnp.einsum('qhd,khd->hqk', query_block, key_block, precision=HIGHEST) * score_scale)
        scores = jnp.where(allowed[None], scores, -1e+30)
        weights_soft = jax.nn.softmax(scores, axis=-1)
        return jnp.einsum('hqk,khd->qhd', low(weights_soft), value_block, precision=HIGHEST)
    starts = jnp.arange(SEQ_LEN // block_rows, dtype=jnp.int32) * block_rows
    blocks = lax.map(jax.checkpoint(one_block), starts)
    return blocks.reshape(SEQ_LEN, HEADS, HD)

def layer(params, hidden_in, seg_ids, route_ids):
    attn_gain, query_weight, query_bias, key_weight, key_bias, value_weight, value_bias, out_weight, mlp_gain, router_weight, shared_router, shared_gate, shared_up, shared_down, expert_gate, expert_up, expert_down = params
    cosine, sine_table = rope_tables()
    normed_one = low(rms_norm(hidden_in, attn_gain))
    query_pre = low_back(matmul(normed_one, query_weight) + query_bias.reshape(D))
    key_pre = low_back(matmul(normed_one, key_weight) + key_bias.reshape(D))
    value_low = low(low_back(matmul(normed_one, value_weight) + value_bias.reshape(D)))
    query_rot = low(rotate(query_pre.reshape(SEQ_LEN, HEADS, HD), cosine, sine_table))
    key_rot = low(rotate(key_pre.reshape(SEQ_LEN, HEADS, HD), cosine, sine_table))
    attended = attend(query_rot, key_rot, value_low.reshape(SEQ_LEN, HEADS, HD), seg_ids)
    attended = low(low_back(attended.reshape(SEQ_LEN, D)))
    after_attn = hidden_in + low_back(matmul(attended, out_weight))
    normed_two = low(rms_norm(after_attn, mlp_gain))
    router_logits = low_back(matmul(normed_two, router_weight))
    router_probs = jax.nn.softmax(router_logits, axis=-1)
    chosen = lax.optimization_barrier(jnp.sum((route_ids[:, :, None] == jnp.arange(E, dtype=jnp.int32)[None, None, :]).astype(jnp.float32), axis=1))
    combine = router_probs * chosen
    mixture = jnp.zeros((SEQ_LEN, D), jnp.float32)
    for expert in range(E):
        gate_val = low_back(matmul(normed_two, expert_gate[expert]))
        up_val = low_back(matmul(normed_two, expert_up[expert]))
        inner = low(jax.nn.silu(gate_val) * up_val)
        mixture = mixture + combine[:, expert:expert + 1] * low_back(matmul(inner, expert_down[expert]))
    shared_gate_val = low_back(matmul(normed_two, shared_gate))
    shared_up_val = low_back(matmul(normed_two, shared_up))
    shared_inner = low(jax.nn.silu(shared_gate_val) * shared_up_val)
    shared_logit = low_back(matmul(normed_two, shared_router[:, None]))
    mixture = mixture + jax.nn.sigmoid(shared_logit) * low_back(matmul(shared_inner, shared_down))
    return after_attn + mixture

def reference(tokens, segments, routes, attn_gain, query_weight, query_bias, key_weight, key_bias, value_weight, value_bias, out_weight, mlp_gain, router_weight, shared_router, shared_gate, shared_up, shared_down, expert_gate, expert_up, expert_down, grad_out):
    params = tuple((weight.astype(jnp.float32) for weight in (attn_gain, query_weight, query_bias, key_weight, key_bias, value_weight, value_bias, out_weight, mlp_gain, router_weight, shared_router, shared_gate, shared_up, shared_down, expert_gate, expert_up, expert_down)))
    seq_count = TOKENS // SEQ_LEN
    inputs = tokens.astype(jnp.float32).reshape(seq_count, SEQ_LEN, D)
    seg_blocks = segments.reshape(seq_count, SEQ_LEN)
    route_blocks = routes.reshape(seq_count, SEQ_LEN, TOPK)
    saved_layer = jax.checkpoint(layer)

    def forward(values, weights):

        def advance(carry, item):
            return (carry, saved_layer(weights, item[0], item[1], item[2]))
        _, result = lax.scan(advance, None, (values, seg_blocks, route_blocks))
        return result
    result, pullback = jax.vjp(forward, inputs, params)
    grad_in, grad_params = pullback(grad_out.astype(jnp.float32).reshape(seq_count, SEQ_LEN, D))
    grad_attn_gain, grad_query_weight, grad_query_bias, grad_key_weight, grad_key_bias, grad_value_weight, grad_value_bias, grad_out_weight, grad_mlp_gain, grad_router_weight, grad_shared_router, grad_shared_gate, grad_shared_up, grad_shared_down, grad_expert_gate, grad_expert_up, grad_expert_down = grad_params
    return (result.reshape(TOKENS, D).astype(jnp.bfloat16), grad_in.reshape(TOKENS, D), grad_attn_gain, grad_query_weight, grad_query_bias, grad_key_weight, grad_key_bias, grad_value_weight, grad_value_bias, grad_out_weight, grad_mlp_gain, grad_router_weight, grad_shared_router, grad_shared_gate, grad_shared_up, grad_shared_down, grad_expert_gate, grad_expert_up, grad_expert_down)
```

```python
import functools

import jax
import jax.numpy as jnp
from jax import lax
from jax.experimental import pallas as pl
from jax.experimental.pallas import tpu as pltpu
from jax.sharding import PartitionSpec as P

HD = 128
SEQ_LEN = 4096
WINDOW = 1024
EPS = 1e-06
THETA = 1000000.0
NEG_LARGE = -1e30
QUERY_BLOCK = 256
F32 = jnp.float32
BF16 = jnp.bfloat16


def dot(left, right):
    return jnp.dot(left, right, preferred_element_type=F32)


def dot_nt(left, right):
    return lax.dot_general(left, right, (((1,), (1,)), ((), ())), preferred_element_type=F32)


def dot_tn(left, right):
    return lax.dot_general(left, right, (((0,), (0,)), ((), ())), preferred_element_type=F32)


def shift_pairs(count, step):
    if count & (count - 1) == 0:
        return [(source, source ^ step) for source in range(count)]
    return [(source, (source + step) % count) for source in range(count)]


def partner(index, count, step):
    if count & (count - 1) == 0:
        return index ^ step
    return (index + step) % count


def source(index, count, step):
    if count & (count - 1) == 0:
        return index ^ step
    return (index - step + count) % count


def gather_plane(own):
    groups, cores = lax.axis_size("expert"), lax.axis_size("tensor")
    mine, core = lax.axis_index("expert"), lax.axis_index("tensor")
    rows, width = own.shape
    pieces = jnp.zeros((groups, rows, width), own.dtype)
    pieces = lax.dynamic_update_slice(pieces, own[None], (mine, 0, 0))
    for step in range(1, groups):
        came = lax.ppermute(own, "expert", shift_pairs(groups, step))
        pieces = lax.dynamic_update_slice(pieces, came[None], (source(mine, groups, step), 0, 0))
    whole = jnp.zeros((groups, cores, rows, width), own.dtype)
    whole = lax.dynamic_update_slice(whole, pieces[:, None], (0, core, 0, 0))
    for step in range(1, cores):
        came = lax.ppermute(pieces, "tensor", shift_pairs(cores, step))
        whole = lax.dynamic_update_slice(whole, came[:, None], (0, source(core, cores, step), 0, 0))
    return whole.reshape(groups * cores * rows, width)


def scatter_plane(partial):
    groups, cores = lax.axis_size("expert"), lax.axis_size("tensor")
    mine, core = lax.axis_index("expert"), lax.axis_index("tensor")
    total, width = partial.shape
    rows = total // (groups * cores)
    blocks = partial.reshape(groups, cores, rows, width)

    def of_core(index):
        return lax.dynamic_slice(blocks, (0, index, 0, 0), (groups, 1, rows, width))[:, 0]

    held = of_core(core).astype(F32)
    for step in range(1, cores):
        sent = of_core(partner(core, cores, step)).astype(BF16)
        held = held + lax.ppermute(sent, "tensor", shift_pairs(cores, step)).astype(F32)

    def of_group(index):
        return lax.dynamic_slice(held, (index, 0, 0), (1, rows, width))[0]

    result = of_group(mine)
    for step in range(1, groups):
        sent = of_group(partner(mine, groups, step)).astype(BF16)
        result = result + lax.ppermute(sent, "expert", shift_pairs(groups, step)).astype(F32)
    return result


def rotate(values, cosine, sine_table):
    rows, width = values.shape
    split = values.reshape(rows, width // HD, 2, HD // 2)
    first_half, second_half = split[:, :, 0], split[:, :, 1]
    cosine = cosine[:, None, :]
    sine_table = sine_table[:, None, :]
    return jnp.concatenate(
        [
            first_half * cosine - second_half * sine_table,
            second_half * cosine + first_half * sine_table,
        ],
        axis=-1,
    ).reshape(rows, width)


def norm_back(values, inv_scale, gain_vec, grad_normed):
    weighted = grad_normed * gain_vec
    inner_mean = jnp.mean(weighted * values, axis=-1, keepdims=True)
    return inv_scale * weighted - values * inv_scale * inv_scale * inv_scale * inner_mean


def masked_scores(query, keys, seg_query, seg_keys, offset):
    scores = dot_nt(query, keys) * (HD ** (-0.5))
    rows, columns = scores.shape
    distance = (
        lax.broadcasted_iota(jnp.int32, (rows, columns), 0)
        - lax.broadcasted_iota(jnp.int32, (rows, columns), 1)
        + offset
    )
    allowed = (seg_query == seg_keys) & (distance >= 0) & (distance < WINDOW)
    return jnp.where(allowed, scores, NEG_LARGE)


def key_ranges(start, block, rows):
    first_before = min(rows, max(0, (start + rows - WINDOW + 1) // block * block))
    first_own = max(0, (start - WINDOW + 1) // block * block)
    return (first_before, rows), (first_own, start + block)


def probabilities(query, parts, seg_query):
    scores = [masked_scores(query, keys, seg_query, seg_keys, offset) for keys, seg_keys, offset in parts]
    top = functools.reduce(jnp.maximum, [jnp.max(part, axis=-1, keepdims=True) for part in scores])
    expo = [jnp.exp(part - top) for part in scores]
    total = functools.reduce(jnp.add, [jnp.sum(part, axis=-1, keepdims=True) for part in expo])
    inverse = 1.0 / total
    return [part * inverse for part in expo]


def attend_kernel(block, q_ref, kb_ref, vb_ref, ko_ref, vo_ref, sq_ref, sb_ref, so_ref, out_ref):
    rows = q_ref.shape[0]
    for start in range(0, rows, block):
        (before, before_end), (own, own_end) = key_ranges(start, block, rows)
        parts, values = [], []
        if before < before_end:
            parts.append((kb_ref[before:before_end, :], sb_ref[:, before:before_end], start + rows - before))
            values.append(vb_ref[before:before_end, :])
        parts.append((ko_ref[own:own_end, :], so_ref[:, own:own_end], start - own))
        values.append(vo_ref[own:own_end, :])
        probs = probabilities(q_ref[start : start + block, :], parts, sq_ref[start : start + block, :])
        total = functools.reduce(
            jnp.add, [dot(part.astype(BF16), value) for part, value in zip(probs, values, strict=True)]
        )
        out_ref[start : start + block, :] = total.astype(BF16)


def attend_back_kernel(
    block,
    q_ref,
    kb_ref,
    vb_ref,
    ko_ref,
    vo_ref,
    sq_ref,
    sb_ref,
    so_ref,
    grad_ref,
    gq_ref,
    gkb_ref,
    gvb_ref,
    gko_ref,
    gvo_ref,
):
    rows = q_ref.shape[0]
    for ref in (gkb_ref, gvb_ref, gko_ref, gvo_ref):
        ref[...] = jnp.zeros_like(ref)
    scale = HD ** (-0.5)
    for start in range(0, rows, block):
        (before, before_end), (own, own_end) = key_ranges(start, block, rows)
        query = q_ref[start : start + block, :]
        grad = grad_ref[start : start + block, :]
        parts, values, sinks = [], [], []
        if before < before_end:
            parts.append((kb_ref[before:before_end, :], sb_ref[:, before:before_end], start + rows - before))
            values.append(vb_ref[before:before_end, :])
            sinks.append((gkb_ref, gvb_ref, before, before_end))
        parts.append((ko_ref[own:own_end, :], so_ref[:, own:own_end], start - own))
        values.append(vo_ref[own:own_end, :])
        sinks.append((gko_ref, gvo_ref, own, own_end))
        probs = probabilities(query, parts, sq_ref[start : start + block, :])
        grad_probs = [dot_nt(grad, value) for value in values]
        delta = functools.reduce(
            jnp.add,
            [jnp.sum(p * g, axis=-1, keepdims=True) for p, g in zip(probs, grad_probs, strict=True)],
        )
        grad_query = None
        for p, g, part, (gk_ref, gv_ref, low, high) in zip(probs, grad_probs, parts, sinks, strict=True):
            grad_scores = (p * (g - delta)).astype(BF16)
            term = dot(grad_scores, part[0])
            grad_query = term if grad_query is None else grad_query + term
            gk_ref[low:high, :] += dot_tn(grad_scores, query) * scale
            gv_ref[low:high, :] += dot_tn(p.astype(BF16), grad)
        gq_ref[start : start + block, :] = grad_query * scale


def attention_specs(rows, heads):
    column = pl.BlockSpec((rows, HD), lambda h: (0, h))
    value_column = pl.BlockSpec((rows, HD), lambda h: (0, heads + h))
    seg_rows = pl.BlockSpec((rows, 1), lambda h: (0, 0))
    seg_columns = pl.BlockSpec((1, rows), lambda h: (0, 0))
    return column, [column, column, value_column, column, value_column, seg_rows, seg_columns, seg_columns]


def attend(query, before, own, seg_rows, seg_before, seg_own):
    rows, width = query.shape
    heads = width // HD
    column, specs = attention_specs(rows, heads)
    return pl.pallas_call(
        functools.partial(attend_kernel, min(QUERY_BLOCK, rows)),
        grid=(heads,),
        in_specs=specs,
        out_specs=column,
        out_shape=jax.ShapeDtypeStruct((rows, width), BF16),
        compiler_params=pltpu.CompilerParams(vmem_limit_bytes=48 * 2**20),
        cost_estimate=pl.CostEstimate(
            flops=4 * rows * WINDOW * width, bytes_accessed=12 * rows * width, transcendentals=rows * WINDOW * heads
        ),
        name="attend",
    )(query, before, before, own, own, seg_rows, seg_before, seg_own)


def attend_back(query, before, own, seg_rows, seg_before, seg_own, grad_heads):
    rows, width = query.shape
    heads = width // HD
    column, specs = attention_specs(rows, heads)
    return pl.pallas_call(
        functools.partial(attend_back_kernel, min(QUERY_BLOCK, rows)),
        grid=(heads,),
        in_specs=specs + [column],
        out_specs=[column] * 5,
        out_shape=[jax.ShapeDtypeStruct((rows, width), F32)] * 5,
        compiler_params=pltpu.CompilerParams(vmem_limit_bytes=48 * 2**20),
        cost_estimate=pl.CostEstimate(
            flops=10 * rows * WINDOW * width, bytes_accessed=32 * rows * width, transcendentals=rows * WINDOW * heads
        ),
        name="attend_back",
    )(query, before, before, own, own, seg_rows, seg_before, seg_own, grad_heads)


def per_device(
    tokens,
    segments,
    routes,
    attn_gain,
    query_weight,
    query_bias,
    key_weight,
    key_bias,
    value_weight,
    value_bias,
    out_weight,
    mlp_gain,
    router_weight,
    shared_router,
    shared_gate,
    shared_up,
    shared_down,
    expert_gate,
    expert_up,
    expert_down,
    grad_out,
):
    tok_rows, model_width = tokens.shape
    groups, cores = lax.axis_size("expert"), lax.axis_size("tensor")
    planes = lax.axis_size("dp")
    mine, core, plane = lax.axis_index("expert"), lax.axis_index("tensor"), lax.axis_index("dp")
    rows = tok_rows // cores
    plane_rows = tok_rows * groups
    heads_here = query_weight.shape[1] // HD
    width = query_weight.shape[1] // groups
    heads = width // HD
    local_experts, _, hidden = expert_gate.shape
    expert_count = local_experts * groups
    shared_hidden = shared_gate.shape[1] // groups

    picks = jnp.sum(1 << routes, axis=1).astype(jnp.int32)
    facts = lax.all_gather(jnp.stack([segments, picks]), ("dp", "expert"), axis=1, tiled=True)
    facts_own = lax.dynamic_slice(facts, (0, plane * plane_rows), (2, plane_rows))
    seg_own = facts_own[:1]
    seg_before = lax.dynamic_slice(facts, (0, jnp.maximum(plane - 1, 0) * plane_rows), (1, plane_rows))
    seg_before = jnp.where(plane > 0, seg_before, -1)
    seg_rows = seg_own.reshape(plane_rows, 1)
    chosen = (facts_own[1][:, None] >> jnp.arange(expert_count, dtype=jnp.int32)[None, :]) & 1

    grad_top_plane = lax.all_gather(grad_out, "expert", axis=0, tiled=True)

    own_tokens = lax.dynamic_slice(tokens, (core * rows, 0), (rows, model_width))
    inputs = own_tokens.astype(F32)
    gain_one = attn_gain.astype(F32)
    scale_one = lax.rsqrt(jnp.mean(inputs * inputs, axis=-1, keepdims=True) + EPS)
    normed_one = gather_plane((inputs * scale_one * gain_one).astype(BF16))

    def columns(weight):
        return lax.dynamic_slice(weight, (0, mine * width), (model_width, width))

    def bias_of(bias):
        return lax.dynamic_slice(bias, (mine * heads, 0), (heads, HD)).reshape(1, width).astype(F32)

    weight_kv = jnp.concatenate([columns(key_weight), columns(value_weight)], axis=1)
    weight_q = columns(query_weight)
    row_index = plane * plane_rows + jnp.arange(plane_rows, dtype=jnp.int32)
    places = (row_index % SEQ_LEN).astype(F32)
    frequency = THETA ** (-2.0 * jnp.arange(HD // 2, dtype=F32) / HD)
    angles = places[:, None] * frequency[None, :]
    cosine = jnp.cos(angles)
    sine_table = jnp.sin(angles)
    kv_pre = dot(normed_one, weight_kv) + jnp.concatenate([bias_of(key_bias), bias_of(value_bias)], axis=1)
    own_kv = jnp.concatenate(
        [rotate(kv_pre[:, :width], cosine, sine_table).astype(BF16), kv_pre[:, width:].astype(BF16)], axis=1
    )
    before_kv = lax.ppermute(own_kv, "dp", [(i, i + 1) for i in range(planes - 1)])
    query_pre = dot(normed_one, weight_q) + bias_of(query_bias)
    query_rot = rotate(query_pre, cosine, sine_table).astype(BF16)
    attended = attend(query_rot, before_kv, own_kv, seg_rows, seg_before, seg_own)
    out_rows = lax.dynamic_slice(out_weight, (mine * width, 0), (width, model_width))
    after_attn = inputs + scatter_plane(dot(attended, out_rows))

    gain_two = mlp_gain.astype(F32)
    scale_two = lax.rsqrt(jnp.mean(after_attn * after_attn, axis=-1, keepdims=True) + EPS)
    normed_two = gather_plane((after_attn * scale_two * gain_two).astype(BF16))
    gate_columns = jnp.concatenate([router_weight, shared_router[:, None]], axis=1)
    small_logits = dot(normed_two, gate_columns)
    router_probs = jax.nn.softmax(small_logits[:, :expert_count], axis=-1)
    shared_mix = jax.nn.sigmoid(small_logits[:, expert_count:])
    combine = router_probs * chosen.astype(F32)
    own_gates = lax.dynamic_slice(combine, (0, mine * local_experts), (plane_rows, local_experts))

    def shared_columns(weight):
        return lax.dynamic_slice(weight, (0, mine * shared_hidden), (model_width, shared_hidden))

    shared_rows = lax.dynamic_slice(shared_down, (mine * shared_hidden, 0), (shared_hidden, model_width))
    segments_of_hidden = [
        (expert_gate[e], expert_up[e], expert_down[e], own_gates[:, e : e + 1]) for e in range(local_experts)
    ] + [(shared_columns(shared_gate), shared_columns(shared_up), shared_rows, shared_mix)]
    mixed_part, grad_normed_part = None, None
    gate_slopes, gate_grads, up_grads, down_grads = [], [], [], []
    for w_gate, w_up, w_down, gate in segments_of_hidden:
        gate_val = dot(normed_two, w_gate)
        up_val = dot(normed_two, w_up)
        inner_grad = dot_nt(grad_top_plane, w_down)
        sigmoid_val = jax.nn.sigmoid(gate_val)
        silu_val = gate_val * sigmoid_val
        inner = silu_val * up_val
        gate_slopes.append(jnp.sum(inner * inner_grad, axis=-1, keepdims=True))
        gated = (gate * inner).astype(BF16)
        inner_grad = gate * inner_grad
        grad_gate_val = (inner_grad * up_val * (sigmoid_val * (1.0 + gate_val * (1.0 - sigmoid_val)))).astype(BF16)
        grad_up_val = (inner_grad * silu_val).astype(BF16)
        term = dot(gated, w_down)
        mixed_part = term if mixed_part is None else mixed_part + term
        term = dot_nt(grad_gate_val, w_gate) + dot_nt(grad_up_val, w_up)
        grad_normed_part = term if grad_normed_part is None else grad_normed_part + term
        down_grads.append(dot_tn(gated, grad_top_plane).astype(BF16))
        gate_grads.append(dot_tn(normed_two, grad_gate_val).astype(BF16))
        up_grads.append(dot_tn(normed_two, grad_up_val).astype(BF16))

    slopes = jnp.concatenate(gate_slopes[:local_experts], axis=1)
    slopes = lax.dynamic_update_slice(
        jnp.zeros((plane_rows, expert_count), F32), slopes, (0, mine * local_experts)
    ) * chosen.astype(F32)
    grad_logits = router_probs * (slopes - jnp.sum(router_probs * slopes, axis=-1, keepdims=True))
    grad_shared_logit = gate_slopes[local_experts] * shared_mix * (1.0 - shared_mix)
    grad_small = jnp.concatenate([grad_logits, grad_shared_logit], axis=1).astype(BF16)
    grad_normed_part = grad_normed_part + dot_nt(grad_small, gate_columns)
    grad_columns = dot_tn(normed_two, grad_small)
    mixed_part = mixed_part.astype(BF16)
    mixed = lax.psum_scatter(mixed_part, ("expert", "tensor"), scatter_dimension=0, tiled=True)
    out_own = (after_attn + mixed.astype(F32)).astype(BF16)
    out = lax.all_gather(out_own, "tensor", axis=0, tiled=True)

    def summed_rows(pieces):
        return lax.psum_scatter(jnp.concatenate(pieces, axis=1), "dp", scatter_dimension=0, tiled=True)

    def shared_of_rows(values):
        part_rows = values.shape[0] // groups
        return (
            lax.all_to_all(values.reshape(groups, part_rows, shared_hidden), "expert", 0, 0)
            .transpose(1, 0, 2)
            .reshape(part_rows, groups * shared_hidden)
        )

    gate_sum = summed_rows(gate_grads)
    up_sum = summed_rows(up_grads)
    down_sum = lax.psum_scatter(jnp.concatenate(down_grads, axis=0), "dp", scatter_dimension=1, tiled=True)
    routed = local_experts * hidden
    part_rows = model_width // planes

    def expert_columns(values):
        return values[:, :routed].reshape(part_rows, local_experts, hidden).transpose(1, 0, 2).astype(F32)

    grad_expert_gate = expert_columns(gate_sum)
    grad_expert_up = expert_columns(up_sum)
    grad_expert_down = down_sum[:routed].reshape(local_experts, hidden, part_rows).astype(F32)
    grad_shared_gate = shared_of_rows(gate_sum[:, routed:]).astype(F32)
    grad_shared_up = shared_of_rows(up_sum[:, routed:]).astype(F32)
    grad_shared_down = lax.all_to_all(
        down_sum[routed:].reshape(shared_hidden, groups, part_rows // groups), "expert", 1, 0
    ).reshape(groups * shared_hidden, part_rows // groups).astype(F32)

    grad_top = lax.dynamic_slice(grad_out, (core * rows, 0), (rows, model_width)).astype(F32)
    grad_normed_two = scatter_plane(grad_normed_part)
    grad_mlp_gain = jnp.sum(grad_normed_two * after_attn * scale_two, axis=0)
    grad_after = grad_top + norm_back(after_attn, scale_two, gain_two, grad_normed_two)

    grad_attended = gather_plane(grad_after.astype(BF16))
    grad_heads = dot_nt(grad_attended, out_rows).astype(BF16)
    grad_out_part = dot_tn(attended, grad_attended).astype(BF16)
    grad_query_rot, back_keys, back_values, own_keys, own_values = attend_back(
        query_rot, before_kv, own_kv, seg_rows, seg_before, seg_own, grad_heads
    )
    back_kv = jnp.concatenate([back_keys, back_values], axis=1).astype(BF16)
    came_kv = lax.ppermute(back_kv, "dp", [(i + 1, i) for i in range(planes - 1)]).astype(F32)
    grad_query = rotate(grad_query_rot, cosine, -sine_table).astype(BF16)
    grad_key = rotate(own_keys + came_kv[:, :width], cosine, -sine_table).astype(BF16)
    grad_value = (own_values + came_kv[:, width:]).astype(BF16)
    grad_qkv = jnp.concatenate([grad_query, grad_key, grad_value], axis=1)
    weight_qkv = jnp.concatenate([weight_q, weight_kv], axis=1)
    grad_normed_one = scatter_plane(dot_nt(grad_qkv, weight_qkv))
    grad_attn_gain = jnp.sum(grad_normed_one * inputs * scale_one, axis=0)
    grad_own = grad_after + norm_back(inputs, scale_one, gain_one, grad_normed_one)
    grad_tokens = lax.all_gather(grad_own, "tensor", axis=0, tiled=True)

    grad_qkv_part = dot_tn(normed_one, grad_qkv).astype(BF16)
    qkv_sum = lax.psum_scatter(grad_qkv_part, "dp", scatter_dimension=0, tiled=True)
    qkv_rows = (
        lax.all_to_all(qkv_sum.reshape(groups, part_rows // groups, 3, width), "expert", 0, 0)
        .transpose(2, 1, 0, 3)
        .reshape(3, part_rows // groups, groups * width)
        .astype(F32)
    )
    out_sum = lax.psum_scatter(grad_out_part, "dp", scatter_dimension=1, tiled=True)
    grad_out_weight = lax.all_to_all(
        out_sum.reshape(width, groups, part_rows // groups), "expert", 1, 0
    ).reshape(groups * width, part_rows // groups).astype(F32)

    bias_sums = jnp.sum(grad_qkv, axis=0, dtype=F32).reshape(1, 3, heads, HD)
    bias_table = lax.dynamic_update_slice(
        jnp.zeros((cores, 3, heads_here, HD), F32), bias_sums, (core, 0, mine * heads, 0)
    )
    devices = planes * groups
    spread = jnp.concatenate(
        [
            grad_attn_gain.reshape(devices, -1),
            grad_mlp_gain.reshape(devices, -1),
            grad_columns.reshape(devices, -1),
            bias_table.reshape(cores * 3 * heads_here, devices, HD // devices).transpose(1, 0, 2).reshape(devices, -1),
        ],
        axis=1,
    )
    sums = lax.psum_scatter(lax.psum(spread, "tensor"), ("dp", "expert"), scatter_dimension=0, tiled=True)[0]
    gain_part = model_width // devices
    grad_attn_gain, grad_mlp_gain = sums[:gain_part], sums[gain_part : 2 * gain_part]
    table = sums[2 * gain_part :]
    column_size = gain_part * (expert_count + 1)
    column_sums = table[:column_size].reshape(gain_part, expert_count + 1)
    bias_sums = table[column_size:].reshape(cores, 3, heads_here, HD // devices)
    bias_sums = lax.dynamic_slice(bias_sums, (core, 0, 0, 0), (1, 3, heads_here, HD // devices))[0]
    return (
        out,
        grad_tokens,
        grad_attn_gain,
        qkv_rows[0],
        bias_sums[0],
        qkv_rows[1],
        bias_sums[1],
        qkv_rows[2],
        bias_sums[2],
        grad_out_weight,
        grad_mlp_gain,
        column_sums[:, :expert_count],
        column_sums[:, expert_count],
        grad_shared_gate,
        grad_shared_up,
        grad_shared_down,
        grad_expert_gate,
        grad_expert_up,
        grad_expert_down,
    )


def solution(mesh):
    tokens = ("dp", "expert")
    return jax.shard_map(
        per_device,
        mesh=mesh,
        in_specs=(
            P(tokens, None),
            P(tokens),
            P(tokens, None),
            P(),
            P(None, "tensor"),
            P("tensor", None),
            P(None, "tensor"),
            P("tensor", None),
            P(None, "tensor"),
            P("tensor", None),
            P("tensor", None),
            P(),
            P(),
            P(),
            P(None, "tensor"),
            P(None, "tensor"),
            P("tensor", None),
            P("expert", None, "tensor"),
            P("expert", None, "tensor"),
            P("expert", "tensor", None),
            P(tokens, None),
        ),
        out_specs=(
            P(tokens, None),
            P(tokens, None),
            P(tokens),
            P(tokens, "tensor"),
            P("tensor", tokens),
            P(tokens, "tensor"),
            P("tensor", tokens),
            P(tokens, "tensor"),
            P("tensor", tokens),
            P("tensor", tokens),
            P(tokens),
            P(tokens, None),
            P(tokens),
            P(tokens, "tensor"),
            P(tokens, "tensor"),
            P("tensor", tokens),
            P("expert", "dp", "tensor"),
            P("expert", "dp", "tensor"),
            P("expert", "tensor", "dp"),
        ),
        check_vma=False,
    )
```

```python
import functools

import jax
import jax.numpy as jnp
from jax import lax
from jax.experimental import pallas as pl
from jax.experimental.pallas import tpu as pltpu
from jax.sharding import PartitionSpec as P

HD = 128
SEQ_LEN = 4096
WINDOW = 1024
EPS = 1e-06
THETA = 1000000.0
NEG_LARGE = -1e30
QUERY_BLOCK = 256
FEED_BLOCK = 512
LANE = 128
FACT_ROWS = 16
GATHERED_PLANES = 4
F32 = jnp.float32
BF16 = jnp.bfloat16


def dot(left, right):
    return jnp.dot(left, right, preferred_element_type=F32)


def dot_nt(left, right):
    return lax.dot_general(left, right, (((1,), (1,)), ((), ())), preferred_element_type=F32)


def dot_tn(left, right):
    return lax.dot_general(left, right, (((0,), (0,)), ((), ())), preferred_element_type=F32)


def shift_pairs(count, step):
    if count & (count - 1) == 0:
        return [(source, source ^ step) for source in range(count)]
    return [(source, (source + step) % count) for source in range(count)]


def partner(index, count, step):
    if count & (count - 1) == 0:
        return index ^ step
    return (index + step) % count


def source(index, count, step):
    if count & (count - 1) == 0:
        return index ^ step
    return (index - step + count) % count


def joined(own, came, axis_name):
    core = lax.axis_index(axis_name)
    first = jnp.where(core == 0, own, came)
    second = jnp.where(core == 0, came, own)
    return jnp.concatenate([first, second], axis=0)


def gather_plane(own, meanwhile=()):
    groups, cores = lax.axis_size("expert"), lax.axis_size("tensor")
    mine, core = lax.axis_index("expert"), lax.axis_index("tensor")
    rows, width = own.shape
    pieces = jnp.zeros((groups * rows, width), own.dtype)
    pieces = lax.dynamic_update_slice(pieces, own, (mine * rows, 0))
    for step in range(1, groups):
        came = lax.ppermute(own, "expert", shift_pairs(groups, step))
        came = after(came, own, *meanwhile)
        pieces = lax.dynamic_update_slice(pieces, came, (source(mine, groups, step) * rows, 0))
    if cores == 2:
        return joined(pieces, lax.ppermute(pieces, "tensor", shift_pairs(cores, 1)), "tensor")
    return core_blocks(pieces)


def core_blocks(own):
    cores, core = lax.axis_size("tensor"), lax.axis_index("tensor")
    rows, width = own.shape
    whole = lax.dynamic_update_slice(jnp.zeros((cores * rows, width), own.dtype), own, (core * rows, 0))
    for step in range(1, cores):
        came = lax.ppermute(own, "tensor", shift_pairs(cores, step))
        whole = lax.dynamic_update_slice(whole, came, (source(core, cores, step) * rows, 0))
    return whole


def scatter_plane(partial_of_core, meanwhile=None):
    groups, cores = lax.axis_size("expert"), lax.axis_size("tensor")
    mine, core = lax.axis_index("expert"), lax.axis_index("tensor")
    sent = [partial_of_core(partner(core, cores, step)).astype(BF16) for step in range(1, cores)]
    came = [lax.ppermute(sent[step - 1], "tensor", shift_pairs(cores, step)) for step in range(1, cores)]
    held = functools.reduce(jnp.add, [part.astype(F32) for part in came], partial_of_core(core).astype(F32))
    rows, width = held.shape[0] // groups, held.shape[1]

    def of_group(index):
        return lax.dynamic_slice(held, (index * rows, 0), (rows, width))

    sent = [of_group(partner(mine, groups, step)).astype(BF16) for step in range(1, groups)]
    came = [lax.ppermute(sent[step - 1], "expert", shift_pairs(groups, step)) for step in range(1, groups)]
    result = of_group(mine)
    if meanwhile is None:
        return functools.reduce(jnp.add, [part.astype(F32) for part in came], result)
    side = meanwhile(tuple(sent))
    came = lax.optimization_barrier((tuple(came), side))[0]
    return functools.reduce(jnp.add, [part.astype(F32) for part in came], result), side


def after(value, *others):
    return lax.optimization_barrier((value, *others))[0]


def both_cores(own):
    if lax.axis_size("tensor") == 2:
        return joined(own, lax.ppermute(own, "tensor", shift_pairs(2, 1)), "tensor")
    return core_blocks(own)


def token_order(values, groups, cores):
    total, width = values.shape
    return values.reshape(cores, groups, -1, width).transpose(1, 0, 2, 3).reshape(total, width)


def core_order(values, groups, cores):
    total, width = values.shape
    return values.reshape(groups, cores, -1, width).transpose(1, 0, 2, 3).reshape(total, width)


def rotate(values, cosine, sine_table):
    rows, width = values.shape
    split = values.reshape(rows, width // HD, 2, HD // 2)
    first_half, second_half = split[:, :, 0], split[:, :, 1]
    cosine = cosine[:, None, :]
    sine_table = sine_table[:, None, :]
    return jnp.concatenate(
        [
            first_half * cosine - second_half * sine_table,
            second_half * cosine + first_half * sine_table,
        ],
        axis=-1,
    ).reshape(rows, width)


def norm_back(values, inv_scale, gain_vec, grad_normed):
    weighted = grad_normed * gain_vec
    inner_mean = jnp.mean(weighted * values, axis=-1, keepdims=True)
    return inv_scale * weighted - values * inv_scale * inv_scale * inv_scale * inner_mean


def masked_scores(query, keys, seg_query, seg_keys, offset):
    scores = dot_nt(query, keys) * (HD ** (-0.5))
    rows, columns = scores.shape
    distance = (
        lax.broadcasted_iota(jnp.int32, (rows, columns), 0)
        - lax.broadcasted_iota(jnp.int32, (rows, columns), 1)
        + offset
    )
    allowed = (seg_query == seg_keys) & (distance >= 0) & (distance < WINDOW)
    return jnp.where(allowed, scores, NEG_LARGE)


def key_ranges(start, block, rows):
    first_before = min(rows, max(0, (start + rows - WINDOW + 1) // block * block))
    first_own = max(0, (start - WINDOW + 1) // block * block)
    return (first_before, rows), (first_own, start + block)


def probabilities(query, parts, seg_query):
    scores = [masked_scores(query, keys, seg_query, seg_keys, offset) for keys, seg_keys, offset in parts]
    top = functools.reduce(jnp.maximum, [jnp.max(part, axis=-1, keepdims=True) for part in scores])
    expo = [jnp.exp(part - top) for part in scores]
    total = functools.reduce(jnp.add, [jnp.sum(part, axis=-1, keepdims=True) for part in expo])
    inverse = 1.0 / total
    return [part * inverse for part in expo]


def attend_kernel(block, q_ref, kb_ref, vb_ref, ko_ref, vo_ref, sq_ref, sb_ref, so_ref, out_ref):
    rows = q_ref.shape[0]
    for start in range(0, rows, block):
        (before, before_end), (own, own_end) = key_ranges(start, block, rows)
        parts, values = [], []
        if before < before_end:
            parts.append((kb_ref[before:before_end, :], sb_ref[:, before:before_end], start + rows - before))
            values.append(vb_ref[before:before_end, :])
        parts.append((ko_ref[own:own_end, :], so_ref[:, own:own_end], start - own))
        values.append(vo_ref[own:own_end, :])
        probs = probabilities(q_ref[start : start + block, :], parts, sq_ref[start : start + block, :])
        total = functools.reduce(
            jnp.add, [dot(part.astype(BF16), value) for part, value in zip(probs, values, strict=True)]
        )
        out_ref[start : start + block, :] = total.astype(BF16)


def attend_back_kernel(
    block,
    q_ref,
    kb_ref,
    vb_ref,
    ko_ref,
    vo_ref,
    sq_ref,
    sb_ref,
    so_ref,
    grad_ref,
    gq_ref,
    gkb_ref,
    gvb_ref,
    gko_ref,
    gvo_ref,
):
    rows = q_ref.shape[0]
    for ref in (gkb_ref, gvb_ref, gko_ref, gvo_ref):
        ref[...] = jnp.zeros_like(ref)
    scale = HD ** (-0.5)
    for start in range(0, rows, block):
        (before, before_end), (own, own_end) = key_ranges(start, block, rows)
        query = q_ref[start : start + block, :]
        grad = grad_ref[start : start + block, :]
        parts, values, sinks = [], [], []
        if before < before_end:
            parts.append((kb_ref[before:before_end, :], sb_ref[:, before:before_end], start + rows - before))
            values.append(vb_ref[before:before_end, :])
            sinks.append((gkb_ref, gvb_ref, before, before_end))
        parts.append((ko_ref[own:own_end, :], so_ref[:, own:own_end], start - own))
        values.append(vo_ref[own:own_end, :])
        sinks.append((gko_ref, gvo_ref, own, own_end))
        probs = probabilities(query, parts, sq_ref[start : start + block, :])
        grad_probs = [dot_nt(grad, value) for value in values]
        delta = functools.reduce(
            jnp.add,
            [jnp.sum(p * g, axis=-1, keepdims=True) for p, g in zip(probs, grad_probs, strict=True)],
        )
        grad_query = None
        for p, g, part, (gk_ref, gv_ref, low, high) in zip(probs, grad_probs, parts, sinks, strict=True):
            grad_scores = (p * (g - delta)).astype(BF16)
            term = dot(grad_scores, part[0])
            grad_query = term if grad_query is None else grad_query + term
            gk_ref[low:high, :] += dot_tn(grad_scores, query) * scale
            gv_ref[low:high, :] += dot_tn(p.astype(BF16), grad)
        gq_ref[start : start + block, :] = grad_query * scale


def attention_specs(rows, heads):
    column = pl.BlockSpec((rows, HD), lambda h: (0, h))
    value_column = pl.BlockSpec((rows, HD), lambda h: (0, heads + h))
    seg_rows = pl.BlockSpec((rows, 1), lambda h: (0, 0))
    seg_columns = pl.BlockSpec((1, rows), lambda h: (0, 0))
    return column, [column, column, value_column, column, value_column, seg_rows, seg_columns, seg_columns]


def attend(query, before, own, seg_rows, seg_before, seg_own):
    rows, width = query.shape
    heads = width // HD
    column, specs = attention_specs(rows, heads)
    return pl.pallas_call(
        functools.partial(attend_kernel, min(QUERY_BLOCK, rows)),
        grid=(heads,),
        in_specs=specs,
        out_specs=column,
        out_shape=jax.ShapeDtypeStruct((rows, width), BF16),
        compiler_params=pltpu.CompilerParams(vmem_limit_bytes=48 * 2**20),
        cost_estimate=pl.CostEstimate(
            flops=4 * rows * WINDOW * width, bytes_accessed=12 * rows * width, transcendentals=rows * WINDOW * heads
        ),
        name="attend",
    )(query, before, before, own, own, seg_rows, seg_before, seg_own)


def attend_back(query, before, own, seg_rows, seg_before, seg_own, grad_heads):
    rows, width = query.shape
    heads = width // HD
    column, specs = attention_specs(rows, heads)
    return pl.pallas_call(
        functools.partial(attend_back_kernel, min(QUERY_BLOCK, rows)),
        grid=(heads,),
        in_specs=specs + [column],
        out_specs=[column] * 5,
        out_shape=[jax.ShapeDtypeStruct((rows, width), F32)] * 5,
        compiler_params=pltpu.CompilerParams(vmem_limit_bytes=48 * 2**20),
        cost_estimate=pl.CostEstimate(
            flops=10 * rows * WINDOW * width, bytes_accessed=32 * rows * width, transcendentals=rows * WINDOW * heads
        ),
        name="attend_back",
    )(query, before, before, own, own, seg_rows, seg_before, seg_own, grad_heads)


def hidden_grads(rows, top, gate, weight_gu, weight_down):
    hidden = weight_down.shape[0]
    both = dot_nt(rows, weight_gu)
    inner_grad = dot_nt(top, weight_down)
    gate_val, up_val = both[:, :hidden], both[:, hidden:]
    sigmoid_val = jax.nn.sigmoid(gate_val)
    silu_val = gate_val * sigmoid_val
    inner = silu_val * up_val
    slope = jnp.sum(inner * inner_grad, axis=-1, keepdims=True)
    inner_grad = inner_grad * gate
    gated = (inner * gate).astype(BF16)
    grad_gate_val = (inner_grad * up_val * (sigmoid_val + silu_val * (1.0 - sigmoid_val))).astype(BF16)
    grad_up_val = (inner_grad * silu_val).astype(BF16)
    return gated, grad_gate_val, grad_up_val, slope


def gate_of(gates, block):
    lane = lax.broadcasted_iota(jnp.int32, gates.shape, 1)
    return jnp.sum(jnp.where(lane == block, gates, 0.0), axis=1, keepdims=True)


def feed_kernel(chunk_ref, rows_ref, top_ref, gates_ref, gu_ref, down_ref, gated_ref, grad_ref, slope_ref):
    del chunk_ref
    hidden = down_ref.shape[0]
    gate = gate_of(gates_ref[...], pl.program_id(0))
    gated, grad_gate_val, grad_up_val, slope = hidden_grads(
        rows_ref[...], top_ref[...], gate, gu_ref[...], down_ref[...]
    )
    gated_ref[...] = gated
    grad_ref[:, :hidden] = grad_gate_val
    grad_ref[:, hidden:] = grad_up_val
    slope_ref[0] = slope


def weight_kernel(
    routed,
    hidden_out,
    chunk_ref,
    rows_ref,
    top_ref,
    rows_t_ref,
    top_t_ref,
    gates_ref,
    gu_ref,
    down_ref,
    gu_in,
    down_in,
    *rest,
):
    del chunk_ref
    gate_out, up_out, down_out, gate_sum, up_sum, down_sum = rest[-6:]
    hidden = down_ref.shape[0]
    step = pl.program_id(0)

    @pl.when(step == 0)
    def _():
        gate_sum[...] = gu_in[:, :hidden]
        up_sum[...] = gu_in[:, hidden:]
        down_sum[...] = down_in[...]

    gate = gate_of(gates_ref[...], routed)
    gated, grad_gate_val, grad_up_val, _ = hidden_grads(
        rows_ref[...], top_ref[...], gate, gu_ref[...], down_ref[...]
    )
    gate_sum[...] += dot(rows_t_ref[...], grad_gate_val)
    up_sum[...] += dot(rows_t_ref[...], grad_up_val)
    down_sum[...] += dot(top_t_ref[...], gated)

    @pl.when(step == pl.num_programs(0) - 1)
    def _():
        if len(gate_out.shape) == 3 and gate_out.shape[0] == 1:
            gate_out[0] = gate_sum[...].T[:hidden_out]
            up_out[0] = up_sum[...].T[:hidden_out]
            down_out[0] = down_sum[...].T[:hidden_out]
        else:
            groups, part = gate_out.shape[:2]
            turned = down_sum[...].T.astype(BF16)
            for g in range(groups):
                gate_out[g] = gate_sum[g * part : (g + 1) * part, :].astype(BF16)
                up_out[g] = up_sum[g * part : (g + 1) * part, :].astype(BF16)
                down_out[g] = turned[:, g * part : (g + 1) * part]


def pack_kernel(local, hidden, units, window_ref, *refs):
    gate_ref, up_ref, down_ref = refs[:3]
    shared_gate, shared_up = refs[3 : 3 + units], refs[3 + units : 3 + 2 * units]
    shared_down = refs[3 + 2 * units : 3 + 3 * units]
    gu_out, down_out = refs[-2:]
    padded = units * LANE
    columns = down_out.shape[1]
    for e in range(local):
        for ref, out, at in ((gate_ref, gu_out, 2 * e), (up_ref, gu_out, 2 * e + 1), (down_ref, down_out, e)):
            out[at * padded : at * padded + hidden, :] = ref[e]
            if hidden < padded:
                out[at * padded + hidden : (at + 1) * padded, :] = jnp.zeros((padded - hidden, columns), BF16)
    skip = window_ref[1]
    for k in range(units):
        line = lax.broadcasted_iota(jnp.int32, (LANE, columns), 0) + k * LANE
        keep = (line >= skip) & (line < skip + hidden)
        for block, out, at in (
            (shared_gate[k][...].T, gu_out, 2 * local),
            (shared_up[k][...].T, gu_out, 2 * local + 1),
            (shared_down[k][...], down_out, local),
        ):
            out[at * padded + k * LANE : at * padded + (k + 1) * LANE, :] = jnp.where(
                keep, block.astype(F32), 0.0
            ).astype(BF16)


def pack_weights(window, expert_gate, expert_up, expert_down, shared_gate, shared_up, shared_down, padded):
    local, hidden, model_width = expert_down.shape
    units = padded // LANE
    blocks = local + 1
    tile = min(256, model_width)
    expert_spec = pl.BlockSpec((local, hidden, tile), lambda i, w: (0, 0, i))
    column_specs = [pl.BlockSpec((tile, LANE), lambda i, w, k=k: (i, w[0] + k)) for k in range(units)]
    row_specs = [pl.BlockSpec((LANE, tile), lambda i, w, k=k: (w[0] + k, i)) for k in range(units)]
    return pl.pallas_call(
        functools.partial(pack_kernel, local, hidden, units),
        grid_spec=pltpu.PrefetchScalarGridSpec(
            num_scalar_prefetch=1,
            grid=(model_width // tile,),
            in_specs=[expert_spec] * 3 + column_specs * 2 + row_specs,
            out_specs=[
                pl.BlockSpec((2 * blocks * padded, tile), lambda i, w: (0, i)),
                pl.BlockSpec((blocks * padded, tile), lambda i, w: (0, i)),
            ],
        ),
        out_shape=[
            jax.ShapeDtypeStruct((2 * blocks * padded, model_width), BF16),
            jax.ShapeDtypeStruct((blocks * padded, model_width), BF16),
        ],
        compiler_params=pltpu.CompilerParams(vmem_limit_bytes=40 * 2**20),
        cost_estimate=pl.CostEstimate(
            flops=0, bytes_accessed=12 * blocks * padded * model_width, transcendentals=0
        ),
        name="pack_weights",
    )(
        window,
        jnp.swapaxes(expert_gate, 1, 2),
        jnp.swapaxes(expert_up, 1, 2),
        expert_down,
        *([shared_gate] * units),
        *([shared_up] * units),
        *([shared_down] * units),
    )


def turn_kernel(plane_ref, part_ref, out_ref):
    del plane_ref
    out_ref[...] = part_ref[...].T


def turn_logits_kernel(plane_ref, part_ref, rows_ref, columns_ref, out_ref, logits_ref):
    del plane_ref
    out_ref[...] = part_ref[...].T
    logits_ref[...] = dot(rows_ref[...], columns_ref[...])


def turn(plane, values, part, columns=None):
    total, model_width = values.shape
    tile = min(512, total)
    specs = [pl.BlockSpec((tile, part), lambda i, p: (i, p[0]))]
    turned = pl.BlockSpec((part, tile), lambda i, p: (0, i))
    shape = jax.ShapeDtypeStruct((part, total), BF16)
    args, out_specs, shapes, kernel = [values], turned, shape, turn_kernel
    if columns is not None:
        specs += [
            pl.BlockSpec((tile, model_width), lambda i, p: (i, 0)),
            pl.BlockSpec(columns.shape, lambda i, p: (0, 0)),
        ]
        args += [values, columns]
        out_specs = [turned, pl.BlockSpec((tile, columns.shape[1]), lambda i, p: (i, 0))]
        shapes = [shape, jax.ShapeDtypeStruct((total, columns.shape[1]), F32)]
        kernel = turn_logits_kernel
    return pl.pallas_call(
        kernel,
        grid_spec=pltpu.PrefetchScalarGridSpec(
            num_scalar_prefetch=1, grid=(total // tile,), in_specs=specs, out_specs=out_specs
        ),
        out_shape=shapes,
        compiler_params=pltpu.CompilerParams(vmem_limit_bytes=40 * 2**20),
        cost_estimate=pl.CostEstimate(flops=0, bytes_accessed=2 * total * model_width, transcendentals=0),
        name="turn",
    )(plane, *args)


def feed(chunk, rows, top_all, gates, weight_gu, weight_down, blocks):
    count, model_width = rows.shape
    hidden = weight_down.shape[0] // blocks
    tile = min(FEED_BLOCK, count)
    steps = count // tile
    grid_spec = pltpu.PrefetchScalarGridSpec(
        num_scalar_prefetch=1,
        grid=(blocks, steps),
        in_specs=[
            pl.BlockSpec((tile, model_width), lambda s, i, c: (i, 0)),
            pl.BlockSpec((tile, model_width), lambda s, i, c: (c[0] * steps + i, 0)),
            pl.BlockSpec((tile, gates.shape[1]), lambda s, i, c: (i, 0)),
            pl.BlockSpec((2 * hidden, model_width), lambda s, i, c: (s, 0)),
            pl.BlockSpec((hidden, model_width), lambda s, i, c: (s, 0)),
        ],
        out_specs=[
            pl.BlockSpec((tile, hidden), lambda s, i, c: (i, s)),
            pl.BlockSpec((tile, 2 * hidden), lambda s, i, c: (i, s)),
            pl.BlockSpec((1, tile, 1), lambda s, i, c: (s, i, 0)),
        ],
    )
    return pl.pallas_call(
        feed_kernel,
        grid_spec=grid_spec,
        out_shape=[
            jax.ShapeDtypeStruct((count, blocks * hidden), BF16),
            jax.ShapeDtypeStruct((count, 2 * blocks * hidden), BF16),
            jax.ShapeDtypeStruct((blocks, count, 1), F32),
        ],
        compiler_params=pltpu.CompilerParams(vmem_limit_bytes=56 * 2**20),
        cost_estimate=pl.CostEstimate(
            flops=6 * count * model_width * hidden * blocks,
            bytes_accessed=6 * model_width * hidden * blocks + 4 * count * model_width * blocks,
            transcendentals=count * hidden * blocks,
        ),
        name="feed",
    )(chunk, rows, top_all, gates, weight_gu, weight_down)


def weight_grads(plane, planes, block, rows_all, top_all, rows_t, top_t, gates, packed, sums, outs, groups, hidden):
    weight_gu, weight_down = packed
    total, model_width = rows_all.shape
    count = total // planes
    part = rows_t.shape[0]
    padded = sums[1].shape[1]
    tile = min(FEED_BLOCK, count)
    steps = count // tile
    local = outs[0] if isinstance(outs[0], int) else outs[0].shape[0]

    def at(i, c):
        return lax.rem(c[0] + 1 + i // steps, planes) * steps + lax.rem(i, steps)

    tokens = pl.BlockSpec((tile, model_width), lambda i, c: (at(i, c), 0))
    turned = pl.BlockSpec((part, tile), lambda i, c: (0, at(i, c)))
    in_specs = [
        tokens,
        tokens,
        turned,
        turned,
        pl.BlockSpec((tile, gates.shape[1]), lambda i, c: (at(i, c), 0)),
        pl.BlockSpec((2 * padded, model_width), lambda i, c: (block, 0)),
        pl.BlockSpec((padded, model_width), lambda i, c: (block, 0)),
        pl.BlockSpec((part, 2 * padded), lambda i, c: (0, 0)),
        pl.BlockSpec((part, padded), lambda i, c: (0, 0)),
    ]
    args = [rows_all, top_all, rows_t, top_t, gates, weight_gu, weight_down, *sums]
    aliases = {}
    if block < local:
        out_shape = [jax.ShapeDtypeStruct((local, hidden, part), F32)] * 3
        out_specs = [pl.BlockSpec((1, hidden, part), lambda i, c: (block, 0, 0))] * 3
        if not isinstance(outs[0], int):
            in_specs += [pl.BlockSpec(memory_space=pl.ANY)] * 3
            aliases = {len(args) + 1 + k: k for k in range(3)}
            args += list(outs)
    else:
        wide = jax.ShapeDtypeStruct((groups, part // groups, padded), BF16)
        out_shape = [wide, wide, jax.ShapeDtypeStruct((groups, padded, part // groups), BF16)]
        out_specs = [
            pl.BlockSpec(shape.shape, lambda i, c: (0, 0, 0)) for shape in out_shape
        ]
    return pl.pallas_call(
        functools.partial(weight_kernel, block, hidden),
        grid_spec=pltpu.PrefetchScalarGridSpec(
            num_scalar_prefetch=1,
            grid=((planes - 1) * steps,),
            in_specs=in_specs,
            out_specs=out_specs,
            scratch_shapes=[pltpu.VMEM((part, padded), F32)] * 3,
        ),
        out_shape=out_shape,
        input_output_aliases=aliases,
        compiler_params=pltpu.CompilerParams(vmem_limit_bytes=62 * 2**20),
        cost_estimate=pl.CostEstimate(
            flops=6 * (total - count) * (model_width + part) * padded,
            bytes_accessed=6 * model_width * padded + 4 * total * model_width,
            transcendentals=total * padded,
        ),
        name="weight_grads",
    )(plane, *args)


def per_device(
    tokens,
    segments,
    routes,
    attn_gain,
    query_weight,
    query_bias,
    key_weight,
    key_bias,
    value_weight,
    value_bias,
    out_weight,
    mlp_gain,
    router_weight,
    shared_router,
    shared_gate,
    shared_up,
    shared_down,
    expert_gate,
    expert_up,
    expert_down,
    grad_out,
):
    tok_rows, model_width = tokens.shape
    groups, cores = lax.axis_size("expert"), lax.axis_size("tensor")
    planes = lax.axis_size("dp")
    mine, core, plane = lax.axis_index("expert"), lax.axis_index("tensor"), lax.axis_index("dp")
    rows = tok_rows // cores
    plane_rows = tok_rows * groups
    heads_here = query_weight.shape[1] // HD
    width = query_weight.shape[1] // groups
    heads = width // HD
    local_experts, _, hidden = expert_gate.shape
    expert_count = local_experts * groups
    blocks = local_experts + 1
    gathered = planes <= GATHERED_PLANES
    padded = -(-hidden // LANE) * LANE
    part_rows = model_width // planes

    def in_tokens(values):
        return token_order(values, groups, cores)

    def in_cores(values):
        return core_order(values, groups, cores)

    first_unit = mine * hidden // LANE
    window = jnp.stack([first_unit, mine * hidden - first_unit * LANE]).astype(jnp.int32)
    packed = pack_weights(window, expert_gate, expert_up, expert_down, shared_gate, shared_up, shared_down, padded)

    own_tokens = lax.dynamic_slice(tokens, (core * rows, 0), (rows, model_width))
    inputs = own_tokens.astype(F32)
    gain_one = attn_gain.astype(F32)
    scale_one = lax.rsqrt(jnp.mean(inputs * inputs, axis=-1, keepdims=True) + EPS)
    weight_gu, weight_down = packed
    normed_one = gather_plane((inputs * scale_one * gain_one).astype(BF16), (weight_gu, weight_down))
    grad_top_own = lax.dynamic_slice(grad_out, (core * rows, 0), (rows, model_width))
    picks = jnp.sum(1 << routes, axis=1)
    facts_own = jnp.zeros((FACT_ROWS, tok_rows), BF16)
    facts_own = facts_own.at[0].set(segments.astype(BF16)).at[1].set(picks.astype(BF16))
    facts = jnp.zeros((groups, FACT_ROWS, tok_rows), BF16)
    facts = lax.dynamic_update_slice(facts, facts_own[None], (mine, 0, 0))
    for step in range(1, groups):
        came = lax.ppermute(facts_own, "expert", shift_pairs(groups, step))
        facts = lax.dynamic_update_slice(facts, came[None], (source(mine, groups, step), 0, 0))
    facts = facts.transpose(1, 0, 2).reshape(FACT_ROWS, plane_rows)
    facts_all = jnp.zeros((planes, FACT_ROWS, plane_rows), BF16)
    facts_all = lax.dynamic_update_slice(facts_all, facts[None], (plane, 0, 0))
    seg_before = facts[:1]
    for step in range(1, planes):
        came = lax.ppermute(facts, "dp", [(i, (i + step) % planes) for i in range(planes)])
        if step == 1:
            seg_before = came[:1]
        facts_all = lax.dynamic_update_slice(facts_all, came[None], ((plane - step + planes) % planes, 0, 0))
    top_axes = ("dp", "tensor", "expert") if gathered else ("tensor", "expert")
    grad_top_all = lax.all_gather(grad_top_own, top_axes, axis=0, tiled=True)
    seg_own = facts[:1].astype(F32)
    seg_before = jnp.where(plane > 0, seg_before.astype(F32), -1.0)
    seg_rows = seg_own.reshape(plane_rows, 1)
    bits_all = (
        facts_all[:, 1].reshape(planes, groups, cores, rows).transpose(0, 2, 1, 3).reshape(-1, 1).astype(jnp.int32)
    )

    def columns(weight):
        return lax.dynamic_slice(weight, (0, mine * width), (model_width, width))

    def bias_of(bias):
        return lax.dynamic_slice(bias, (mine * heads, 0), (heads, HD)).reshape(1, width).astype(F32)

    weight_kv = jnp.concatenate([columns(key_weight), columns(value_weight)], axis=1)
    weight_q = columns(query_weight)
    row_index = plane * plane_rows + jnp.arange(plane_rows, dtype=jnp.int32)
    places = (row_index % SEQ_LEN).astype(F32)
    frequency = THETA ** (-2.0 * jnp.arange(HD // 2, dtype=F32) / HD)
    angles = places[:, None] * frequency[None, :]
    cosine = jnp.cos(angles)
    sine_table = jnp.sin(angles)
    kv_pre = in_tokens(
        dot(normed_one, weight_kv) + jnp.concatenate([bias_of(key_bias), bias_of(value_bias)], axis=1)
    )
    own_kv = jnp.concatenate(
        [rotate(kv_pre[:, :width], cosine, sine_table).astype(BF16), kv_pre[:, width:].astype(BF16)], axis=1
    )
    before_kv = after(lax.ppermute(own_kv, "dp", [(i, i + 1) for i in range(planes - 1)]), facts_all)
    query_pre = in_tokens(dot(normed_one, weight_q) + bias_of(query_bias))
    query_rot = rotate(query_pre, cosine, sine_table).astype(BF16)
    attended = in_cores(attend(query_rot, before_kv, own_kv, seg_rows, seg_before, seg_own))
    out_rows = lax.dynamic_slice(out_weight, (mine * width, 0), (width, model_width))
    half = plane_rows // cores

    def of_core(values, index):
        return lax.dynamic_slice(values, (index * half, 0), (half, values.shape[1]))

    after_attn = inputs + scatter_plane(lambda index: dot(of_core(attended, index), out_rows))

    gain_two = mlp_gain.astype(F32)
    scale_two = lax.rsqrt(jnp.mean(after_attn * after_attn, axis=-1, keepdims=True) + EPS)
    normed_own = (after_attn * scale_two * gain_two).astype(BF16)
    normed_two = gather_plane(normed_own)
    if gathered:
        normed_all = lax.all_gather(after(normed_own, normed_two), ("dp", "tensor", "expert"), axis=0, tiled=True)
    gate_columns = jnp.concatenate([router_weight, shared_router[:, None]], axis=1)

    def gates_from(logits, bits):
        router_probs = jax.nn.softmax(logits[:, :expert_count], axis=-1)
        shared_mix = jax.nn.sigmoid(logits[:, expert_count : expert_count + 1])
        chosen = ((bits >> jnp.arange(expert_count, dtype=jnp.int32)[None, :]) & 1).astype(F32)
        own = lax.dynamic_slice(router_probs * chosen, (0, mine * local_experts), (bits.shape[0], local_experts))
        return jnp.concatenate([own, shared_mix], axis=1), router_probs, chosen

    bits = lax.dynamic_slice(bits_all, (plane * plane_rows, 0), (plane_rows, 1))
    gates, router_probs, chosen = gates_from(dot(normed_two, gate_columns), bits)
    shared_mix = gates[:, local_experts:]
    plane_number = plane.reshape(1).astype(jnp.int32)
    top_chunk = plane_number if gathered else jnp.zeros_like(plane_number)
    gated, grad_hidden, slopes = feed(top_chunk, normed_two, grad_top_all, gates, weight_gu, weight_down, blocks)

    own_slopes = jnp.concatenate([slopes[e] for e in range(local_experts)], axis=1)
    all_slopes = lax.dynamic_update_slice(
        jnp.zeros((plane_rows, expert_count), F32), own_slopes, (0, mine * local_experts)
    ) * chosen
    grad_logits = router_probs * (all_slopes - jnp.sum(router_probs * all_slopes, axis=-1, keepdims=True))
    grad_shared_logit = slopes[local_experts] * shared_mix * (1.0 - shared_mix)
    grad_small = jnp.concatenate([grad_logits, grad_shared_logit], axis=1).astype(BF16)
    grad_normed_part = (dot(grad_hidden, weight_gu) + dot_nt(grad_small, gate_columns)).astype(BF16)
    own_part = lax.dynamic_slice(normed_two, (0, plane * part_rows), (plane_rows, part_rows))

    def mix_meanwhile(token):
        values, grads = after((gated, grad_hidden), token)
        mixed_part = dot(values, weight_down).astype(BF16)
        return mixed_part, dot_tn(own_part, grads[:, 2 * local_experts * padded :]) if gathered else ()

    grad_normed_two, (mixed_part, shared_sum) = scatter_plane(
        lambda index: of_core(grad_normed_part, index), mix_meanwhile
    )
    mixed = lax.psum_scatter(
        after(mixed_part, grad_normed_two), ("tensor", "expert"), scatter_dimension=0, tiled=True
    )
    out = both_cores((after_attn + mixed.astype(F32)).astype(BF16))
    grad_columns = dot_tn(normed_two, grad_small)

    grad_mlp_gain = jnp.sum(grad_normed_two * after_attn * scale_two, axis=0)
    grad_after = grad_top_own.astype(F32) + norm_back(after_attn, scale_two, gain_two, grad_normed_two)

    grad_sent = grad_after.astype(BF16)
    values, grads, top_all = after((gated, grad_hidden, grad_top_all), grad_sent)
    own_sums = []
    if gathered:
        top_t = turn(plane_number, top_all, part_rows)
        own_top_t = lax.dynamic_slice(top_t, (0, plane * plane_rows), (part_rows, plane_rows))
    for block in range(blocks if gathered else 0):
        if block < local_experts:
            gu_sum = dot_tn(own_part, grads[:, 2 * block * padded : 2 * (block + 1) * padded])
        else:
            gu_sum = shared_sum
        own_sums.append((gu_sum, dot(own_top_t, values[:, block * padded : (block + 1) * padded])))
    grad_attended = gather_plane(grad_sent, tuple(own_sums))
    grad_heads = in_tokens(dot_nt(grad_attended, out_rows).astype(BF16))
    grad_query_rot, back_keys, back_values, own_keys, own_values = attend_back(
        query_rot, before_kv, own_kv, seg_rows, seg_before, seg_own, grad_heads
    )
    back_kv = jnp.concatenate([back_keys, back_values], axis=1).astype(BF16)
    small_rows = part_rows // groups

    def to_owners(values):
        return lax.all_to_all(values, "expert", 0, 0)

    def placed(pieces, axis):
        total = None
        for j in range(groups):
            at = j * hidden // LANE * LANE
            pads = [(0, 0), (0, 0)]
            pads[axis] = (at, groups * hidden - at - padded)
            piece = jnp.pad(pieces[j].astype(F32), pads)
            total = piece if total is None else total + piece
        return total

    if gathered:
        wide_columns = jnp.concatenate(
            [gate_columns, jnp.zeros((model_width, LANE - expert_count - 1), BF16)], axis=1
        )
        normed_all = after(normed_all, back_kv)
        rows_t, logits_all = turn(plane_number, normed_all, part_rows, wide_columns)
        gates_all, _, _ = gates_from(logits_all, bits_all)

        def weight_sums(block, outs, *tokens):
            return weight_grads(
                plane_number,
                planes,
                block,
                after(normed_all, *tokens),
                grad_top_all,
                rows_t,
                top_t,
                gates_all,
                (weight_gu, weight_down),
                own_sums[block],
                outs,
                groups,
                hidden,
            )

        shared_grads = weight_sums(local_experts, (local_experts,), back_kv)
    else:
        gu_part = lax.psum_scatter(
            dot_tn(normed_two, grad_hidden).astype(BF16), "dp", scatter_dimension=0, tiled=True
        )
        down_part = lax.psum_scatter(
            dot_tn(grad_top_all, gated).astype(BF16), "dp", scatter_dimension=0, tiled=True
        )

        def block_of(values, index, size):
            return values[:, index * padded : index * padded + size]

        shared_grads = [
            block_of(gu_part, 2 * local_experts, padded).reshape(groups, small_rows, padded),
            block_of(gu_part, 2 * local_experts + 1, padded).reshape(groups, small_rows, padded),
            block_of(down_part, local_experts, padded).reshape(groups, small_rows, padded).transpose(0, 2, 1),
        ]
    wide_grads = to_owners(jnp.stack(shared_grads[:2], axis=1))
    shared_down_grads = to_owners(shared_grads[2])
    came_kv = after(
        lax.ppermute(back_kv, "dp", [(i + 1, i) for i in range(planes - 1)]), shared_grads
    ).astype(F32)
    grad_query = rotate(grad_query_rot, cosine, -sine_table).astype(BF16)
    grad_key = rotate(own_keys + came_kv[:, :width], cosine, -sine_table).astype(BF16)
    grad_value = (own_values + came_kv[:, width:]).astype(BF16)
    grad_qkv = in_cores(jnp.concatenate([grad_query, grad_key, grad_value], axis=1))
    weight_qkv = jnp.concatenate([weight_q, weight_kv], axis=1)
    grad_one_part = dot_nt(grad_qkv, weight_qkv).astype(BF16)
    grad_part = jnp.concatenate([dot_tn(normed_one, grad_qkv), dot_tn(grad_attended, attended)], axis=1).astype(BF16)
    weight_sum = lax.psum_scatter(grad_part, "dp", scatter_dimension=0, tiled=True)
    weight_sum = weight_sum.reshape(groups, small_rows, 4, width)
    if gathered:
        expert_grads = (local_experts,)
        for e in range(local_experts - 2):
            expert_grads = weight_sums(e, expert_grads, grad_part)
        grad_normed_one, expert_grads = scatter_plane(
            lambda index: of_core(grad_one_part, index),
            lambda token: weight_sums(local_experts - 2, expert_grads, token, grad_part),
        )
        wide_grads, shared_down_grads = after((wide_grads, shared_down_grads), expert_grads)
    else:
        grad_normed_one = scatter_plane(lambda index: of_core(grad_one_part, index))
    grad_shared_gate = placed(wide_grads[:, 0], 1)
    grad_shared_up = placed(wide_grads[:, 1], 1)
    grad_shared_down = placed(shared_down_grads, 0)
    grad_attn_gain = jnp.sum(grad_normed_one * inputs * scale_one, axis=0)
    grad_own = grad_after + norm_back(inputs, scale_one, gain_one, grad_normed_one)
    if gathered:
        expert_grads = weight_sums(local_experts - 1, expert_grads, grad_own, weight_sum)
    else:
        expert_grads = [
            jnp.stack([block_of(values, first + stride * e, hidden).T for e in range(local_experts)]).astype(F32)
            for values, first, stride in ((gu_part, 0, 2), (gu_part, 1, 2), (down_part, 0, 1))
        ]
    grad_expert_gate, grad_expert_up = (jnp.swapaxes(grad, 1, 2) for grad in expert_grads[:2])
    grad_expert_down = expert_grads[2]
    grad_tokens = both_cores(grad_own)

    weight_rows = (
        lax.all_to_all(weight_sum, "expert", 0, 0)
        .transpose(2, 1, 0, 3)
        .reshape(4, small_rows, groups * width)
        .astype(F32)
    )
    qkv_rows = weight_rows[:3]
    grad_out_weight = weight_rows[3].T

    bias_sums = jnp.sum(grad_qkv, axis=0, dtype=F32).reshape(1, 3, heads, HD)
    bias_table = lax.dynamic_update_slice(
        jnp.zeros((cores, 3, heads_here, HD), F32), bias_sums, (core, 0, mine * heads, 0)
    )
    devices = planes * groups
    spread = jnp.concatenate(
        [
            grad_attn_gain.reshape(devices, -1),
            grad_mlp_gain.reshape(devices, -1),
            grad_columns.reshape(devices, -1),
            bias_table.reshape(cores * 3 * heads_here, devices, HD // devices).transpose(1, 0, 2).reshape(devices, -1),
        ],
        axis=1,
    )
    sums = jnp.sum(lax.all_to_all(spread, ("dp", "expert"), 0, 0, tiled=True), axis=0, keepdims=True)
    sums = lax.psum(sums, "tensor")[0] if cores != 2 else (sums + lax.ppermute(sums, "tensor", [(0, 1), (1, 0)]))[0]
    gain_part = model_width // devices
    grad_attn_gain, grad_mlp_gain = sums[:gain_part], sums[gain_part : 2 * gain_part]
    table = sums[2 * gain_part :]
    column_size = gain_part * (expert_count + 1)
    column_sums = table[:column_size].reshape(gain_part, expert_count + 1)
    bias_sums = table[column_size:].reshape(cores, 3, heads_here, HD // devices)
    bias_sums = lax.dynamic_slice(bias_sums, (core, 0, 0, 0), (1, 3, heads_here, HD // devices))[0]
    return (
        out,
        grad_tokens,
        grad_attn_gain,
        qkv_rows[0],
        bias_sums[0],
        qkv_rows[1],
        bias_sums[1],
        qkv_rows[2],
        bias_sums[2],
        grad_out_weight,
        grad_mlp_gain,
        column_sums[:, :expert_count],
        column_sums[:, expert_count],
        grad_shared_gate,
        grad_shared_up,
        grad_shared_down,
        grad_expert_gate,
        grad_expert_up,
        grad_expert_down,
    )


def solution(mesh):
    tokens = ("dp", "expert")
    return jax.shard_map(
        per_device,
        mesh=mesh,
        in_specs=(
            P(tokens, None),
            P(tokens),
            P(tokens, None),
            P(),
            P(None, "tensor"),
            P("tensor", None),
            P(None, "tensor"),
            P("tensor", None),
            P(None, "tensor"),
            P("tensor", None),
            P("tensor", None),
            P(),
            P(),
            P(),
            P(None, "tensor"),
            P(None, "tensor"),
            P("tensor", None),
            P("expert", None, "tensor"),
            P("expert", None, "tensor"),
            P("expert", "tensor", None),
            P(tokens, None),
        ),
        out_specs=(
            P(tokens, None),
            P(tokens, None),
            P(tokens),
            P(tokens, "tensor"),
            P("tensor", tokens),
            P(tokens, "tensor"),
            P("tensor", tokens),
            P(tokens, "tensor"),
            P("tensor", tokens),
            P("tensor", tokens),
            P(tokens),
            P(tokens, None),
            P(tokens),
            P(tokens, "tensor"),
            P(tokens, "tensor"),
            P("tensor", tokens),
            P("expert", "dp", "tensor"),
            P("expert", "dp", "tensor"),
            P("expert", "tensor", "dp"),
        ),
        check_vma=False,
    )
```

```python
import functools

import jax
import jax.numpy as jnp
from jax import lax
from jax.experimental import pallas as pl
from jax.experimental.pallas import tpu as pltpu
from jax.sharding import PartitionSpec as P

HD = 128
SEQ_LEN = 4096
WINDOW = 1024
EPS = 1e-06
THETA = 1000000.0
NEG_LARGE = -1e30
QUERY_BLOCK = 256
FEED_BLOCK = 512
LANE = 128
FACT_ROWS = 16
GATHERED_PLANES = 4
F32 = jnp.float32
BF16 = jnp.bfloat16


def dot(left, right):
    return jnp.dot(left, right, preferred_element_type=F32)


def dot_nt(left, right):
    return lax.dot_general(left, right, (((1,), (1,)), ((), ())), preferred_element_type=F32)


def dot_tn(left, right):
    return lax.dot_general(left, right, (((0,), (0,)), ((), ())), preferred_element_type=F32)


def shift_pairs(count, step):
    if count & (count - 1) == 0:
        return [(source, source ^ step) for source in range(count)]
    return [(source, (source + step) % count) for source in range(count)]


def partner(index, count, step):
    if count & (count - 1) == 0:
        return index ^ step
    return (index + step) % count


def source(index, count, step):
    if count & (count - 1) == 0:
        return index ^ step
    return (index - step + count) % count


def gather_halves(own, meanwhile=()):
    groups, mine = lax.axis_size("expert"), lax.axis_index("expert")
    rows, width = own.shape
    pieces = jnp.zeros((groups * rows, width), own.dtype)
    pieces = lax.dynamic_update_slice(pieces, own, (mine * rows, 0))
    for step in range(1, groups):
        came = lax.ppermute(own, "expert", shift_pairs(groups, step))
        came = after(came, own, *meanwhile)
        pieces = lax.dynamic_update_slice(pieces, came, (source(mine, groups, step) * rows, 0))
    return pieces, swapped(pieces)


def swapped(values):
    return lax.ppermute(values, "tensor", [(0, 1), (1, 0)])


def scatter_halves(own, other, meanwhile=None):
    groups, mine = lax.axis_size("expert"), lax.axis_index("expert")
    held = own.astype(F32) + swapped(other.astype(BF16)).astype(F32)
    rows, width = held.shape[0] // groups, held.shape[1]

    def of_group(index):
        return lax.dynamic_slice(held, (index * rows, 0), (rows, width))

    sent = [of_group(partner(mine, groups, step)).astype(BF16) for step in range(1, groups)]
    came = [lax.ppermute(sent[step - 1], "expert", shift_pairs(groups, step)) for step in range(1, groups)]
    result = of_group(mine)
    if meanwhile is None:
        return functools.reduce(jnp.add, [part.astype(F32) for part in came], result)
    side = meanwhile(tuple(sent))
    came = lax.optimization_barrier((tuple(came), side))[0]
    return functools.reduce(jnp.add, [part.astype(F32) for part in came], result), side


def after(value, *others):
    return lax.optimization_barrier((value, *others))[0]


def both_cores(own):
    return joined(own, swapped(own))


def joined(own, other):
    core = lax.axis_index("tensor")
    return jnp.concatenate([jnp.where(core == 0, own, other), jnp.where(core == 0, other, own)], axis=0)


def token_order(own, other, groups):
    half, width = own.shape
    both = joined(own, other).reshape(2, groups, half // groups, width)
    return both.transpose(1, 0, 2, 3).reshape(2 * half, width)


def half_order(values, groups):
    total, width = values.shape
    core = lax.axis_index("tensor")
    split = values.reshape(groups, 2, total // (2 * groups), width)
    return tuple(
        lax.dynamic_slice(split, (0, index, 0, 0), (groups, 1, total // (2 * groups), width)).reshape(-1, width)
        for index in (core, 1 - core)
    )


def norm_back(values, inv_scale, gain_vec, grad_normed):
    weighted = grad_normed * gain_vec
    inner_mean = jnp.mean(weighted * values, axis=-1, keepdims=True)
    return inv_scale * weighted - values * inv_scale * inv_scale * inv_scale * inner_mean


def masked_scores(query, keys, seg_query, seg_keys, offset):
    scores = dot_nt(query, keys) * (HD ** (-0.5))
    rows, columns = scores.shape
    distance = (
        lax.broadcasted_iota(jnp.int32, (rows, columns), 0)
        - lax.broadcasted_iota(jnp.int32, (rows, columns), 1)
        + offset
    )
    allowed = (seg_query == seg_keys) & (distance >= 0) & (distance < WINDOW)
    return jnp.where(allowed, scores, NEG_LARGE)


def key_ranges(start, block, rows):
    first_before = min(rows, max(0, (start + rows - WINDOW + 1) // block * block))
    first_own = max(0, (start - WINDOW + 1) // block * block)
    return (first_before, rows), (first_own, start + block)


def probabilities(query, parts, seg_query):
    scores = [masked_scores(query, keys, seg_query, seg_keys, offset) for keys, seg_keys, offset in parts]
    top = functools.reduce(jnp.maximum, [jnp.max(part, axis=-1, keepdims=True) for part in scores])
    expo = [jnp.exp(part - top) for part in scores]
    total = functools.reduce(jnp.add, [jnp.sum(part, axis=-1, keepdims=True) for part in expo])
    inverse = 1.0 / total
    return [part * inverse for part in expo]


def key_parts(start, block, rows, before_ref, own_ref, seg_before, seg_own):
    (before, before_end), (own, own_end) = key_ranges(start, block, rows)
    ranges = []
    if before < before_end:
        ranges.append((before_ref, seg_before, before, before_end, start + rows - before))
    ranges.append((own_ref, seg_own, own, own_end, start - own))
    parts = [(ref[low:high, :HD], seg[:, low:high], offset) for ref, seg, low, high, offset in ranges]
    values = [ref[low:high, HD:] for ref, _, low, high, _ in ranges]
    return parts, values, [(low, high) for _, _, low, high, _ in ranges]


def attend_kernel(block, q_ref, before_ref, own_ref, sq_ref, sb_ref, so_ref, out_ref):
    rows = q_ref.shape[0]
    for start in range(0, rows, block):
        parts, values, _ = key_parts(start, block, rows, before_ref, own_ref, sb_ref, so_ref)
        probs = probabilities(q_ref[start : start + block, :], parts, sq_ref[start : start + block, :])
        total = functools.reduce(
            jnp.add, [dot(part.astype(BF16), value) for part, value in zip(probs, values, strict=True)]
        )
        out_ref[start : start + block, :] = total.astype(BF16)


def attend_back_kernel(
    block, q_ref, before_ref, own_ref, sq_ref, sb_ref, so_ref, grad_ref, gq_ref, gb_ref, go_ref, back_ref
):
    rows = q_ref.shape[0]
    back_ref[...] = jnp.zeros_like(back_ref)
    go_ref[...] = jnp.zeros_like(go_ref)
    scale = HD ** (-0.5)
    for start in range(0, rows, block):
        query = q_ref[start : start + block, :]
        grad = grad_ref[start : start + block, :]
        parts, values, ranges = key_parts(start, block, rows, before_ref, own_ref, sb_ref, so_ref)
        sinks = [back_ref, go_ref][-len(parts) :]
        probs = probabilities(query, parts, sq_ref[start : start + block, :])
        grad_probs = [dot_nt(grad, value) for value in values]
        delta = functools.reduce(
            jnp.add,
            [jnp.sum(p * g, axis=-1, keepdims=True) for p, g in zip(probs, grad_probs, strict=True)],
        )
        grad_query = None
        for p, g, part, sink, (low, high) in zip(probs, grad_probs, parts, sinks, ranges, strict=True):
            grad_scores = (p * (g - delta)).astype(BF16)
            term = dot(grad_scores, part[0])
            grad_query = term if grad_query is None else grad_query + term
            sink[low:high, :HD] += dot_tn(grad_scores, query) * scale
            sink[low:high, HD:] += dot_tn(p.astype(BF16), grad)
        gq_ref[start : start + block, :] = grad_query * scale
    gb_ref[...] = back_ref[...].astype(BF16)


def attention_specs(rows):
    column = pl.BlockSpec((rows, HD), lambda h: (0, h))
    pair = pl.BlockSpec((rows, 2 * HD), lambda h: (0, h))
    seg_rows = pl.BlockSpec((rows, 1), lambda h: (0, 0))
    seg_columns = pl.BlockSpec((1, rows), lambda h: (0, 0))
    return column, pair, [column, pair, pair, seg_rows, seg_columns, seg_columns]


def attend(query, before, own, seg_rows, seg_before, seg_own):
    rows, width = query.shape
    heads = width // HD
    column, _, specs = attention_specs(rows)
    return pl.pallas_call(
        functools.partial(attend_kernel, min(QUERY_BLOCK, rows)),
        grid=(heads,),
        in_specs=specs,
        out_specs=column,
        out_shape=jax.ShapeDtypeStruct((rows, width), BF16),
        compiler_params=pltpu.CompilerParams(vmem_limit_bytes=48 * 2**20),
        cost_estimate=pl.CostEstimate(
            flops=4 * rows * WINDOW * width, bytes_accessed=12 * rows * width, transcendentals=rows * WINDOW * heads
        ),
        name="attend",
    )(query, before, own, seg_rows, seg_before, seg_own)


def attend_back(query, before, own, seg_rows, seg_before, seg_own, grad_heads):
    rows, width = query.shape
    heads = width // HD
    column, pair, specs = attention_specs(rows)
    return pl.pallas_call(
        functools.partial(attend_back_kernel, min(QUERY_BLOCK, rows)),
        grid=(heads,),
        in_specs=specs + [column],
        out_specs=[column, pair, pair],
        out_shape=[
            jax.ShapeDtypeStruct((rows, width), F32),
            jax.ShapeDtypeStruct((rows, 2 * width), BF16),
            jax.ShapeDtypeStruct((rows, 2 * width), F32),
        ],
        scratch_shapes=[pltpu.VMEM((rows, 2 * HD), F32)],
        compiler_params=pltpu.CompilerParams(vmem_limit_bytes=48 * 2**20),
        cost_estimate=pl.CostEstimate(
            flops=10 * rows * WINDOW * width, bytes_accessed=32 * rows * width, transcendentals=rows * WINDOW * heads
        ),
        name="attend_back",
    )(query, before, own, seg_rows, seg_before, seg_own, grad_heads)


def turned(values, cosine, sines):
    return values * cosine + pltpu.roll(values, HD // 2, 1) * sines


def half_rows(index, group, rows, core):
    return pl.ds(pl.multiple_of(2 * group * rows + lax.rem(core + index, 2) * rows, rows), rows)


def project_kernel(
    groups, place_ref, own_ref, other_ref, wq_ref, wk_ref, wv_ref, bias_ref, cos_ref, sin_ref, q_ref, kv_ref
):
    core = place_ref[1]
    half, width = own_ref.shape[0], wq_ref.shape[1]
    rows = half // groups
    for index, ref in enumerate((own_ref, other_ref)):
        here = slice(index * half, (index + 1) * half)
        cosine, sines = cos_ref[here, :], sin_ref[here, :]
        normed = ref[...]
        for k, weight in enumerate((wq_ref, wk_ref, wv_ref)):
            product = dot(normed, weight[...]) + bias_ref[k : k + 1, :].astype(F32)
            for h in range(width // HD):
                values = product[:, h * HD : (h + 1) * HD]
                if k < 2:
                    values = turned(values, cosine, sines)
                values = values.astype(BF16)
                out, at = (q_ref, h * HD) if k == 0 else (kv_ref, (2 * h + k - 1) * HD)
                for group in range(groups):
                    out[half_rows(index, group, rows, core), at : at + HD] = values[group * rows : (group + 1) * rows]


def project(place, halves, weights, bias, cosine, sines, groups):
    half, model_width = halves[0].shape
    width = weights[0].shape[1] // groups
    whole = pl.BlockSpec((half, model_width), lambda i, p: (0, 0))
    weight_spec = pl.BlockSpec((model_width, width), lambda i, p: (0, p[0]))
    table = pl.BlockSpec((2 * half, HD), lambda i, p: (0, 0))
    return pl.pallas_call(
        functools.partial(project_kernel, groups),
        grid_spec=pltpu.PrefetchScalarGridSpec(
            num_scalar_prefetch=1,
            grid=(1,),
            in_specs=[whole, whole]
            + [weight_spec] * 3
            + [pl.BlockSpec((3, width), lambda i, p: (0, p[0])), table, table],
            out_specs=[
                pl.BlockSpec((2 * half, width), lambda i, p: (0, 0)),
                pl.BlockSpec((2 * half, 2 * width), lambda i, p: (0, 0)),
            ],
        ),
        out_shape=[
            jax.ShapeDtypeStruct((2 * half, width), BF16),
            jax.ShapeDtypeStruct((2 * half, 2 * width), BF16),
        ],
        compiler_params=pltpu.CompilerParams(vmem_limit_bytes=48 * 2**20),
        cost_estimate=pl.CostEstimate(
            flops=12 * half * model_width * width,
            bytes_accessed=4 * half * model_width + 6 * model_width * width,
            transcendentals=0,
        ),
        name="project",
    )(place, *halves, *weights, bias, cosine, sines)


def project_back_kernel(
    groups,
    place_ref,
    gq_ref,
    go_ref,
    came_ref,
    wq_ref,
    wk_ref,
    wv_ref,
    cos_ref,
    sin_ref,
    own_ref,
    other_ref,
    own_part,
    other_part,
    bias_ref,
):
    core = place_ref[1]
    half, width = own_ref.shape[0], gq_ref.shape[1]
    rows = half // groups
    columns = min(512, own_part.shape[1])
    bias_sum = jnp.zeros((1, 3 * width), F32)
    for index, (out, part) in enumerate(((own_ref, own_part), (other_ref, other_part))):
        here = slice(index * half, (index + 1) * half)
        cosine, sines = cos_ref[here, :], sin_ref[here, :]
        for k in range(3):
            for h in range(width // HD):
                pieces = []
                for group in range(groups):
                    at_rows = half_rows(index, group, rows, core)
                    if k == 0:
                        pieces.append(gq_ref[at_rows, h * HD : (h + 1) * HD])
                    else:
                        at = (2 * h + k - 1) * HD
                        pieces.append(go_ref[at_rows, at : at + HD] + came_ref[at_rows, at : at + HD].astype(F32))
                values = jnp.concatenate(pieces, axis=0)
                if k < 2:
                    values = turned(values, cosine, -sines)
                out[:, k * width + h * HD : k * width + (h + 1) * HD] = values.astype(BF16)
        grads = out[...]
        bias_sum = bias_sum + jnp.sum(grads.astype(F32), axis=0, keepdims=True)
        for at in range(0, part.shape[1], columns):
            total = dot_nt(grads[:, :width], wq_ref[at : at + columns, :])
            total = total + dot_nt(grads[:, width : 2 * width], wk_ref[at : at + columns, :])
            total = total + dot_nt(grads[:, 2 * width :], wv_ref[at : at + columns, :])
            part[:, at : at + columns] = total.astype(BF16)
    bias_ref[...] = jnp.broadcast_to(bias_sum, bias_ref.shape)


def project_back(place, grad_query, own_kv_grad, came_kv, weights, cosine, sines, groups):
    total, width = grad_query.shape
    half = total // 2
    model_width = weights[0].shape[0]
    weight_spec = pl.BlockSpec((model_width, width), lambda i, p: (0, p[0]))

    def full(*shape):
        return pl.BlockSpec(shape, lambda i, p: (0, 0))

    return pl.pallas_call(
        functools.partial(project_back_kernel, groups),
        grid_spec=pltpu.PrefetchScalarGridSpec(
            num_scalar_prefetch=1,
            grid=(1,),
            in_specs=[full(total, width), full(total, 2 * width), full(total, 2 * width)]
            + [weight_spec] * 3
            + [full(total, HD)] * 2,
            out_specs=[full(half, 3 * width)] * 2 + [full(half, model_width)] * 2 + [full(8, 3 * width)],
        ),
        out_shape=[jax.ShapeDtypeStruct((half, 3 * width), BF16)] * 2
        + [jax.ShapeDtypeStruct((half, model_width), BF16)] * 2
        + [jax.ShapeDtypeStruct((8, 3 * width), F32)],
        compiler_params=pltpu.CompilerParams(vmem_limit_bytes=48 * 2**20),
        cost_estimate=pl.CostEstimate(
            flops=12 * half * model_width * width,
            bytes_accessed=8 * half * model_width + 6 * model_width * width,
            transcendentals=0,
        ),
        name="project_back",
    )(place, grad_query, own_kv_grad, came_kv, *weights, cosine, sines)


def projection_grads_kernel(n0, n1, d0, d1, g0, g1, a0, a1, out_ref):
    width = g0.shape[1]
    out_ref[:, :width] = (dot_tn(n0[...], g0[...]) + dot_tn(n1[...], g1[...])).astype(BF16)
    out_ref[:, width:] = (dot_tn(d0[...], a0[...]) + dot_tn(d1[...], a1[...])).astype(BF16)


def projection_grads(normed, grads_after, grads, attended):
    half, model_width = normed[0].shape
    width = grads[0].shape[1] + attended[0].shape[1]
    tile = min(512, model_width)
    wide = pl.BlockSpec((half, tile), lambda i: (0, i))
    return pl.pallas_call(
        projection_grads_kernel,
        grid=(model_width // tile,),
        in_specs=[wide] * 4
        + [pl.BlockSpec(grads[0].shape, lambda i: (0, 0))] * 2
        + [pl.BlockSpec(attended[0].shape, lambda i: (0, 0))] * 2,
        out_specs=pl.BlockSpec((tile, width), lambda i: (i, 0)),
        out_shape=jax.ShapeDtypeStruct((model_width, width), BF16),
        compiler_params=pltpu.CompilerParams(vmem_limit_bytes=40 * 2**20),
        cost_estimate=pl.CostEstimate(
            flops=4 * half * model_width * width, bytes_accessed=8 * half * model_width, transcendentals=0
        ),
        name="projection_grads",
    )(*normed, *grads_after, *grads, *attended)


def hidden_grads(rows, top, gate, weight_gu, weight_down):
    hidden = weight_down.shape[0]
    both = dot_nt(rows, weight_gu)
    inner_grad = dot_nt(top, weight_down)
    gate_val, up_val = both[:, :hidden], both[:, hidden:]
    sigmoid_val = jax.nn.sigmoid(gate_val)
    silu_val = gate_val * sigmoid_val
    inner = silu_val * up_val
    slope = jnp.sum(inner * inner_grad, axis=-1, keepdims=True)
    inner_grad = inner_grad * gate
    gated = (inner * gate).astype(BF16)
    grad_gate_val = (inner_grad * up_val * (sigmoid_val + silu_val * (1.0 - sigmoid_val))).astype(BF16)
    grad_up_val = (inner_grad * silu_val).astype(BF16)
    return gated, grad_gate_val, grad_up_val, slope


def gate_of(gates, block):
    lane = lax.broadcasted_iota(jnp.int32, gates.shape, 1)
    return jnp.sum(jnp.where(lane == block, gates, 0.0), axis=1, keepdims=True)


def feed_kernel(first_ref, rows_ref, top_ref, gates_ref, gu_ref, down_ref, *refs):
    del first_ref
    gated_ref, grad_ref, slope_ref = refs[-3:]
    hidden = down_ref.shape[0]
    gate = gate_of(gates_ref[...], pl.program_id(0))
    gated, grad_gate_val, grad_up_val, slope = hidden_grads(
        rows_ref[...], top_ref[...], gate, gu_ref[...], down_ref[...]
    )
    gated_ref[...] = gated
    grad_ref[:, :hidden] = grad_gate_val
    grad_ref[:, hidden:] = grad_up_val
    slope_ref[0] = slope


def weight_kernel(
    routed,
    hidden_out,
    chunk_ref,
    rows_ref,
    top_ref,
    rows_t_ref,
    top_t_ref,
    gates_ref,
    gu_ref,
    down_ref,
    gu_in,
    down_in,
    *rest,
):
    del chunk_ref
    sums = rest[-3:]
    gate_sum, up_sum, down_sum = sums
    hidden = down_ref.shape[0]
    step = pl.program_id(0)

    @pl.when(step == 0)
    def _():
        gate_sum[...] = gu_in[:, :hidden]
        up_sum[...] = gu_in[:, hidden:]
        down_sum[...] = down_in[...]

    gate = gate_of(gates_ref[...], routed)
    gated, grad_gate_val, grad_up_val, _ = hidden_grads(
        rows_ref[...], top_ref[...], gate, gu_ref[...], down_ref[...]
    )
    gate_sum[...] += dot(rows_t_ref[...], grad_gate_val)
    up_sum[...] += dot(rows_t_ref[...], grad_up_val)
    down_sum[...] += dot(top_t_ref[...], gated)

    @pl.when(step == pl.num_programs(0) - 1)
    def _():
        if len(rest[-4].shape) == 3:
            for out, total in zip(rest[-6:-3], sums, strict=True):
                out[0] = total[...].T[:hidden_out]
        else:
            out = rest[-4]
            groups, _, part = out.shape[:3]
            for g in range(groups):
                for k, total in enumerate(sums):
                    out[g, k] = total[g * part : (g + 1) * part, :].astype(BF16)


def pack_kernel(local, hidden, units, window_ref, *refs):
    gate_ref, up_ref, down_ref = refs[:3]
    shared_gate, shared_up = refs[3 : 3 + units], refs[3 + units : 3 + 2 * units]
    shared_down = refs[3 + 2 * units : 3 + 3 * units]
    gu_out, down_out = refs[-2:]
    padded = units * LANE
    columns = down_out.shape[1]
    for e in range(local):
        for ref, out, at in ((gate_ref, gu_out, 2 * e), (up_ref, gu_out, 2 * e + 1), (down_ref, down_out, e)):
            out[at * padded : at * padded + hidden, :] = ref[e]
            if hidden < padded:
                out[at * padded + hidden : (at + 1) * padded, :] = jnp.zeros((padded - hidden, columns), BF16)
    skip = window_ref[1]
    for k in range(units):
        line = lax.broadcasted_iota(jnp.int32, (LANE, columns), 0) + k * LANE
        keep = (line >= skip) & (line < skip + hidden)
        for block, out, at in (
            (shared_gate[k][...].T, gu_out, 2 * local),
            (shared_up[k][...].T, gu_out, 2 * local + 1),
            (shared_down[k][...], down_out, local),
        ):
            out[at * padded + k * LANE : at * padded + (k + 1) * LANE, :] = jnp.where(
                keep, block.astype(F32), 0.0
            ).astype(BF16)


def pack_weights(window, expert_gate, expert_up, expert_down, shared_gate, shared_up, shared_down, padded):
    local, hidden, model_width = expert_down.shape
    units = padded // LANE
    blocks = local + 1
    tile = min(256, model_width)
    expert_spec = pl.BlockSpec((local, hidden, tile), lambda i, w: (0, 0, i))
    column_specs = [pl.BlockSpec((tile, LANE), lambda i, w, k=k: (i, w[0] + k)) for k in range(units)]
    row_specs = [pl.BlockSpec((LANE, tile), lambda i, w, k=k: (w[0] + k, i)) for k in range(units)]
    return pl.pallas_call(
        functools.partial(pack_kernel, local, hidden, units),
        grid_spec=pltpu.PrefetchScalarGridSpec(
            num_scalar_prefetch=1,
            grid=(model_width // tile,),
            in_specs=[expert_spec] * 3 + column_specs * 2 + row_specs,
            out_specs=[
                pl.BlockSpec((2 * blocks * padded, tile), lambda i, w: (0, i)),
                pl.BlockSpec((blocks * padded, tile), lambda i, w: (0, i)),
            ],
        ),
        out_shape=[
            jax.ShapeDtypeStruct((2 * blocks * padded, model_width), BF16),
            jax.ShapeDtypeStruct((blocks * padded, model_width), BF16),
        ],
        compiler_params=pltpu.CompilerParams(vmem_limit_bytes=40 * 2**20),
        cost_estimate=pl.CostEstimate(
            flops=0, bytes_accessed=12 * blocks * padded * model_width, transcendentals=0
        ),
        name="pack_weights",
    )(
        window,
        jnp.swapaxes(expert_gate, 1, 2),
        jnp.swapaxes(expert_up, 1, 2),
        expert_down,
        *([shared_gate] * units),
        *([shared_up] * units),
        *([shared_down] * units),
    )


def turn_kernel(plane_ref, part_ref, out_ref):
    del plane_ref
    out_ref[...] = part_ref[...].T


def turn(plane, values, part):
    total = values.shape[0]
    tile = min(1024, total)
    return pl.pallas_call(
        turn_kernel,
        grid_spec=pltpu.PrefetchScalarGridSpec(
            num_scalar_prefetch=1,
            grid=(total // tile,),
            in_specs=[pl.BlockSpec((tile, part), lambda i, p: (i, p[0]))],
            out_specs=pl.BlockSpec((part, tile), lambda i, p: (0, i)),
        ),
        out_shape=jax.ShapeDtypeStruct((part, total), BF16),
        compiler_params=pltpu.CompilerParams(vmem_limit_bytes=40 * 2**20),
        cost_estimate=pl.CostEstimate(flops=0, bytes_accessed=4 * total * part, transcendentals=0),
        name="turn",
    )(plane, values)


def feed(first, index, rows, top_all, gates, weight_gu, weight_down, blocks, outs=None):
    count, model_width = rows.shape
    hidden = weight_down.shape[0] // blocks
    tile = min(FEED_BLOCK, count)
    steps = count // tile
    whole = 2 * count
    in_specs = [
        pl.BlockSpec((tile, model_width), lambda s, i, c: (i, 0)),
        pl.BlockSpec((tile, model_width), lambda s, i, c: (c[0] * steps + i, 0)),
        pl.BlockSpec((tile, gates.shape[1]), lambda s, i, c: (i, 0)),
        pl.BlockSpec((2 * hidden, model_width), lambda s, i, c: (s, 0)),
        pl.BlockSpec((hidden, model_width), lambda s, i, c: (s, 0)),
    ]
    args = [first, rows, top_all, gates, weight_gu, weight_down]
    aliases = {}
    if outs is not None:
        aliases = {len(args) + k: k for k in range(3)}
        in_specs += [pl.BlockSpec(memory_space=pl.ANY)] * 3
        args += list(outs)
    grid_spec = pltpu.PrefetchScalarGridSpec(
        num_scalar_prefetch=1,
        grid=(blocks, steps),
        in_specs=in_specs,
        out_specs=[
            pl.BlockSpec((tile, hidden), lambda s, i, c: (index * steps + i, s)),
            pl.BlockSpec((tile, 2 * hidden), lambda s, i, c: (index * steps + i, s)),
            pl.BlockSpec((1, tile, 1), lambda s, i, c: (s, index * steps + i, 0)),
        ],
    )
    return pl.pallas_call(
        feed_kernel,
        grid_spec=grid_spec,
        out_shape=[
            jax.ShapeDtypeStruct((whole, blocks * hidden), BF16),
            jax.ShapeDtypeStruct((whole, 2 * blocks * hidden), BF16),
            jax.ShapeDtypeStruct((blocks, whole, 1), F32),
        ],
        input_output_aliases=aliases,
        compiler_params=pltpu.CompilerParams(vmem_limit_bytes=56 * 2**20),
        cost_estimate=pl.CostEstimate(
            flops=6 * count * model_width * hidden * blocks,
            bytes_accessed=6 * model_width * hidden * blocks + 4 * count * model_width * blocks,
            transcendentals=count * hidden * blocks,
        ),
        name="feed",
    )(*args)


def weight_grads(plane, planes, block, rows_all, top_all, rows_t, top_t, gates, packed, sums, outs, groups, hidden):
    weight_gu, weight_down = packed
    total, model_width = rows_all.shape
    count = total // planes
    part = rows_t.shape[0]
    padded = sums[1].shape[1]
    tile = min(FEED_BLOCK, count // 2)
    steps = count // tile
    local = outs[0] if isinstance(outs[0], int) else outs[0].shape[0]

    half_steps = max(1, steps // 2)

    def at(i, c):
        place = lax.rem(i, steps)
        half = lax.rem(place // half_steps + c[1], 2)
        return lax.rem(c[0] + 1 + i // steps, planes) * steps + half * half_steps + lax.rem(place, half_steps)

    tokens = pl.BlockSpec((tile, model_width), lambda i, c: (at(i, c), 0))
    turned = pl.BlockSpec((part, tile), lambda i, c: (0, at(i, c)))
    in_specs = [
        tokens,
        tokens,
        turned,
        turned,
        pl.BlockSpec((tile, gates.shape[1]), lambda i, c: (i, 0)),
        pl.BlockSpec((2 * padded, model_width), lambda i, c: (block, 0)),
        pl.BlockSpec((padded, model_width), lambda i, c: (block, 0)),
        pl.BlockSpec((part, 2 * padded), lambda i, c: (0, 0)),
        pl.BlockSpec((part, padded), lambda i, c: (0, 0)),
    ]
    args = [rows_all, top_all, rows_t, top_t, gates, weight_gu, weight_down, *sums]
    aliases = {}
    if block < local:
        out_shape = [jax.ShapeDtypeStruct((local, hidden, part), F32)] * 3
        out_specs = [pl.BlockSpec((1, hidden, part), lambda i, c: (block, 0, 0))] * 3
        if not isinstance(outs[0], int):
            in_specs += [pl.BlockSpec(memory_space=pl.ANY)] * 3
            aliases = {len(args) + 1 + k: k for k in range(3)}
            args += list(outs)
    else:
        out_shape = [jax.ShapeDtypeStruct((groups, 3, part // groups, padded), BF16)]
        out_specs = [pl.BlockSpec(out_shape[0].shape, lambda i, c: (0, 0, 0, 0))]
    return pl.pallas_call(
        functools.partial(weight_kernel, block, hidden),
        grid_spec=pltpu.PrefetchScalarGridSpec(
            num_scalar_prefetch=1,
            grid=((planes - 1) * steps,),
            in_specs=in_specs,
            out_specs=out_specs,
            scratch_shapes=[pltpu.VMEM((part, padded), F32)] * 3,
        ),
        out_shape=out_shape,
        input_output_aliases=aliases,
        compiler_params=pltpu.CompilerParams(vmem_limit_bytes=62 * 2**20),
        cost_estimate=pl.CostEstimate(
            flops=6 * (total - count) * (model_width + part) * padded,
            bytes_accessed=6 * model_width * padded + 4 * total * model_width,
            transcendentals=total * padded,
        ),
        name="weight_grads",
    )(plane, *args)


def per_device(
    tokens,
    segments,
    routes,
    attn_gain,
    query_weight,
    query_bias,
    key_weight,
    key_bias,
    value_weight,
    value_bias,
    out_weight,
    mlp_gain,
    router_weight,
    shared_router,
    shared_gate,
    shared_up,
    shared_down,
    expert_gate,
    expert_up,
    expert_down,
    grad_out,
):
    tok_rows, model_width = tokens.shape
    groups, cores = lax.axis_size("expert"), lax.axis_size("tensor")
    planes = lax.axis_size("dp")
    mine, core, plane = lax.axis_index("expert"), lax.axis_index("tensor"), lax.axis_index("dp")
    rows = tok_rows // cores
    plane_rows = tok_rows * groups
    heads_here = query_weight.shape[1] // HD
    width = query_weight.shape[1] // groups
    heads = width // HD
    local_experts, _, hidden = expert_gate.shape
    expert_count = local_experts * groups
    blocks = local_experts + 1
    gathered = planes <= GATHERED_PLANES
    padded = -(-hidden // LANE) * LANE
    part_rows = model_width // planes

    first_unit = mine * hidden // LANE
    window = jnp.stack([first_unit, mine * hidden - first_unit * LANE]).astype(jnp.int32)
    weight_gu, weight_down = pack_weights(
        window, expert_gate, expert_up, expert_down, shared_gate, shared_up, shared_down, padded
    )

    own_tokens = lax.dynamic_slice(tokens, (core * rows, 0), (rows, model_width))
    inputs = own_tokens.astype(F32)
    gain_one = attn_gain.astype(F32)
    scale_one = lax.rsqrt(jnp.mean(inputs * inputs, axis=-1, keepdims=True) + EPS)
    normed_one = gather_halves((inputs * scale_one * gain_one).astype(BF16), (weight_gu, weight_down))
    grad_top_own = lax.dynamic_slice(grad_out, (core * rows, 0), (rows, model_width))
    top_axes = ("dp", "tensor", "expert") if gathered else ("tensor", "expert")
    grad_top_all = lax.all_gather(grad_top_own, top_axes, axis=0, tiled=True)

    picks = jnp.sum(1 << routes, axis=1)
    facts_own = jnp.zeros((FACT_ROWS, tok_rows), BF16)
    facts_own = facts_own.at[0].set(segments.astype(BF16)).at[1].set(picks.astype(BF16))
    facts = jnp.zeros((groups, FACT_ROWS, tok_rows), BF16)
    facts = lax.dynamic_update_slice(facts, facts_own[None], (mine, 0, 0))
    for step in range(1, groups):
        came = lax.ppermute(facts_own, "expert", shift_pairs(groups, step))
        facts = lax.dynamic_update_slice(facts, came[None], (source(mine, groups, step), 0, 0))
    facts = facts.transpose(1, 0, 2).reshape(FACT_ROWS, plane_rows)
    upward = [(i, i + 1) for i in range(planes - 1)]
    seg_own = facts[:1].astype(F32)
    seg_before = jnp.where(plane > 0, lax.ppermute(facts, "dp", upward)[:1].astype(F32), -1.0)
    seg_rows = seg_own.reshape(plane_rows, 1)
    bits = jnp.concatenate(half_order(facts[1].reshape(plane_rows, 1), groups), axis=0).astype(jnp.int32)

    half = plane_rows // 2
    slot = jnp.arange(plane_rows, dtype=jnp.int32)
    half_core = (core + slot // half) % 2
    row_index = plane * plane_rows + slot % half // rows * tok_rows + half_core * rows + slot % rows
    places = (row_index % SEQ_LEN).astype(F32)
    frequency = THETA ** (-2.0 * jnp.arange(HD // 2, dtype=F32) / HD)
    angles = places[:, None] * jnp.concatenate([frequency, frequency])[None, :]
    cosine = jnp.cos(angles)
    sines = jnp.sin(angles) * jnp.where(jnp.arange(HD) < HD // 2, -1.0, 1.0)[None, :]
    place = jnp.stack([mine, core]).astype(jnp.int32)
    weights_in = (query_weight, key_weight, value_weight)
    bias_in = jnp.stack([bias.reshape(-1) for bias in (query_bias, key_bias, value_bias)])
    query_rot, own_kv = project(place, normed_one, weights_in, bias_in, cosine, sines, groups)
    before_kv = lax.ppermute(own_kv, "dp", upward)
    attended = half_order(attend(query_rot, before_kv, own_kv, seg_rows, seg_before, seg_own), groups)
    out_rows = lax.dynamic_slice(out_weight, (mine * width, 0), (width, model_width))
    after_attn = inputs + scatter_halves(*(dot(half, out_rows) for half in attended))

    gain_two = mlp_gain.astype(F32)
    scale_two = lax.rsqrt(jnp.mean(after_attn * after_attn, axis=-1, keepdims=True) + EPS)
    normed_own = (after_attn * scale_two * gain_two).astype(BF16)
    normed_two = gather_halves(normed_own)
    if gathered:
        normed_all = lax.all_gather(after(normed_own, normed_two[0]), ("dp", "tensor", "expert"), axis=0, tiled=True)
    gate_columns = jnp.concatenate([router_weight, shared_router[:, None]], axis=1)
    first_tile = 2 * plane if gathered else jnp.zeros_like(plane)
    outs, half_gates, half_probs = None, [], []
    for index in range(2):
        logits = dot(normed_two[index], gate_columns)
        chosen = (
            (bits[index * half : (index + 1) * half] >> jnp.arange(expert_count, dtype=jnp.int32)[None, :]) & 1
        ).astype(F32)
        probs = jax.nn.softmax(logits[:, :expert_count], axis=-1)
        named = lax.dynamic_slice(probs * chosen, (0, mine * local_experts), (half, local_experts))
        half_gates.append(jnp.concatenate([named, jax.nn.sigmoid(logits[:, expert_count:])], axis=1))
        half_probs.append((probs, chosen))
        first = (first_tile + (core + index) % 2).reshape(1).astype(jnp.int32)
        outs = feed(
            first, index, normed_two[index], grad_top_all, half_gates[index], weight_gu, weight_down, blocks, outs
        )
    gated, grad_hidden, slopes = outs
    gates = jnp.concatenate(half_gates, axis=0)
    router_probs, chosen = (jnp.concatenate(parts, axis=0) for parts in zip(*half_probs, strict=True))

    shared_mix = gates[:, local_experts:]
    own_slopes = jnp.concatenate([slopes[e] for e in range(local_experts)], axis=1)
    all_slopes = lax.dynamic_update_slice(
        jnp.zeros((plane_rows, expert_count), F32), own_slopes, (0, mine * local_experts)
    ) * chosen
    grad_logits = router_probs * (all_slopes - jnp.sum(router_probs * all_slopes, axis=-1, keepdims=True))
    grad_shared_logit = slopes[local_experts] * shared_mix * (1.0 - shared_mix)
    grad_small = jnp.concatenate([grad_logits, grad_shared_logit], axis=1).astype(BF16)
    grad_normed_part = (dot(grad_hidden, weight_gu) + dot_nt(grad_small, gate_columns)).astype(BF16)
    own_part = jnp.concatenate(
        [lax.dynamic_slice(part, (0, plane * part_rows), (half, part_rows)) for part in normed_two], axis=0
    )

    def mix_meanwhile(token):
        values, grads = after((gated, grad_hidden), token)
        in_order = [lax.dynamic_slice(values, ((core + k) % 2 * half, 0), (half, values.shape[1])) for k in range(2)]
        mixed_part = dot(jnp.concatenate(in_order, axis=0), weight_down).astype(BF16)
        first_sums = [dot_tn(own_part, block_grads(grads, b)) for b in range(1, blocks)] if gathered else []
        return mixed_part, first_sums

    def block_grads(grads, block):
        return grads[:, 2 * block * padded : 2 * (block + 1) * padded]

    grad_normed_two, (mixed_part, first_sums) = scatter_halves(
        grad_normed_part[:half], grad_normed_part[half:], mix_meanwhile
    )
    mixed = lax.psum_scatter(
        after(mixed_part, grad_normed_two), ("tensor", "expert"), scatter_dimension=0, tiled=True
    )
    out = both_cores((after_attn + mixed.astype(F32)).astype(BF16))
    grad_columns = functools.reduce(
        jnp.add, [dot_tn(normed_two[k], grad_small[k * half : (k + 1) * half]) for k in range(2)]
    )

    grad_mlp_gain = jnp.sum(grad_normed_two * after_attn * scale_two, axis=0)
    grad_after = grad_top_own.astype(F32) + norm_back(after_attn, scale_two, gain_two, grad_normed_two)

    plane_number = jnp.stack([plane, core]).astype(jnp.int32)
    grad_sent = grad_after.astype(BF16)
    values, grads, top_all = after((gated, grad_hidden, grad_top_all), grad_sent)
    own_sums = []
    if gathered:
        top_t = turn(plane_number, top_all, part_rows)
        own_top_t = jnp.concatenate(
            [
                lax.dynamic_slice(top_t, (0, (2 * plane + (core + k) % 2) * half), (part_rows, half))
                for k in range(2)
            ],
            axis=1,
        )
        first_sums = [dot_tn(own_part, block_grads(grads, 0)), *first_sums]
        own_sums = [
            (first_sums[b], dot(own_top_t, values[:, b * padded : (b + 1) * padded])) for b in range(blocks)
        ]
    grad_attended = gather_halves(grad_sent, tuple(own_sums))
    grad_heads = token_order(*(dot_nt(part, out_rows).astype(BF16) for part in grad_attended), groups)
    grad_query_rot, back_kv, own_kv_grad = attend_back(
        query_rot, before_kv, own_kv, seg_rows, seg_before, seg_own, grad_heads
    )

    small_rows = part_rows // groups

    def to_owners(values):
        return lax.all_to_all(values, "expert", 0, 0)

    def placed(pieces):
        total = None
        for j in range(groups):
            at = j * hidden // LANE * LANE
            piece = jnp.pad(pieces[j].astype(F32), [(0, 0), (at, groups * hidden - at - padded)])
            total = piece if total is None else total + piece
        return total

    if gathered:
        gates_sent = after(
            jnp.pad(gates.T, [(0, -gates.shape[1] % 8), (0, 0)]), back_kv
        )
        gates_came = [
            lax.ppermute(gates_sent, "dp", [((i + step) % planes, i) for i in range(planes)])
            for step in range(1, planes)
        ]
        normed_all = after(normed_all, back_kv)
        rows_t = turn(plane_number, normed_all, part_rows)
        gates_all = jnp.concatenate(gates_came, axis=1).T

        def weight_sums(block, outs, *tokens):
            return weight_grads(
                plane_number,
                planes,
                block,
                after(normed_all, *tokens),
                grad_top_all,
                rows_t,
                top_t,
                gates_all,
                (weight_gu, weight_down),
                own_sums[block],
                outs,
                groups,
                hidden,
            )

        shared_grads = weight_sums(local_experts, (local_experts,), back_kv)[0]
        shared_grads_token = shared_grads
    else:
        top_half = grad_top_all.reshape(2, half, model_width)
        top_here = jnp.concatenate(
            [lax.dynamic_slice(top_half, ((core + k) % 2, 0, 0), (1, half, model_width))[0] for k in range(2)], axis=0
        )
        gu_part = lax.psum_scatter(
            dot_tn(jnp.concatenate(normed_two, axis=0), grad_hidden).astype(BF16),
            "dp",
            scatter_dimension=0,
            tiled=True,
        )
        down_part = lax.psum_scatter(dot_tn(top_here, gated).astype(BF16), "dp", scatter_dimension=0, tiled=True)

        def block_of(values, index, size):
            return values[:, index * padded : index * padded + size]

        shared_grads = jnp.stack(
            [
                block_of(values, index, padded).reshape(groups, small_rows, padded)
                for values, index in (
                    (gu_part, 2 * local_experts),
                    (gu_part, 2 * local_experts + 1),
                    (down_part, local_experts),
                )
            ],
            axis=1,
        )
    shared_grads = to_owners(shared_grads)
    came_kv = lax.ppermute(back_kv, "dp", [(i + 1, i) for i in range(planes - 1)])
    if gathered:
        came_kv = after(came_kv, shared_grads_token)
    *grad_qkv, own_one_part, other_one_part, bias_sums = project_back(
        place, grad_query_rot, own_kv_grad, came_kv, weights_in, cosine, sines, groups
    )
    grad_part = projection_grads(normed_one, grad_attended, grad_qkv, attended)
    weight_sum = lax.psum_scatter(grad_part, "dp", scatter_dimension=0, tiled=True)
    weight_sum = weight_sum.reshape(groups, small_rows, 4, width)
    if gathered:
        expert_grads = (local_experts,)
        for e in range(local_experts - 2):
            expert_grads = weight_sums(e, expert_grads, grad_part)
        grad_normed_one, expert_grads = scatter_halves(
            own_one_part,
            other_one_part,
            lambda token: weight_sums(local_experts - 2, expert_grads, token, grad_part),
        )
        shared_grads = after(shared_grads, expert_grads)
    else:
        grad_normed_one = scatter_halves(own_one_part, other_one_part)
    grad_shared_gate = placed(shared_grads[:, 0])
    grad_shared_up = placed(shared_grads[:, 1])
    grad_shared_down = placed(shared_grads[:, 2]).T
    grad_attn_gain = jnp.sum(grad_normed_one * inputs * scale_one, axis=0)
    grad_own = grad_after + norm_back(inputs, scale_one, gain_one, grad_normed_one)
    if gathered:
        expert_grads = weight_sums(local_experts - 1, expert_grads, grad_own, weight_sum)
    else:
        expert_grads = [
            jnp.stack([block_of(values, first + stride * e, hidden).T for e in range(local_experts)]).astype(F32)
            for values, first, stride in ((gu_part, 0, 2), (gu_part, 1, 2), (down_part, 0, 1))
        ]
    grad_expert_gate, grad_expert_up = (jnp.swapaxes(grad, 1, 2) for grad in expert_grads[:2])
    grad_expert_down = expert_grads[2]
    grad_tokens = both_cores(grad_own)

    weight_rows = (
        to_owners(weight_sum).transpose(2, 1, 0, 3).reshape(4, small_rows, groups * width).astype(F32)
    )
    qkv_rows = weight_rows[:3]
    grad_out_weight = weight_rows[3].T

    bias_sums = bias_sums[0].reshape(1, 3, heads, HD)
    bias_table = lax.dynamic_update_slice(
        jnp.zeros((cores, 3, heads_here, HD), F32), bias_sums, (core, 0, mine * heads, 0)
    )
    devices = planes * groups
    spread = jnp.concatenate(
        [
            grad_attn_gain.reshape(devices, -1),
            grad_mlp_gain.reshape(devices, -1),
            grad_columns.reshape(devices, -1),
            bias_table.reshape(cores * 3 * heads_here, devices, HD // devices).transpose(1, 0, 2).reshape(devices, -1),
        ],
        axis=1,
    )
    sums = jnp.sum(lax.all_to_all(spread, ("dp", "expert"), 0, 0, tiled=True), axis=0, keepdims=True)
    sums = lax.psum(sums, "tensor")[0] if cores != 2 else (sums + lax.ppermute(sums, "tensor", [(0, 1), (1, 0)]))[0]
    gain_part = model_width // devices
    grad_attn_gain, grad_mlp_gain = sums[:gain_part], sums[gain_part : 2 * gain_part]
    table = sums[2 * gain_part :]
    column_size = gain_part * (expert_count + 1)
    column_sums = table[:column_size].reshape(gain_part, expert_count + 1)
    bias_sums = table[column_size:].reshape(cores, 3, heads_here, HD // devices)
    bias_sums = lax.dynamic_slice(bias_sums, (core, 0, 0, 0), (1, 3, heads_here, HD // devices))[0]
    return (
        out,
        grad_tokens,
        grad_attn_gain,
        qkv_rows[0],
        bias_sums[0],
        qkv_rows[1],
        bias_sums[1],
        qkv_rows[2],
        bias_sums[2],
        grad_out_weight,
        grad_mlp_gain,
        column_sums[:, :expert_count],
        column_sums[:, expert_count],
        grad_shared_gate,
        grad_shared_up,
        grad_shared_down,
        grad_expert_gate,
        grad_expert_up,
        grad_expert_down,
    )


def solution(mesh):
    tokens = ("dp", "expert")
    return jax.shard_map(
        per_device,
        mesh=mesh,
        in_specs=(
            P(tokens, None),
            P(tokens),
            P(tokens, None),
            P(),
            P(None, "tensor"),
            P("tensor", None),
            P(None, "tensor"),
            P("tensor", None),
            P(None, "tensor"),
            P("tensor", None),
            P("tensor", None),
            P(),
            P(),
            P(),
            P(None, "tensor"),
            P(None, "tensor"),
            P("tensor", None),
            P("expert", None, "tensor"),
            P("expert", None, "tensor"),
            P("expert", "tensor", None),
            P(tokens, None),
        ),
        out_specs=(
            P(tokens, None),
            P(tokens, None),
            P(tokens),
            P(tokens, "tensor"),
            P("tensor", tokens),
            P(tokens, "tensor"),
            P("tensor", tokens),
            P(tokens, "tensor"),
            P("tensor", tokens),
            P("tensor", tokens),
            P(tokens),
            P(tokens, None),
            P(tokens),
            P(tokens, "tensor"),
            P(tokens, "tensor"),
            P("tensor", tokens),
            P("expert", "dp", "tensor"),
            P("expert", "dp", "tensor"),
            P("expert", "tensor", "dp"),
        ),
        check_vma=False,
    )
```

```python
import functools

import jax
import jax.numpy as jnp
from jax import lax
from jax.experimental import pallas as pl
from jax.experimental.pallas import tpu as pltpu
from jax.sharding import PartitionSpec as P

HD = 128
SEQ_LEN = 4096
WINDOW = 1024
EPS = 1e-06
THETA = 1000000.0
NEG_LARGE = -1e30
QUERY_BLOCK = 256
FEED_BLOCK = 512
LANE = 128
FACT_ROWS = 16
GATHERED_PLANES = 4
F32 = jnp.float32
BF16 = jnp.bfloat16


def dot(left, right):
    return jnp.dot(left, right, preferred_element_type=F32)


def dot_nt(left, right):
    return lax.dot_general(left, right, (((1,), (1,)), ((), ())), preferred_element_type=F32)


def dot_tn(left, right):
    return lax.dot_general(left, right, (((0,), (0,)), ((), ())), preferred_element_type=F32)


def shift_pairs(count, step):
    if count & (count - 1) == 0:
        return [(source, source ^ step) for source in range(count)]
    return [(source, (source + step) % count) for source in range(count)]


def partner(index, count, step):
    if count & (count - 1) == 0:
        return index ^ step
    return (index + step) % count


def source(index, count, step):
    if count & (count - 1) == 0:
        return index ^ step
    return (index - step + count) % count


def gather_halves(own, meanwhile=()):
    groups, mine = lax.axis_size("expert"), lax.axis_index("expert")
    rows, width = own.shape
    pieces = jnp.zeros((groups * rows, width), own.dtype)
    pieces = lax.dynamic_update_slice(pieces, own, (mine * rows, 0))
    for step in range(1, groups):
        came = lax.ppermute(own, "expert", shift_pairs(groups, step))
        came = after(came, own, *meanwhile)
        pieces = lax.dynamic_update_slice(pieces, came, (source(mine, groups, step) * rows, 0))
    return pieces, swapped(pieces)


def swapped(values):
    return lax.ppermute(values, "tensor", [(0, 1), (1, 0)])


def scatter_halves(own, other, meanwhile=None):
    groups, mine = lax.axis_size("expert"), lax.axis_index("expert")
    held = own.astype(F32) + swapped(other.astype(BF16)).astype(F32)
    rows, width = held.shape[0] // groups, held.shape[1]

    def of_group(index):
        return lax.dynamic_slice(held, (index * rows, 0), (rows, width))

    sent = [of_group(partner(mine, groups, step)).astype(BF16) for step in range(1, groups)]
    came = [lax.ppermute(sent[step - 1], "expert", shift_pairs(groups, step)) for step in range(1, groups)]
    result = of_group(mine)
    if meanwhile is None:
        return functools.reduce(jnp.add, [part.astype(F32) for part in came], result)
    side = meanwhile(tuple(sent))
    came = lax.optimization_barrier((tuple(came), side))[0]
    return functools.reduce(jnp.add, [part.astype(F32) for part in came], result), side


def after(value, *others):
    return lax.optimization_barrier((value, *others))[0]


def both_cores(own):
    return joined(own, swapped(own))


def joined(own, other):
    core = lax.axis_index("tensor")
    return jnp.concatenate([jnp.where(core == 0, own, other), jnp.where(core == 0, other, own)], axis=0)


def token_order(own, other, groups):
    half, width = own.shape
    both = joined(own, other).reshape(2, groups, half // groups, width)
    return both.transpose(1, 0, 2, 3).reshape(2 * half, width)


def half_order(values, groups):
    total, width = values.shape
    core = lax.axis_index("tensor")
    split = values.reshape(groups, 2, total // (2 * groups), width)
    return tuple(
        lax.dynamic_slice(split, (0, index, 0, 0), (groups, 1, total // (2 * groups), width)).reshape(-1, width)
        for index in (core, 1 - core)
    )


def norm_back(values, inv_scale, gain_vec, grad_normed):
    weighted = grad_normed * gain_vec
    inner_mean = jnp.mean(weighted * values, axis=-1, keepdims=True)
    return inv_scale * weighted - values * inv_scale * inv_scale * inv_scale * inner_mean


def masked_scores(query, keys, seg_query, seg_keys, offset):
    scores = dot_nt(query, keys) * (HD ** (-0.5))
    rows, columns = scores.shape
    distance = (
        lax.broadcasted_iota(jnp.int32, (rows, columns), 0)
        - lax.broadcasted_iota(jnp.int32, (rows, columns), 1)
        + offset
    )
    allowed = (seg_query == seg_keys) & (distance >= 0) & (distance < WINDOW)
    return jnp.where(allowed, scores, NEG_LARGE)


def key_ranges(start, block, rows):
    first_before = min(rows, max(0, (start + rows - WINDOW + 1) // block * block))
    first_own = max(0, (start - WINDOW + 1) // block * block)
    return (first_before, rows), (first_own, start + block)


def probabilities(query, parts, seg_query):
    scores = [masked_scores(query, keys, seg_query, seg_keys, offset) for keys, seg_keys, offset in parts]
    top = functools.reduce(jnp.maximum, [jnp.max(part, axis=-1, keepdims=True) for part in scores])
    expo = [jnp.exp(part - top) for part in scores]
    total = functools.reduce(jnp.add, [jnp.sum(part, axis=-1, keepdims=True) for part in expo])
    inverse = 1.0 / total
    return [part * inverse for part in expo]


def key_parts(start, block, rows, before_ref, own_ref, seg_before, seg_own):
    (before, before_end), (own, own_end) = key_ranges(start, block, rows)
    ranges = []
    if before < before_end:
        ranges.append((before_ref, seg_before, before, before_end, start + rows - before))
    ranges.append((own_ref, seg_own, own, own_end, start - own))
    parts = [(ref[low:high, :HD], seg[:, low:high], offset) for ref, seg, low, high, offset in ranges]
    values = [ref[low:high, HD:] for ref, _, low, high, _ in ranges]
    return parts, values, [(low, high) for _, _, low, high, _ in ranges]


def attend_kernel(block, q_ref, before_ref, own_ref, sq_ref, sb_ref, so_ref, out_ref):
    rows = q_ref.shape[0]
    for start in range(0, rows, block):
        parts, values, _ = key_parts(start, block, rows, before_ref, own_ref, sb_ref, so_ref)
        probs = probabilities(q_ref[start : start + block, :], parts, sq_ref[start : start + block, :])
        total = functools.reduce(
            jnp.add, [dot(part.astype(BF16), value) for part, value in zip(probs, values, strict=True)]
        )
        out_ref[start : start + block, :] = total.astype(BF16)


def attend_back_kernel(
    block, q_ref, before_ref, own_ref, sq_ref, sb_ref, so_ref, grad_ref, gq_ref, gb_ref, go_ref, back_ref
):
    rows = q_ref.shape[0]
    back_ref[...] = jnp.zeros_like(back_ref)
    go_ref[...] = jnp.zeros_like(go_ref)
    scale = HD ** (-0.5)
    for start in range(0, rows, block):
        query = q_ref[start : start + block, :]
        grad = grad_ref[start : start + block, :]
        parts, values, ranges = key_parts(start, block, rows, before_ref, own_ref, sb_ref, so_ref)
        sinks = [back_ref, go_ref][-len(parts) :]
        probs = probabilities(query, parts, sq_ref[start : start + block, :])
        grad_probs = [dot_nt(grad, value) for value in values]
        delta = functools.reduce(
            jnp.add,
            [jnp.sum(p * g, axis=-1, keepdims=True) for p, g in zip(probs, grad_probs, strict=True)],
        )
        grad_query = None
        for p, g, part, sink, (low, high) in zip(probs, grad_probs, parts, sinks, ranges, strict=True):
            grad_scores = (p * (g - delta)).astype(BF16)
            term = dot(grad_scores, part[0])
            grad_query = term if grad_query is None else grad_query + term
            sink[low:high, :HD] += dot_tn(grad_scores, query) * scale
            sink[low:high, HD:] += dot_tn(p.astype(BF16), grad)
        gq_ref[start : start + block, :] = grad_query * scale
    gb_ref[...] = back_ref[...].astype(BF16)


def attention_specs(rows):
    column = pl.BlockSpec((rows, HD), lambda h: (0, h))
    pair = pl.BlockSpec((rows, 2 * HD), lambda h: (0, h))
    seg_rows = pl.BlockSpec((rows, 1), lambda h: (0, 0))
    seg_columns = pl.BlockSpec((1, rows), lambda h: (0, 0))
    return column, pair, [column, pair, pair, seg_rows, seg_columns, seg_columns]


def attend(query, before, own, seg_rows, seg_before, seg_own):
    rows, width = query.shape
    heads = width // HD
    column, _, specs = attention_specs(rows)
    return pl.pallas_call(
        functools.partial(attend_kernel, min(QUERY_BLOCK, rows)),
        grid=(heads,),
        in_specs=specs,
        out_specs=column,
        out_shape=jax.ShapeDtypeStruct((rows, width), BF16),
        compiler_params=pltpu.CompilerParams(vmem_limit_bytes=48 * 2**20),
        cost_estimate=pl.CostEstimate(
            flops=4 * rows * WINDOW * width, bytes_accessed=12 * rows * width, transcendentals=rows * WINDOW * heads
        ),
        name="attend",
    )(query, before, own, seg_rows, seg_before, seg_own)


def attend_back(query, before, own, seg_rows, seg_before, seg_own, grad_heads):
    rows, width = query.shape
    heads = width // HD
    column, pair, specs = attention_specs(rows)
    return pl.pallas_call(
        functools.partial(attend_back_kernel, min(QUERY_BLOCK, rows)),
        grid=(heads,),
        in_specs=specs + [column],
        out_specs=[column, pair, pair],
        out_shape=[
            jax.ShapeDtypeStruct((rows, width), F32),
            jax.ShapeDtypeStruct((rows, 2 * width), BF16),
            jax.ShapeDtypeStruct((rows, 2 * width), F32),
        ],
        scratch_shapes=[pltpu.VMEM((rows, 2 * HD), F32)],
        compiler_params=pltpu.CompilerParams(vmem_limit_bytes=48 * 2**20),
        cost_estimate=pl.CostEstimate(
            flops=10 * rows * WINDOW * width, bytes_accessed=32 * rows * width, transcendentals=rows * WINDOW * heads
        ),
        name="attend_back",
    )(query, before, own, seg_rows, seg_before, seg_own, grad_heads)


def turned(values, cosine, sines):
    return values * cosine + pltpu.roll(values, HD // 2, 1) * sines


def half_rows(index, group, rows, core):
    return pl.ds(pl.multiple_of(2 * group * rows + lax.rem(core + index, 2) * rows, rows), rows)


def project_kernel(
    groups, place_ref, own_ref, other_ref, wq_ref, wk_ref, wv_ref, bias_ref, cos_ref, sin_ref, q_ref, kv_ref
):
    core = place_ref[1]
    half, width = own_ref.shape[0], wq_ref.shape[1]
    rows = half // groups
    for index, ref in enumerate((own_ref, other_ref)):
        here = slice(index * half, (index + 1) * half)
        cosine, sines = cos_ref[here, :], sin_ref[here, :]
        normed = ref[...]
        for k, weight in enumerate((wq_ref, wk_ref, wv_ref)):
            product = dot(normed, weight[...]) + bias_ref[k : k + 1, :].astype(F32)
            for h in range(width // HD):
                values = product[:, h * HD : (h + 1) * HD]
                if k < 2:
                    values = turned(values, cosine, sines)
                values = values.astype(BF16)
                out, at = (q_ref, h * HD) if k == 0 else (kv_ref, (2 * h + k - 1) * HD)
                for group in range(groups):
                    out[half_rows(index, group, rows, core), at : at + HD] = values[group * rows : (group + 1) * rows]


def project(place, halves, weights, bias, cosine, sines, groups):
    half, model_width = halves[0].shape
    width = weights[0].shape[1] // groups
    whole = pl.BlockSpec((half, model_width), lambda i, p: (0, 0))
    weight_spec = pl.BlockSpec((model_width, width), lambda i, p: (0, p[0]))
    table = pl.BlockSpec((2 * half, HD), lambda i, p: (0, 0))
    return pl.pallas_call(
        functools.partial(project_kernel, groups),
        grid_spec=pltpu.PrefetchScalarGridSpec(
            num_scalar_prefetch=1,
            grid=(1,),
            in_specs=[whole, whole]
            + [weight_spec] * 3
            + [pl.BlockSpec((3, width), lambda i, p: (0, p[0])), table, table],
            out_specs=[
                pl.BlockSpec((2 * half, width), lambda i, p: (0, 0)),
                pl.BlockSpec((2 * half, 2 * width), lambda i, p: (0, 0)),
            ],
        ),
        out_shape=[
            jax.ShapeDtypeStruct((2 * half, width), BF16),
            jax.ShapeDtypeStruct((2 * half, 2 * width), BF16),
        ],
        compiler_params=pltpu.CompilerParams(vmem_limit_bytes=48 * 2**20),
        cost_estimate=pl.CostEstimate(
            flops=12 * half * model_width * width,
            bytes_accessed=4 * half * model_width + 6 * model_width * width,
            transcendentals=0,
        ),
        name="project",
    )(place, *halves, *weights, bias, cosine, sines)


def project_back_kernel(
    groups,
    place_ref,
    gq_ref,
    go_ref,
    came_ref,
    wq_ref,
    wk_ref,
    wv_ref,
    cos_ref,
    sin_ref,
    own_ref,
    other_ref,
    own_part,
    other_part,
    bias_ref,
):
    core = place_ref[1]
    half, width = own_ref.shape[0], gq_ref.shape[1]
    rows = half // groups
    columns = min(512, own_part.shape[1])
    bias_sum = jnp.zeros((1, 3 * width), F32)
    for index, (out, part) in enumerate(((own_ref, own_part), (other_ref, other_part))):
        here = slice(index * half, (index + 1) * half)
        cosine, sines = cos_ref[here, :], sin_ref[here, :]
        for k in range(3):
            for h in range(width // HD):
                pieces = []
                for group in range(groups):
                    at_rows = half_rows(index, group, rows, core)
                    if k == 0:
                        pieces.append(gq_ref[at_rows, h * HD : (h + 1) * HD])
                    else:
                        at = (2 * h + k - 1) * HD
                        pieces.append(go_ref[at_rows, at : at + HD] + came_ref[at_rows, at : at + HD].astype(F32))
                values = jnp.concatenate(pieces, axis=0)
                if k < 2:
                    values = turned(values, cosine, -sines)
                out[:, k * width + h * HD : k * width + (h + 1) * HD] = values.astype(BF16)
        grads = out[...]
        bias_sum = bias_sum + jnp.sum(grads.astype(F32), axis=0, keepdims=True)
        for at in range(0, part.shape[1], columns):
            total = dot_nt(grads[:, :width], wq_ref[at : at + columns, :])
            total = total + dot_nt(grads[:, width : 2 * width], wk_ref[at : at + columns, :])
            total = total + dot_nt(grads[:, 2 * width :], wv_ref[at : at + columns, :])
            part[:, at : at + columns] = total.astype(BF16)
    bias_ref[...] = jnp.broadcast_to(bias_sum, bias_ref.shape)


def project_back(place, grad_query, own_kv_grad, came_kv, weights, cosine, sines, groups):
    total, width = grad_query.shape
    half = total // 2
    model_width = weights[0].shape[0]
    weight_spec = pl.BlockSpec((model_width, width), lambda i, p: (0, p[0]))

    def full(*shape):
        return pl.BlockSpec(shape, lambda i, p: (0, 0))

    return pl.pallas_call(
        functools.partial(project_back_kernel, groups),
        grid_spec=pltpu.PrefetchScalarGridSpec(
            num_scalar_prefetch=1,
            grid=(1,),
            in_specs=[full(total, width), full(total, 2 * width), full(total, 2 * width)]
            + [weight_spec] * 3
            + [full(total, HD)] * 2,
            out_specs=[full(half, 3 * width)] * 2 + [full(half, model_width)] * 2 + [full(8, 3 * width)],
        ),
        out_shape=[jax.ShapeDtypeStruct((half, 3 * width), BF16)] * 2
        + [jax.ShapeDtypeStruct((half, model_width), BF16)] * 2
        + [jax.ShapeDtypeStruct((8, 3 * width), F32)],
        compiler_params=pltpu.CompilerParams(vmem_limit_bytes=48 * 2**20),
        cost_estimate=pl.CostEstimate(
            flops=12 * half * model_width * width,
            bytes_accessed=8 * half * model_width + 6 * model_width * width,
            transcendentals=0,
        ),
        name="project_back",
    )(place, grad_query, own_kv_grad, came_kv, *weights, cosine, sines)


def projection_grads_kernel(n0, n1, d0, d1, g0, g1, a0, a1, out_ref):
    width = g0.shape[1]
    out_ref[:, :width] = (dot_tn(n0[...], g0[...]) + dot_tn(n1[...], g1[...])).astype(BF16)
    out_ref[:, width:] = (dot_tn(d0[...], a0[...]) + dot_tn(d1[...], a1[...])).astype(BF16)


def projection_grads(normed, grads_after, grads, attended):
    half, model_width = normed[0].shape
    width = grads[0].shape[1] + attended[0].shape[1]
    tile = min(512, model_width)
    wide = pl.BlockSpec((half, tile), lambda i: (0, i))
    return pl.pallas_call(
        projection_grads_kernel,
        grid=(model_width // tile,),
        in_specs=[wide] * 4
        + [pl.BlockSpec(grads[0].shape, lambda i: (0, 0))] * 2
        + [pl.BlockSpec(attended[0].shape, lambda i: (0, 0))] * 2,
        out_specs=pl.BlockSpec((tile, width), lambda i: (i, 0)),
        out_shape=jax.ShapeDtypeStruct((model_width, width), BF16),
        compiler_params=pltpu.CompilerParams(vmem_limit_bytes=40 * 2**20),
        cost_estimate=pl.CostEstimate(
            flops=4 * half * model_width * width, bytes_accessed=8 * half * model_width, transcendentals=0
        ),
        name="projection_grads",
    )(*normed, *grads_after, *grads, *attended)


def hidden_grads(rows, top, gate, weight_gu, weight_down):
    hidden = weight_down.shape[0]
    both = dot_nt(rows, weight_gu)
    inner_grad = dot_nt(top, weight_down)
    gate_val, up_val = both[:, :hidden], both[:, hidden:]
    sigmoid_val = jax.nn.sigmoid(gate_val)
    silu_val = gate_val * sigmoid_val
    inner = silu_val * up_val
    slope = jnp.sum(inner * inner_grad, axis=-1, keepdims=True)
    inner_grad = inner_grad * gate
    gated = (inner * gate).astype(BF16)
    grad_gate_val = (inner_grad * up_val * (sigmoid_val + silu_val * (1.0 - sigmoid_val))).astype(BF16)
    grad_up_val = (inner_grad * silu_val).astype(BF16)
    return gated, grad_gate_val, grad_up_val, slope


def gate_of(gates, block):
    lane = lax.broadcasted_iota(jnp.int32, gates.shape, 1)
    return jnp.sum(jnp.where(lane == block, gates, 0.0), axis=1, keepdims=True)


def feed_kernel(
    first_ref, own_ref, other_ref, top_own, top_other, gates_ref, gu_ref, down_ref, gated_ref, grad_ref, slope_ref
):
    del first_ref
    hidden = down_ref.shape[0]
    half = own_ref.shape[0]
    for index, (rows, top) in enumerate(((own_ref, top_own), (other_ref, top_other))):
        here = slice(index * half, (index + 1) * half)
        gate = gate_of(gates_ref[here, :], pl.program_id(0))
        gated, grad_gate_val, grad_up_val, slope = hidden_grads(rows[...], top[...], gate, gu_ref[...], down_ref[...])
        gated_ref[here, :] = gated
        grad_ref[here, :hidden] = grad_gate_val
        grad_ref[here, hidden:] = grad_up_val
        slope_ref[0, here] = slope


def weight_kernel(
    routed,
    hidden_out,
    chunk_ref,
    rows_ref,
    top_ref,
    rows_t_ref,
    top_t_ref,
    gates_ref,
    gu_ref,
    down_ref,
    gu_in,
    down_in,
    *rest,
):
    del chunk_ref
    sums = rest[-3:]
    gate_sum, up_sum, down_sum = sums
    hidden = down_ref.shape[0]
    step = pl.program_id(0)

    @pl.when(step == 0)
    def _():
        gate_sum[...] = gu_in[:, :hidden]
        up_sum[...] = gu_in[:, hidden:]
        down_sum[...] = down_in[...]

    gate = gate_of(gates_ref[...], routed)
    gated, grad_gate_val, grad_up_val, _ = hidden_grads(
        rows_ref[...], top_ref[...], gate, gu_ref[...], down_ref[...]
    )
    gate_sum[...] += dot(rows_t_ref[...], grad_gate_val)
    up_sum[...] += dot(rows_t_ref[...], grad_up_val)
    down_sum[...] += dot(top_t_ref[...], gated)

    @pl.when(step == pl.num_programs(0) - 1)
    def _():
        if len(rest[-4].shape) == 3:
            for out, total in zip(rest[-6:-3], sums, strict=True):
                out[0] = total[...].T[:hidden_out]
        else:
            out = rest[-4]
            groups, _, part = out.shape[:3]
            for g in range(groups):
                for k, total in enumerate(sums):
                    out[g, k] = total[g * part : (g + 1) * part, :].astype(BF16)


def pack_kernel(local, hidden, units, window_ref, *refs):
    gate_ref, up_ref, down_ref = refs[:3]
    shared_gate, shared_up = refs[3 : 3 + units], refs[3 + units : 3 + 2 * units]
    shared_down = refs[3 + 2 * units : 3 + 3 * units]
    gu_out, down_out = refs[-2:]
    padded = units * LANE
    columns = down_out.shape[1]
    for e in range(local):
        for ref, out, at in ((gate_ref, gu_out, 2 * e), (up_ref, gu_out, 2 * e + 1), (down_ref, down_out, e)):
            out[at * padded : at * padded + hidden, :] = ref[e]
            if hidden < padded:
                out[at * padded + hidden : (at + 1) * padded, :] = jnp.zeros((padded - hidden, columns), BF16)
    skip = window_ref[1]
    for k in range(units):
        line = lax.broadcasted_iota(jnp.int32, (LANE, columns), 0) + k * LANE
        keep = (line >= skip) & (line < skip + hidden)
        for block, out, at in (
            (shared_gate[k][...].T, gu_out, 2 * local),
            (shared_up[k][...].T, gu_out, 2 * local + 1),
            (shared_down[k][...], down_out, local),
        ):
            out[at * padded + k * LANE : at * padded + (k + 1) * LANE, :] = jnp.where(
                keep, block.astype(F32), 0.0
            ).astype(BF16)


def pack_weights(window, expert_gate, expert_up, expert_down, shared_gate, shared_up, shared_down, padded):
    local, hidden, model_width = expert_down.shape
    units = padded // LANE
    blocks = local + 1
    tile = min(256, model_width)
    expert_spec = pl.BlockSpec((local, hidden, tile), lambda i, w: (0, 0, i))
    column_specs = [pl.BlockSpec((tile, LANE), lambda i, w, k=k: (i, w[0] + k)) for k in range(units)]
    row_specs = [pl.BlockSpec((LANE, tile), lambda i, w, k=k: (w[0] + k, i)) for k in range(units)]
    return pl.pallas_call(
        functools.partial(pack_kernel, local, hidden, units),
        grid_spec=pltpu.PrefetchScalarGridSpec(
            num_scalar_prefetch=1,
            grid=(model_width // tile,),
            in_specs=[expert_spec] * 3 + column_specs * 2 + row_specs,
            out_specs=[
                pl.BlockSpec((2 * blocks * padded, tile), lambda i, w: (0, i)),
                pl.BlockSpec((blocks * padded, tile), lambda i, w: (0, i)),
            ],
        ),
        out_shape=[
            jax.ShapeDtypeStruct((2 * blocks * padded, model_width), BF16),
            jax.ShapeDtypeStruct((blocks * padded, model_width), BF16),
        ],
        compiler_params=pltpu.CompilerParams(vmem_limit_bytes=40 * 2**20),
        cost_estimate=pl.CostEstimate(
            flops=0, bytes_accessed=12 * blocks * padded * model_width, transcendentals=0
        ),
        name="pack_weights",
    )(
        window,
        jnp.swapaxes(expert_gate, 1, 2),
        jnp.swapaxes(expert_up, 1, 2),
        expert_down,
        *([shared_gate] * units),
        *([shared_up] * units),
        *([shared_down] * units),
    )


def turn_kernel(plane_ref, part_ref, out_ref):
    del plane_ref
    out_ref[...] = part_ref[...].T


def turn(plane, values, part):
    total = values.shape[0]
    tile = min(1024, total)
    return pl.pallas_call(
        turn_kernel,
        grid_spec=pltpu.PrefetchScalarGridSpec(
            num_scalar_prefetch=1,
            grid=(total // tile,),
            in_specs=[pl.BlockSpec((tile, part), lambda i, p: (i, p[0]))],
            out_specs=pl.BlockSpec((part, tile), lambda i, p: (0, i)),
        ),
        out_shape=jax.ShapeDtypeStruct((part, total), BF16),
        compiler_params=pltpu.CompilerParams(vmem_limit_bytes=40 * 2**20),
        cost_estimate=pl.CostEstimate(flops=0, bytes_accessed=4 * total * part, transcendentals=0),
        name="turn",
    )(plane, values)


def feed(first_tiles, halves, top_all, gates, weight_gu, weight_down, blocks):
    half, model_width = halves[0].shape
    hidden = weight_down.shape[0] // blocks
    whole = 2 * half
    rows = pl.BlockSpec((half, model_width), lambda s, c: (0, 0))
    grid_spec = pltpu.PrefetchScalarGridSpec(
        num_scalar_prefetch=1,
        grid=(blocks,),
        in_specs=[rows, rows]
        + [pl.BlockSpec((half, model_width), lambda s, c, k=k: (c[k], 0)) for k in range(2)]
        + [
            pl.BlockSpec(gates.shape, lambda s, c: (0, 0)),
            pl.BlockSpec((2 * hidden, model_width), lambda s, c: (s, 0)),
            pl.BlockSpec((hidden, model_width), lambda s, c: (s, 0)),
        ],
        out_specs=[
            pl.BlockSpec((whole, hidden), lambda s, c: (0, s)),
            pl.BlockSpec((whole, 2 * hidden), lambda s, c: (0, s)),
            pl.BlockSpec((1, whole, 1), lambda s, c: (s, 0, 0)),
        ],
    )
    return pl.pallas_call(
        feed_kernel,
        grid_spec=grid_spec,
        out_shape=[
            jax.ShapeDtypeStruct((whole, blocks * hidden), BF16),
            jax.ShapeDtypeStruct((whole, 2 * blocks * hidden), BF16),
            jax.ShapeDtypeStruct((blocks, whole, 1), F32),
        ],
        compiler_params=pltpu.CompilerParams(vmem_limit_bytes=62 * 2**20),
        cost_estimate=pl.CostEstimate(
            flops=6 * whole * model_width * hidden * blocks,
            bytes_accessed=6 * model_width * hidden * blocks + 4 * whole * model_width,
            transcendentals=whole * hidden * blocks,
        ),
        name="feed",
    )(first_tiles, *halves, top_all, top_all, gates, weight_gu, weight_down)


def weight_grads(plane, planes, block, rows_all, top_all, rows_t, top_t, gates, packed, sums, outs, groups, hidden):
    weight_gu, weight_down = packed
    total, model_width = rows_all.shape
    count = total // planes
    part = rows_t.shape[0]
    padded = sums[1].shape[1]
    tile = min(FEED_BLOCK, count // 2)
    steps = count // tile
    local = outs[0] if isinstance(outs[0], int) else outs[0].shape[0]

    half_steps = max(1, steps // 2)

    def at(i, c):
        place = lax.rem(i, steps)
        half = lax.rem(place // half_steps + c[1], 2)
        return lax.rem(c[0] + 1 + i // steps, planes) * steps + half * half_steps + lax.rem(place, half_steps)

    tokens = pl.BlockSpec((tile, model_width), lambda i, c: (at(i, c), 0))
    turned = pl.BlockSpec((part, tile), lambda i, c: (0, at(i, c)))
    in_specs = [
        tokens,
        tokens,
        turned,
        turned,
        pl.BlockSpec((tile, gates.shape[1]), lambda i, c: (i, 0)),
        pl.BlockSpec((2 * padded, model_width), lambda i, c: (block, 0)),
        pl.BlockSpec((padded, model_width), lambda i, c: (block, 0)),
        pl.BlockSpec((part, 2 * padded), lambda i, c: (0, 0)),
        pl.BlockSpec((part, padded), lambda i, c: (0, 0)),
    ]
    args = [rows_all, top_all, rows_t, top_t, gates, weight_gu, weight_down, *sums]
    aliases = {}
    if block < local:
        out_shape = [jax.ShapeDtypeStruct((local, hidden, part), F32)] * 3
        out_specs = [pl.BlockSpec((1, hidden, part), lambda i, c: (block, 0, 0))] * 3
        if not isinstance(outs[0], int):
            in_specs += [pl.BlockSpec(memory_space=pl.ANY)] * 3
            aliases = {len(args) + 1 + k: k for k in range(3)}
            args += list(outs)
    else:
        out_shape = [jax.ShapeDtypeStruct((groups, 3, part // groups, padded), BF16)]
        out_specs = [pl.BlockSpec(out_shape[0].shape, lambda i, c: (0, 0, 0, 0))]
    return pl.pallas_call(
        functools.partial(weight_kernel, block, hidden),
        grid_spec=pltpu.PrefetchScalarGridSpec(
            num_scalar_prefetch=1,
            grid=((planes - 1) * steps,),
            in_specs=in_specs,
            out_specs=out_specs,
            scratch_shapes=[pltpu.VMEM((part, padded), F32)] * 3,
        ),
        out_shape=out_shape,
        input_output_aliases=aliases,
        compiler_params=pltpu.CompilerParams(vmem_limit_bytes=62 * 2**20),
        cost_estimate=pl.CostEstimate(
            flops=6 * (total - count) * (model_width + part) * padded,
            bytes_accessed=6 * model_width * padded + 4 * total * model_width,
            transcendentals=total * padded,
        ),
        name="weight_grads",
    )(plane, *args)


def per_device(
    tokens,
    segments,
    routes,
    attn_gain,
    query_weight,
    query_bias,
    key_weight,
    key_bias,
    value_weight,
    value_bias,
    out_weight,
    mlp_gain,
    router_weight,
    shared_router,
    shared_gate,
    shared_up,
    shared_down,
    expert_gate,
    expert_up,
    expert_down,
    grad_out,
):
    tok_rows, model_width = tokens.shape
    groups, cores = lax.axis_size("expert"), lax.axis_size("tensor")
    planes = lax.axis_size("dp")
    mine, core, plane = lax.axis_index("expert"), lax.axis_index("tensor"), lax.axis_index("dp")
    rows = tok_rows // cores
    plane_rows = tok_rows * groups
    heads_here = query_weight.shape[1] // HD
    width = query_weight.shape[1] // groups
    heads = width // HD
    local_experts, _, hidden = expert_gate.shape
    expert_count = local_experts * groups
    blocks = local_experts + 1
    gathered = planes <= GATHERED_PLANES
    padded = -(-hidden // LANE) * LANE
    part_rows = model_width // planes

    first_unit = mine * hidden // LANE
    window = jnp.stack([first_unit, mine * hidden - first_unit * LANE]).astype(jnp.int32)
    weight_gu, weight_down = pack_weights(
        window, expert_gate, expert_up, expert_down, shared_gate, shared_up, shared_down, padded
    )

    own_tokens = lax.dynamic_slice(tokens, (core * rows, 0), (rows, model_width))
    inputs = own_tokens.astype(F32)
    gain_one = attn_gain.astype(F32)
    scale_one = lax.rsqrt(jnp.mean(inputs * inputs, axis=-1, keepdims=True) + EPS)
    normed_one = gather_halves((inputs * scale_one * gain_one).astype(BF16), (weight_gu, weight_down))
    grad_top_own = lax.dynamic_slice(grad_out, (core * rows, 0), (rows, model_width))
    top_axes = ("dp", "tensor", "expert") if gathered else ("tensor", "expert")
    grad_top_all = lax.all_gather(grad_top_own, top_axes, axis=0, tiled=True)

    picks = jnp.sum(1 << routes, axis=1)
    facts_own = jnp.zeros((FACT_ROWS, tok_rows), BF16)
    facts_own = facts_own.at[0].set(segments.astype(BF16)).at[1].set(picks.astype(BF16))
    facts = jnp.zeros((groups, FACT_ROWS, tok_rows), BF16)
    facts = lax.dynamic_update_slice(facts, facts_own[None], (mine, 0, 0))
    for step in range(1, groups):
        came = lax.ppermute(facts_own, "expert", shift_pairs(groups, step))
        facts = lax.dynamic_update_slice(facts, came[None], (source(mine, groups, step), 0, 0))
    facts = facts.transpose(1, 0, 2).reshape(FACT_ROWS, plane_rows)
    upward = [(i, i + 1) for i in range(planes - 1)]
    seg_own = facts[:1].astype(F32)
    seg_before = jnp.where(plane > 0, lax.ppermute(facts, "dp", upward)[:1].astype(F32), -1.0)
    seg_rows = seg_own.reshape(plane_rows, 1)
    bits = jnp.concatenate(half_order(facts[1].reshape(plane_rows, 1), groups), axis=0).astype(jnp.int32)

    half = plane_rows // 2
    slot = jnp.arange(plane_rows, dtype=jnp.int32)
    half_core = (core + slot // half) % 2
    row_index = plane * plane_rows + slot % half // rows * tok_rows + half_core * rows + slot % rows
    places = (row_index % SEQ_LEN).astype(F32)
    frequency = THETA ** (-2.0 * jnp.arange(HD // 2, dtype=F32) / HD)
    angles = places[:, None] * jnp.concatenate([frequency, frequency])[None, :]
    cosine = jnp.cos(angles)
    sines = jnp.sin(angles) * jnp.where(jnp.arange(HD) < HD // 2, -1.0, 1.0)[None, :]
    place = jnp.stack([mine, core]).astype(jnp.int32)
    weights_in = (query_weight, key_weight, value_weight)
    bias_in = jnp.stack([bias.reshape(-1) for bias in (query_bias, key_bias, value_bias)])
    query_rot, own_kv = project(place, normed_one, weights_in, bias_in, cosine, sines, groups)
    before_kv = lax.ppermute(own_kv, "dp", upward)
    attended = half_order(attend(query_rot, before_kv, own_kv, seg_rows, seg_before, seg_own), groups)
    out_rows = lax.dynamic_slice(out_weight, (mine * width, 0), (width, model_width))
    after_attn = inputs + scatter_halves(*(dot(half, out_rows) for half in attended))

    gain_two = mlp_gain.astype(F32)
    scale_two = lax.rsqrt(jnp.mean(after_attn * after_attn, axis=-1, keepdims=True) + EPS)
    normed_own = (after_attn * scale_two * gain_two).astype(BF16)
    normed_two = gather_halves(normed_own)
    if gathered:
        normed_all = lax.all_gather(after(normed_own, normed_two[0]), ("dp", "tensor", "expert"), axis=0, tiled=True)
    gate_columns = jnp.concatenate([router_weight, shared_router[:, None]], axis=1)
    first_tile = 2 * plane if gathered else jnp.zeros_like(plane)
    top_tiles = jnp.stack([first_tile + (core + k) % 2 for k in range(2)]).astype(jnp.int32)
    half_gates, half_probs = [], []
    for index in range(2):
        logits = dot(normed_two[index], gate_columns)
        chosen = (
            (bits[index * half : (index + 1) * half] >> jnp.arange(expert_count, dtype=jnp.int32)[None, :]) & 1
        ).astype(F32)
        probs = jax.nn.softmax(logits[:, :expert_count], axis=-1)
        named = lax.dynamic_slice(probs * chosen, (0, mine * local_experts), (half, local_experts))
        half_gates.append(jnp.concatenate([named, jax.nn.sigmoid(logits[:, expert_count:])], axis=1))
        half_probs.append((probs, chosen))
    gates = jnp.concatenate(half_gates, axis=0)
    gated, grad_hidden, slopes = feed(
        top_tiles, normed_two, grad_top_all, gates, weight_gu, weight_down, blocks
    )
    router_probs, chosen = (jnp.concatenate(parts, axis=0) for parts in zip(*half_probs, strict=True))

    shared_mix = gates[:, local_experts:]
    own_slopes = jnp.concatenate([slopes[e] for e in range(local_experts)], axis=1)
    all_slopes = lax.dynamic_update_slice(
        jnp.zeros((plane_rows, expert_count), F32), own_slopes, (0, mine * local_experts)
    ) * chosen
    grad_logits = router_probs * (all_slopes - jnp.sum(router_probs * all_slopes, axis=-1, keepdims=True))
    grad_shared_logit = slopes[local_experts] * shared_mix * (1.0 - shared_mix)
    grad_small = jnp.concatenate([grad_logits, grad_shared_logit], axis=1).astype(BF16)
    grad_normed_part = (dot(grad_hidden, weight_gu) + dot_nt(grad_small, gate_columns)).astype(BF16)
    own_part = jnp.concatenate(
        [lax.dynamic_slice(part, (0, plane * part_rows), (half, part_rows)) for part in normed_two], axis=0
    )

    def mix_meanwhile(token):
        values, grads = after((gated, grad_hidden), token)
        in_order = [lax.dynamic_slice(values, ((core + k) % 2 * half, 0), (half, values.shape[1])) for k in range(2)]
        mixed_part = dot(jnp.concatenate(in_order, axis=0), weight_down).astype(BF16)
        first_sums = [dot_tn(own_part, block_grads(grads, b)) for b in range(1, blocks)] if gathered else []
        return mixed_part, first_sums

    def block_grads(grads, block):
        return grads[:, 2 * block * padded : 2 * (block + 1) * padded]

    grad_normed_two, (mixed_part, first_sums) = scatter_halves(
        grad_normed_part[:half], grad_normed_part[half:], mix_meanwhile
    )
    mixed = lax.psum_scatter(
        after(mixed_part, grad_normed_two), ("tensor", "expert"), scatter_dimension=0, tiled=True
    )
    out = both_cores((after_attn + mixed.astype(F32)).astype(BF16))
    grad_columns = functools.reduce(
        jnp.add, [dot_tn(normed_two[k], grad_small[k * half : (k + 1) * half]) for k in range(2)]
    )

    grad_mlp_gain = jnp.sum(grad_normed_two * after_attn * scale_two, axis=0)
    grad_after = grad_top_own.astype(F32) + norm_back(after_attn, scale_two, gain_two, grad_normed_two)

    plane_number = jnp.stack([plane, core]).astype(jnp.int32)
    grad_sent = grad_after.astype(BF16)
    values, grads, top_all = after((gated, grad_hidden, grad_top_all), grad_sent)
    own_sums = []
    if gathered:
        top_t = turn(plane_number, top_all, part_rows)
        own_top_t = jnp.concatenate(
            [
                lax.dynamic_slice(top_t, (0, (2 * plane + (core + k) % 2) * half), (part_rows, half))
                for k in range(2)
            ],
            axis=1,
        )
        first_sums = [dot_tn(own_part, block_grads(grads, 0)), *first_sums]
        own_sums = [
            (first_sums[b], dot(own_top_t, values[:, b * padded : (b + 1) * padded])) for b in range(blocks)
        ]
    grad_attended = gather_halves(grad_sent, tuple(own_sums))
    grad_heads = token_order(*(dot_nt(part, out_rows).astype(BF16) for part in grad_attended), groups)
    grad_query_rot, back_kv, own_kv_grad = attend_back(
        query_rot, before_kv, own_kv, seg_rows, seg_before, seg_own, grad_heads
    )

    small_rows = part_rows // groups

    def to_owners(values):
        return lax.all_to_all(values, "expert", 0, 0)

    def placed(pieces):
        total = None
        for j in range(groups):
            at = j * hidden // LANE * LANE
            piece = jnp.pad(pieces[j].astype(F32), [(0, 0), (at, groups * hidden - at - padded)])
            total = piece if total is None else total + piece
        return total

    if gathered:
        gates_sent = after(
            jnp.pad(gates.T, [(0, -gates.shape[1] % 8), (0, 0)]), back_kv
        )
        gates_came = [
            lax.ppermute(gates_sent, "dp", [((i + step) % planes, i) for i in range(planes)])
            for step in range(1, planes)
        ]
        normed_all = after(normed_all, back_kv)
        rows_t = turn(plane_number, normed_all, part_rows)
        gates_all = jnp.concatenate(gates_came, axis=1).T

        def weight_sums(block, outs, *tokens):
            return weight_grads(
                plane_number,
                planes,
                block,
                after(normed_all, *tokens),
                grad_top_all,
                rows_t,
                top_t,
                gates_all,
                (weight_gu, weight_down),
                own_sums[block],
                outs,
                groups,
                hidden,
            )

        shared_grads = weight_sums(local_experts, (local_experts,), back_kv)[0]
        shared_grads_token = shared_grads
    else:
        top_half = grad_top_all.reshape(2, half, model_width)
        top_here = jnp.concatenate(
            [lax.dynamic_slice(top_half, ((core + k) % 2, 0, 0), (1, half, model_width))[0] for k in range(2)], axis=0
        )
        gu_part = lax.psum_scatter(
            dot_tn(jnp.concatenate(normed_two, axis=0), grad_hidden).astype(BF16),
            "dp",
            scatter_dimension=0,
            tiled=True,
        )
        down_part = lax.psum_scatter(dot_tn(top_here, gated).astype(BF16), "dp", scatter_dimension=0, tiled=True)

        def block_of(values, index, size):
            return values[:, index * padded : index * padded + size]

        shared_grads = jnp.stack(
            [
                block_of(values, index, padded).reshape(groups, small_rows, padded)
                for values, index in (
                    (gu_part, 2 * local_experts),
                    (gu_part, 2 * local_experts + 1),
                    (down_part, local_experts),
                )
            ],
            axis=1,
        )
    shared_grads = to_owners(shared_grads)
    came_kv = lax.ppermute(back_kv, "dp", [(i + 1, i) for i in range(planes - 1)])
    if gathered:
        came_kv = after(came_kv, shared_grads_token)
    *grad_qkv, own_one_part, other_one_part, bias_sums = project_back(
        place, grad_query_rot, own_kv_grad, came_kv, weights_in, cosine, sines, groups
    )
    grad_part = projection_grads(normed_one, grad_attended, grad_qkv, attended)
    def attn_gain_of(grads):
        return jnp.sum(grads * inputs * scale_one, axis=0)

    weight_sum = lax.psum_scatter(grad_part, "dp", scatter_dimension=0, tiled=True)
    weight_sum = weight_sum.reshape(groups, small_rows, 4, width)
    if gathered:
        expert_grads = (local_experts,)
        for e in range(local_experts - 2):
            expert_grads = weight_sums(e, expert_grads, grad_part)
        grad_normed_one, expert_grads = scatter_halves(
            own_one_part,
            other_one_part,
            lambda token: weight_sums(local_experts - 2, expert_grads, token, grad_part),
        )
        shared_grads, grad_attn_gain = after((shared_grads, attn_gain_of(grad_normed_one)), expert_grads)
    else:
        grad_normed_one = scatter_halves(own_one_part, other_one_part)
        grad_attn_gain = attn_gain_of(grad_normed_one)
    grad_shared_gate = placed(shared_grads[:, 0])
    grad_shared_up = placed(shared_grads[:, 1])
    grad_shared_down = placed(shared_grads[:, 2]).T
    grad_own = grad_after + norm_back(inputs, scale_one, gain_one, grad_normed_one)
    if gathered:
        expert_grads = weight_sums(local_experts - 1, expert_grads, grad_own, weight_sum)
    else:
        expert_grads = [
            jnp.stack([block_of(values, first + stride * e, hidden).T for e in range(local_experts)]).astype(F32)
            for values, first, stride in ((gu_part, 0, 2), (gu_part, 1, 2), (down_part, 0, 1))
        ]
    grad_expert_gate, grad_expert_up = (jnp.swapaxes(grad, 1, 2) for grad in expert_grads[:2])
    grad_expert_down = expert_grads[2]
    grad_tokens = both_cores(grad_own)

    weight_rows = (
        to_owners(weight_sum).transpose(2, 1, 0, 3).reshape(4, small_rows, groups * width).astype(F32)
    )
    qkv_rows = weight_rows[:3]
    grad_out_weight = weight_rows[3].T

    bias_sums = bias_sums[0].reshape(1, 3, heads, HD)
    bias_table = lax.dynamic_update_slice(
        jnp.zeros((cores, 3, heads_here, HD), F32), bias_sums, (core, 0, mine * heads, 0)
    )
    devices = planes * groups
    spread = jnp.concatenate(
        [
            grad_attn_gain.reshape(devices, -1),
            grad_mlp_gain.reshape(devices, -1),
            grad_columns.reshape(devices, -1),
            bias_table.reshape(cores * 3 * heads_here, devices, HD // devices).transpose(1, 0, 2).reshape(devices, -1),
        ],
        axis=1,
    )
    sums = jnp.sum(lax.all_to_all(spread, ("dp", "expert"), 0, 0, tiled=True), axis=0, keepdims=True)
    sums = lax.psum(sums, "tensor")[0] if cores != 2 else (sums + lax.ppermute(sums, "tensor", [(0, 1), (1, 0)]))[0]
    gain_part = model_width // devices
    grad_attn_gain, grad_mlp_gain = sums[:gain_part], sums[gain_part : 2 * gain_part]
    table = sums[2 * gain_part :]
    column_size = gain_part * (expert_count + 1)
    column_sums = table[:column_size].reshape(gain_part, expert_count + 1)
    bias_sums = table[column_size:].reshape(cores, 3, heads_here, HD // devices)
    bias_sums = lax.dynamic_slice(bias_sums, (core, 0, 0, 0), (1, 3, heads_here, HD // devices))[0]
    return (
        out,
        grad_tokens,
        grad_attn_gain,
        qkv_rows[0],
        bias_sums[0],
        qkv_rows[1],
        bias_sums[1],
        qkv_rows[2],
        bias_sums[2],
        grad_out_weight,
        grad_mlp_gain,
        column_sums[:, :expert_count],
        column_sums[:, expert_count],
        grad_shared_gate,
        grad_shared_up,
        grad_shared_down,
        grad_expert_gate,
        grad_expert_up,
        grad_expert_down,
    )


def solution(mesh):
    tokens = ("dp", "expert")
    return jax.shard_map(
        per_device,
        mesh=mesh,
        in_specs=(
            P(tokens, None),
            P(tokens),
            P(tokens, None),
            P(),
            P(None, "tensor"),
            P("tensor", None),
            P(None, "tensor"),
            P("tensor", None),
            P(None, "tensor"),
            P("tensor", None),
            P("tensor", None),
            P(),
            P(),
            P(),
            P(None, "tensor"),
            P(None, "tensor"),
            P("tensor", None),
            P("expert", None, "tensor"),
            P("expert", None, "tensor"),
            P("expert", "tensor", None),
            P(tokens, None),
        ),
        out_specs=(
            P(tokens, None),
            P(tokens, None),
            P(tokens),
            P(tokens, "tensor"),
            P("tensor", tokens),
            P(tokens, "tensor"),
            P("tensor", tokens),
            P(tokens, "tensor"),
            P("tensor", tokens),
            P("tensor", tokens),
            P(tokens),
            P(tokens, None),
            P(tokens),
            P(tokens, "tensor"),
            P(tokens, "tensor"),
            P("tensor", tokens),
            P("expert", "dp", "tensor"),
            P("expert", "dp", "tensor"),
            P("expert", "tensor", "dp"),
        ),
        check_vma=False,
    )
```

```python
import functools

import jax
import jax.numpy as jnp
from jax import lax
from jax.experimental import pallas as pl
from jax.experimental.pallas import tpu as pltpu
from jax.sharding import PartitionSpec as P

HD = 128
SEQ_LEN = 4096
WINDOW = 1024
EPS = 1e-06
THETA = 1000000.0
NEG_LARGE = -1e30
QUERY_BLOCK = 256
FEED_BLOCK = 512
LANE = 128
FACT_ROWS = 16
GATHERED_PLANES = 4
F32 = jnp.float32
BF16 = jnp.bfloat16


def dot(left, right):
    return jnp.dot(left, right, preferred_element_type=F32)


def dot_nt(left, right):
    return lax.dot_general(left, right, (((1,), (1,)), ((), ())), preferred_element_type=F32)


def dot_tn(left, right):
    return lax.dot_general(left, right, (((0,), (0,)), ((), ())), preferred_element_type=F32)


def shift_pairs(count, step):
    if count & (count - 1) == 0:
        return [(source, source ^ step) for source in range(count)]
    return [(source, (source + step) % count) for source in range(count)]


def partner(index, count, step):
    if count & (count - 1) == 0:
        return index ^ step
    return (index + step) % count


def source(index, count, step):
    if count & (count - 1) == 0:
        return index ^ step
    return (index - step + count) % count


def gather_halves(own, meanwhile=()):
    groups, mine = lax.axis_size("expert"), lax.axis_index("expert")
    rows, width = own.shape
    pieces = jnp.zeros((groups * rows, width), own.dtype)
    pieces = lax.dynamic_update_slice(pieces, own, (mine * rows, 0))
    for step in range(1, groups):
        came = lax.ppermute(own, "expert", shift_pairs(groups, step))
        came = after(came, own, *meanwhile)
        pieces = lax.dynamic_update_slice(pieces, came, (source(mine, groups, step) * rows, 0))
    return pieces, swapped(pieces)


def swapped(values):
    return lax.ppermute(values, "tensor", [(0, 1), (1, 0)])


def scatter_halves(own, other, meanwhile=None):
    groups, mine = lax.axis_size("expert"), lax.axis_index("expert")
    crossed = swapped(other.astype(BF16))
    rows, width = own.shape[0] // groups, own.shape[1]

    def of_group(index):
        parts = [lax.dynamic_slice(values, (index * rows, 0), (rows, width)) for values in (own, crossed)]
        return parts[0].astype(F32) + parts[1].astype(F32)

    sent = [of_group(partner(mine, groups, step)).astype(BF16) for step in range(1, groups)]
    came = [lax.ppermute(sent[step - 1], "expert", shift_pairs(groups, step)) for step in range(1, groups)]
    result = of_group(mine)
    if meanwhile is None:
        return functools.reduce(jnp.add, [part.astype(F32) for part in came], result)
    side = meanwhile(tuple(sent))
    came = lax.optimization_barrier((tuple(came), side))[0]
    return functools.reduce(jnp.add, [part.astype(F32) for part in came], result), side


def after(value, *others):
    return lax.optimization_barrier((value, *others))[0]


def both_cores(own):
    return joined(own, swapped(own))


def joined(own, other):
    core = lax.axis_index("tensor")
    return jnp.concatenate([jnp.where(core == 0, own, other), jnp.where(core == 0, other, own)], axis=0)


def token_order(own, other, groups):
    half, width = own.shape
    both = joined(own, other).reshape(2, groups, half // groups, width)
    return both.transpose(1, 0, 2, 3).reshape(2 * half, width)


def half_order(values, groups):
    total, width = values.shape
    core = lax.axis_index("tensor")
    split = values.reshape(groups, 2, total // (2 * groups), width)
    return tuple(
        lax.dynamic_slice(split, (0, index, 0, 0), (groups, 1, total // (2 * groups), width)).reshape(-1, width)
        for index in (core, 1 - core)
    )


def norm_back(values, inv_scale, gain_vec, grad_normed):
    weighted = grad_normed * gain_vec
    inner_mean = jnp.mean(weighted * values, axis=-1, keepdims=True)
    return inv_scale * weighted - values * inv_scale * inv_scale * inv_scale * inner_mean


def masked_scores(query, keys, seg_query, seg_keys, offset):
    scores = dot_nt(query, keys) * (HD ** (-0.5))
    rows, columns = scores.shape
    distance = (
        lax.broadcasted_iota(jnp.int32, (rows, columns), 0)
        - lax.broadcasted_iota(jnp.int32, (rows, columns), 1)
        + offset
    )
    allowed = (seg_query == seg_keys) & (distance >= 0) & (distance < WINDOW)
    return jnp.where(allowed, scores, NEG_LARGE)


def key_ranges(start, block, rows):
    first_before = min(rows, max(0, (start + rows - WINDOW + 1) // block * block))
    first_own = max(0, (start - WINDOW + 1) // block * block)
    return (first_before, rows), (first_own, start + block)


def probabilities(query, parts, seg_query):
    scores = [masked_scores(query, keys, seg_query, seg_keys, offset) for keys, seg_keys, offset in parts]
    top = functools.reduce(jnp.maximum, [jnp.max(part, axis=-1, keepdims=True) for part in scores])
    expo = [jnp.exp(part - top) for part in scores]
    total = functools.reduce(jnp.add, [jnp.sum(part, axis=-1, keepdims=True) for part in expo])
    inverse = 1.0 / total
    return [part * inverse for part in expo]


def key_parts(start, block, rows, before_ref, own_ref, seg_before, seg_own):
    (before, before_end), (own, own_end) = key_ranges(start, block, rows)
    ranges = []
    if before < before_end:
        ranges.append((before_ref, seg_before, before, before_end, start + rows - before))
    ranges.append((own_ref, seg_own, own, own_end, start - own))
    parts = [(ref[low:high, :HD], seg[:, low:high], offset) for ref, seg, low, high, offset in ranges]
    values = [ref[low:high, HD:] for ref, _, low, high, _ in ranges]
    return parts, values, [(low, high) for _, _, low, high, _ in ranges]


def attend_kernel(block, q_ref, before_ref, own_ref, sq_ref, sb_ref, so_ref, out_ref):
    rows = q_ref.shape[0]
    for start in range(0, rows, block):
        parts, values, _ = key_parts(start, block, rows, before_ref, own_ref, sb_ref, so_ref)
        probs = probabilities(q_ref[start : start + block, :], parts, sq_ref[start : start + block, :])
        total = functools.reduce(
            jnp.add, [dot(part.astype(BF16), value) for part, value in zip(probs, values, strict=True)]
        )
        out_ref[start : start + block, :] = total.astype(BF16)


def attend_back_kernel(
    block, q_ref, before_ref, own_ref, sq_ref, sb_ref, so_ref, grad_ref, gq_ref, gb_ref, go_ref, back_ref
):
    rows = q_ref.shape[0]
    back_ref[...] = jnp.zeros_like(back_ref)
    go_ref[...] = jnp.zeros_like(go_ref)
    scale = HD ** (-0.5)
    for start in range(0, rows, block):
        query = q_ref[start : start + block, :]
        grad = grad_ref[start : start + block, :]
        parts, values, ranges = key_parts(start, block, rows, before_ref, own_ref, sb_ref, so_ref)
        sinks = [back_ref, go_ref][-len(parts) :]
        probs = probabilities(query, parts, sq_ref[start : start + block, :])
        grad_probs = [dot_nt(grad, value) for value in values]
        delta = functools.reduce(
            jnp.add,
            [jnp.sum(p * g, axis=-1, keepdims=True) for p, g in zip(probs, grad_probs, strict=True)],
        )
        grad_query = None
        for p, g, part, sink, (low, high) in zip(probs, grad_probs, parts, sinks, ranges, strict=True):
            grad_scores = (p * (g - delta)).astype(BF16)
            term = dot(grad_scores, part[0])
            grad_query = term if grad_query is None else grad_query + term
            sink[low:high, :HD] += dot_tn(grad_scores, query) * scale
            sink[low:high, HD:] += dot_tn(p.astype(BF16), grad)
        gq_ref[start : start + block, :] = grad_query * scale
    gb_ref[...] = back_ref[...].astype(BF16)


def attention_specs(rows):
    column = pl.BlockSpec((rows, HD), lambda h: (0, h))
    pair = pl.BlockSpec((rows, 2 * HD), lambda h: (0, h))
    seg_rows = pl.BlockSpec((rows, 1), lambda h: (0, 0))
    seg_columns = pl.BlockSpec((1, rows), lambda h: (0, 0))
    return column, pair, [column, pair, pair, seg_rows, seg_columns, seg_columns]


def attend(query, before, own, seg_rows, seg_before, seg_own):
    rows, width = query.shape
    heads = width // HD
    column, _, specs = attention_specs(rows)
    return pl.pallas_call(
        functools.partial(attend_kernel, min(QUERY_BLOCK, rows)),
        grid=(heads,),
        in_specs=specs,
        out_specs=column,
        out_shape=jax.ShapeDtypeStruct((rows, width), BF16),
        compiler_params=pltpu.CompilerParams(vmem_limit_bytes=48 * 2**20),
        cost_estimate=pl.CostEstimate(
            flops=4 * rows * WINDOW * width, bytes_accessed=12 * rows * width, transcendentals=rows * WINDOW * heads
        ),
        name="attend",
    )(query, before, own, seg_rows, seg_before, seg_own)


def attend_back(query, before, own, seg_rows, seg_before, seg_own, grad_heads):
    rows, width = query.shape
    heads = width // HD
    column, pair, specs = attention_specs(rows)
    return pl.pallas_call(
        functools.partial(attend_back_kernel, min(QUERY_BLOCK, rows)),
        grid=(heads,),
        in_specs=specs + [column],
        out_specs=[column, pair, pair],
        out_shape=[
            jax.ShapeDtypeStruct((rows, width), F32),
            jax.ShapeDtypeStruct((rows, 2 * width), BF16),
            jax.ShapeDtypeStruct((rows, 2 * width), F32),
        ],
        scratch_shapes=[pltpu.VMEM((rows, 2 * HD), F32)],
        compiler_params=pltpu.CompilerParams(vmem_limit_bytes=48 * 2**20),
        cost_estimate=pl.CostEstimate(
            flops=10 * rows * WINDOW * width, bytes_accessed=32 * rows * width, transcendentals=rows * WINDOW * heads
        ),
        name="attend_back",
    )(query, before, own, seg_rows, seg_before, seg_own, grad_heads)


def turned(values, cosine, sines):
    return values * cosine + pltpu.roll(values, HD // 2, 1) * sines


def half_rows(index, group, rows, core):
    return pl.ds(pl.multiple_of(2 * group * rows + lax.rem(core + index, 2) * rows, rows), rows)


def project_kernel(
    groups, place_ref, own_ref, other_ref, wq_ref, wk_ref, wv_ref, bias_ref, cos_ref, sin_ref, q_ref, kv_ref
):
    core = place_ref[1]
    half, width = own_ref.shape[0], wq_ref.shape[1]
    rows = half // groups
    for index, ref in enumerate((own_ref, other_ref)):
        here = slice(index * half, (index + 1) * half)
        cosine, sines = cos_ref[here, :], sin_ref[here, :]
        normed = ref[...]
        for k, weight in enumerate((wq_ref, wk_ref, wv_ref)):
            product = dot(normed, weight[...]) + bias_ref[k : k + 1, :].astype(F32)
            for h in range(width // HD):
                values = product[:, h * HD : (h + 1) * HD]
                if k < 2:
                    values = turned(values, cosine, sines)
                values = values.astype(BF16)
                out, at = (q_ref, h * HD) if k == 0 else (kv_ref, (2 * h + k - 1) * HD)
                for group in range(groups):
                    out[half_rows(index, group, rows, core), at : at + HD] = values[group * rows : (group + 1) * rows]


def project(place, halves, weights, bias, cosine, sines, groups):
    half, model_width = halves[0].shape
    width = weights[0].shape[1] // groups
    whole = pl.BlockSpec((half, model_width), lambda i, p: (0, 0))
    weight_spec = pl.BlockSpec((model_width, width), lambda i, p: (0, p[0]))
    table = pl.BlockSpec((2 * half, HD), lambda i, p: (0, 0))
    return pl.pallas_call(
        functools.partial(project_kernel, groups),
        grid_spec=pltpu.PrefetchScalarGridSpec(
            num_scalar_prefetch=1,
            grid=(1,),
            in_specs=[whole, whole]
            + [weight_spec] * 3
            + [pl.BlockSpec((3, width), lambda i, p: (0, p[0])), table, table],
            out_specs=[
                pl.BlockSpec((2 * half, width), lambda i, p: (0, 0)),
                pl.BlockSpec((2 * half, 2 * width), lambda i, p: (0, 0)),
            ],
        ),
        out_shape=[
            jax.ShapeDtypeStruct((2 * half, width), BF16),
            jax.ShapeDtypeStruct((2 * half, 2 * width), BF16),
        ],
        compiler_params=pltpu.CompilerParams(vmem_limit_bytes=48 * 2**20),
        cost_estimate=pl.CostEstimate(
            flops=12 * half * model_width * width,
            bytes_accessed=4 * half * model_width + 6 * model_width * width,
            transcendentals=0,
        ),
        name="project",
    )(place, *halves, *weights, bias, cosine, sines)


def project_back_kernel(
    groups,
    place_ref,
    gq_ref,
    go_ref,
    came_ref,
    wq_ref,
    wk_ref,
    wv_ref,
    cos_ref,
    sin_ref,
    own_ref,
    other_ref,
    own_part,
    other_part,
    bias_ref,
):
    core = place_ref[1]
    half, width = own_ref.shape[0], gq_ref.shape[1]
    rows = half // groups
    columns = min(512, own_part.shape[1])
    bias_sum = jnp.zeros((1, 3 * width), F32)
    for index, (out, part) in enumerate(((own_ref, own_part), (other_ref, other_part))):
        here = slice(index * half, (index + 1) * half)
        cosine, sines = cos_ref[here, :], sin_ref[here, :]
        for k in range(3):
            for h in range(width // HD):
                pieces = []
                for group in range(groups):
                    at_rows = half_rows(index, group, rows, core)
                    if k == 0:
                        pieces.append(gq_ref[at_rows, h * HD : (h + 1) * HD])
                    else:
                        at = (2 * h + k - 1) * HD
                        pieces.append(go_ref[at_rows, at : at + HD] + came_ref[at_rows, at : at + HD].astype(F32))
                values = jnp.concatenate(pieces, axis=0)
                if k < 2:
                    values = turned(values, cosine, -sines)
                out[:, k * width + h * HD : k * width + (h + 1) * HD] = values.astype(BF16)
        grads = out[...]
        bias_sum = bias_sum + jnp.sum(grads.astype(F32), axis=0, keepdims=True)
        for at in range(0, part.shape[1], columns):
            total = dot_nt(grads[:, :width], wq_ref[at : at + columns, :])
            total = total + dot_nt(grads[:, width : 2 * width], wk_ref[at : at + columns, :])
            total = total + dot_nt(grads[:, 2 * width :], wv_ref[at : at + columns, :])
            part[:, at : at + columns] = total.astype(BF16)
    bias_ref[...] = jnp.broadcast_to(bias_sum, bias_ref.shape)


def project_back(place, grad_query, own_kv_grad, came_kv, weights, cosine, sines, groups):
    total, width = grad_query.shape
    half = total // 2
    model_width = weights[0].shape[0]
    weight_spec = pl.BlockSpec((model_width, width), lambda i, p: (0, p[0]))

    def full(*shape):
        return pl.BlockSpec(shape, lambda i, p: (0, 0))

    return pl.pallas_call(
        functools.partial(project_back_kernel, groups),
        grid_spec=pltpu.PrefetchScalarGridSpec(
            num_scalar_prefetch=1,
            grid=(1,),
            in_specs=[full(total, width), full(total, 2 * width), full(total, 2 * width)]
            + [weight_spec] * 3
            + [full(total, HD)] * 2,
            out_specs=[full(half, 3 * width)] * 2 + [full(half, model_width)] * 2 + [full(8, 3 * width)],
        ),
        out_shape=[jax.ShapeDtypeStruct((half, 3 * width), BF16)] * 2
        + [jax.ShapeDtypeStruct((half, model_width), BF16)] * 2
        + [jax.ShapeDtypeStruct((8, 3 * width), F32)],
        compiler_params=pltpu.CompilerParams(vmem_limit_bytes=48 * 2**20),
        cost_estimate=pl.CostEstimate(
            flops=12 * half * model_width * width,
            bytes_accessed=8 * half * model_width + 6 * model_width * width,
            transcendentals=0,
        ),
        name="project_back",
    )(place, grad_query, own_kv_grad, came_kv, *weights, cosine, sines)


def projection_grads_kernel(n0, n1, d0, d1, g0, g1, a0, a1, out_ref):
    width = g0.shape[1]
    out_ref[:, :width] = (dot_tn(n0[...], g0[...]) + dot_tn(n1[...], g1[...])).astype(BF16)
    out_ref[:, width:] = (dot_tn(d0[...], a0[...]) + dot_tn(d1[...], a1[...])).astype(BF16)


def projection_grads(normed, grads_after, grads, attended):
    half, model_width = normed[0].shape
    width = grads[0].shape[1] + attended[0].shape[1]
    tile = min(512, model_width)
    wide = pl.BlockSpec((half, tile), lambda i: (0, i))
    return pl.pallas_call(
        projection_grads_kernel,
        grid=(model_width // tile,),
        in_specs=[wide] * 4
        + [pl.BlockSpec(grads[0].shape, lambda i: (0, 0))] * 2
        + [pl.BlockSpec(attended[0].shape, lambda i: (0, 0))] * 2,
        out_specs=pl.BlockSpec((tile, width), lambda i: (i, 0)),
        out_shape=jax.ShapeDtypeStruct((model_width, width), BF16),
        compiler_params=pltpu.CompilerParams(vmem_limit_bytes=40 * 2**20),
        cost_estimate=pl.CostEstimate(
            flops=4 * half * model_width * width, bytes_accessed=8 * half * model_width, transcendentals=0
        ),
        name="projection_grads",
    )(*normed, *grads_after, *grads, *attended)


def hidden_grads(rows, top, gate, weight_gu, weight_down):
    hidden = weight_down.shape[0]
    both = dot_nt(rows, weight_gu)
    inner_grad = dot_nt(top, weight_down)
    gate_val, up_val = both[:, :hidden], both[:, hidden:]
    sigmoid_val = jax.nn.sigmoid(gate_val)
    silu_val = gate_val * sigmoid_val
    inner = silu_val * up_val
    slope = jnp.sum(inner * inner_grad, axis=-1, keepdims=True)
    inner_grad = inner_grad * gate
    gated = (inner * gate).astype(BF16)
    grad_gate_val = (inner_grad * up_val * (sigmoid_val + silu_val * (1.0 - sigmoid_val))).astype(BF16)
    grad_up_val = (inner_grad * silu_val).astype(BF16)
    return gated, grad_gate_val, grad_up_val, slope


def gate_of(gates, block):
    lane = lax.broadcasted_iota(jnp.int32, gates.shape, 1)
    return jnp.sum(jnp.where(lane == block, gates, 0.0), axis=1, keepdims=True)


def feed_kernel(
    first_ref, own_ref, other_ref, top_own, top_other, gates_ref, gu_ref, down_ref, gated_ref, grad_ref, slope_ref
):
    del first_ref
    hidden = down_ref.shape[0]
    half = own_ref.shape[0]
    for index, (rows, top) in enumerate(((own_ref, top_own), (other_ref, top_other))):
        here = slice(index * half, (index + 1) * half)
        gate = gate_of(gates_ref[here, :], pl.program_id(0))
        gated, grad_gate_val, grad_up_val, slope = hidden_grads(rows[...], top[...], gate, gu_ref[...], down_ref[...])
        gated_ref[here, :] = gated
        grad_ref[here, :hidden] = grad_gate_val
        grad_ref[here, hidden:] = grad_up_val
        slope_ref[0, here] = slope


def weight_kernel(
    routed,
    hidden_out,
    chunk_ref,
    rows_ref,
    top_ref,
    rows_t_ref,
    top_t_ref,
    gates_ref,
    gu_ref,
    down_ref,
    gu_in,
    down_in,
    *rest,
):
    del chunk_ref
    sums = rest[-3:]
    gate_sum, up_sum, down_sum = sums
    hidden = down_ref.shape[0]
    step = pl.program_id(0)

    @pl.when(step == 0)
    def _():
        gate_sum[...] = gu_in[:, :hidden]
        up_sum[...] = gu_in[:, hidden:]
        down_sum[...] = down_in[...]

    gate = gate_of(gates_ref[...], routed)
    gated, grad_gate_val, grad_up_val, _ = hidden_grads(
        rows_ref[...], top_ref[...], gate, gu_ref[...], down_ref[...]
    )
    gate_sum[...] += dot(rows_t_ref[...], grad_gate_val)
    up_sum[...] += dot(rows_t_ref[...], grad_up_val)
    down_sum[...] += dot(top_t_ref[...], gated)

    @pl.when(step == pl.num_programs(0) - 1)
    def _():
        if len(rest[-4].shape) == 3:
            for out, total in zip(rest[-6:-3], sums, strict=True):
                out[0] = total[...].T[:hidden_out]
        else:
            out = rest[-4]
            groups, _, part = out.shape[:3]
            for g in range(groups):
                for k, total in enumerate(sums):
                    out[g, k] = total[g * part : (g + 1) * part, :].astype(BF16)


def pack_kernel(local, hidden, units, window_ref, *refs):
    gate_ref, up_ref, down_ref = refs[:3]
    shared_gate, shared_up = refs[3 : 3 + units], refs[3 + units : 3 + 2 * units]
    shared_down = refs[3 + 2 * units : 3 + 3 * units]
    gu_out, down_out = refs[-2:]
    padded = units * LANE
    columns = down_out.shape[1]
    for e in range(local):
        for ref, out, at in ((gate_ref, gu_out, 2 * e), (up_ref, gu_out, 2 * e + 1), (down_ref, down_out, e)):
            out[at * padded : at * padded + hidden, :] = ref[e]
            if hidden < padded:
                out[at * padded + hidden : (at + 1) * padded, :] = jnp.zeros((padded - hidden, columns), BF16)
    skip = window_ref[1]
    for k in range(units):
        line = lax.broadcasted_iota(jnp.int32, (LANE, columns), 0) + k * LANE
        keep = (line >= skip) & (line < skip + hidden)
        for block, out, at in (
            (shared_gate[k][...].T, gu_out, 2 * local),
            (shared_up[k][...].T, gu_out, 2 * local + 1),
            (shared_down[k][...], down_out, local),
        ):
            out[at * padded + k * LANE : at * padded + (k + 1) * LANE, :] = jnp.where(
                keep, block.astype(F32), 0.0
            ).astype(BF16)


def pack_weights(window, expert_gate, expert_up, expert_down, shared_gate, shared_up, shared_down, padded):
    local, hidden, model_width = expert_down.shape
    units = padded // LANE
    blocks = local + 1
    tile = min(256, model_width)
    expert_spec = pl.BlockSpec((local, hidden, tile), lambda i, w: (0, 0, i))
    column_specs = [pl.BlockSpec((tile, LANE), lambda i, w, k=k: (i, w[0] + k)) for k in range(units)]
    row_specs = [pl.BlockSpec((LANE, tile), lambda i, w, k=k: (w[0] + k, i)) for k in range(units)]
    return pl.pallas_call(
        functools.partial(pack_kernel, local, hidden, units),
        grid_spec=pltpu.PrefetchScalarGridSpec(
            num_scalar_prefetch=1,
            grid=(model_width // tile,),
            in_specs=[expert_spec] * 3 + column_specs * 2 + row_specs,
            out_specs=[
                pl.BlockSpec((2 * blocks * padded, tile), lambda i, w: (0, i)),
                pl.BlockSpec((blocks * padded, tile), lambda i, w: (0, i)),
            ],
        ),
        out_shape=[
            jax.ShapeDtypeStruct((2 * blocks * padded, model_width), BF16),
            jax.ShapeDtypeStruct((blocks * padded, model_width), BF16),
        ],
        compiler_params=pltpu.CompilerParams(vmem_limit_bytes=40 * 2**20),
        cost_estimate=pl.CostEstimate(
            flops=0, bytes_accessed=12 * blocks * padded * model_width, transcendentals=0
        ),
        name="pack_weights",
    )(
        window,
        jnp.swapaxes(expert_gate, 1, 2),
        jnp.swapaxes(expert_up, 1, 2),
        expert_down,
        *([shared_gate] * units),
        *([shared_up] * units),
        *([shared_down] * units),
    )


def turn_kernel(plane_ref, part_ref, out_ref):
    del plane_ref
    out_ref[...] = part_ref[...].T


def turn(plane, values, part):
    total = values.shape[0]
    tile = min(1024, total)
    return pl.pallas_call(
        turn_kernel,
        grid_spec=pltpu.PrefetchScalarGridSpec(
            num_scalar_prefetch=1,
            grid=(total // tile,),
            in_specs=[pl.BlockSpec((tile, part), lambda i, p: (i, p[0]))],
            out_specs=pl.BlockSpec((part, tile), lambda i, p: (0, i)),
        ),
        out_shape=jax.ShapeDtypeStruct((part, total), BF16),
        compiler_params=pltpu.CompilerParams(vmem_limit_bytes=40 * 2**20),
        cost_estimate=pl.CostEstimate(flops=0, bytes_accessed=4 * total * part, transcendentals=0),
        name="turn",
    )(plane, values)


def feed(first_tiles, halves, top_all, gates, weight_gu, weight_down, blocks):
    half, model_width = halves[0].shape
    hidden = weight_down.shape[0] // blocks
    whole = 2 * half
    rows = pl.BlockSpec((half, model_width), lambda s, c: (0, 0))
    grid_spec = pltpu.PrefetchScalarGridSpec(
        num_scalar_prefetch=1,
        grid=(blocks,),
        in_specs=[rows, rows]
        + [pl.BlockSpec((half, model_width), lambda s, c, k=k: (c[k], 0)) for k in range(2)]
        + [
            pl.BlockSpec(gates.shape, lambda s, c: (0, 0)),
            pl.BlockSpec((2 * hidden, model_width), lambda s, c: (s, 0)),
            pl.BlockSpec((hidden, model_width), lambda s, c: (s, 0)),
        ],
        out_specs=[
            pl.BlockSpec((whole, hidden), lambda s, c: (0, s)),
            pl.BlockSpec((whole, 2 * hidden), lambda s, c: (0, s)),
            pl.BlockSpec((1, whole, 1), lambda s, c: (s, 0, 0)),
        ],
    )
    return pl.pallas_call(
        feed_kernel,
        grid_spec=grid_spec,
        out_shape=[
            jax.ShapeDtypeStruct((whole, blocks * hidden), BF16),
            jax.ShapeDtypeStruct((whole, 2 * blocks * hidden), BF16),
            jax.ShapeDtypeStruct((blocks, whole, 1), F32),
        ],
        compiler_params=pltpu.CompilerParams(vmem_limit_bytes=62 * 2**20),
        cost_estimate=pl.CostEstimate(
            flops=6 * whole * model_width * hidden * blocks,
            bytes_accessed=6 * model_width * hidden * blocks + 4 * whole * model_width,
            transcendentals=whole * hidden * blocks,
        ),
        name="feed",
    )(first_tiles, *halves, top_all, top_all, gates, weight_gu, weight_down)


def weight_grads(plane, planes, block, rows_all, top_all, rows_t, top_t, gates, packed, sums, outs, groups, hidden):
    weight_gu, weight_down = packed
    total, model_width = rows_all.shape
    count = total // planes
    part = rows_t.shape[0]
    padded = sums[1].shape[1]
    tile = min(FEED_BLOCK, count // 2)
    steps = count // tile
    local = outs[0] if isinstance(outs[0], int) else outs[0].shape[0]

    half_steps = max(1, steps // 2)

    def at(i, c):
        place = lax.rem(i, steps)
        half = lax.rem(place // half_steps + c[1], 2)
        return lax.rem(c[0] + 1 + i // steps, planes) * steps + half * half_steps + lax.rem(place, half_steps)

    tokens = pl.BlockSpec((tile, model_width), lambda i, c: (at(i, c), 0))
    turned = pl.BlockSpec((part, tile), lambda i, c: (0, at(i, c)))
    in_specs = [
        tokens,
        tokens,
        turned,
        turned,
        pl.BlockSpec(
            (tile, gates.shape[1]),
            lambda i, c: (lax.rem(c[0] + 1 + i // steps, planes) * steps + lax.rem(i, steps), 0),
        ),
        pl.BlockSpec((2 * padded, model_width), lambda i, c: (block, 0)),
        pl.BlockSpec((padded, model_width), lambda i, c: (block, 0)),
        pl.BlockSpec((part, 2 * padded), lambda i, c: (0, 0)),
        pl.BlockSpec((part, padded), lambda i, c: (0, 0)),
    ]
    args = [rows_all, top_all, rows_t, top_t, gates, weight_gu, weight_down, *sums]
    aliases = {}
    if block < local:
        out_shape = [jax.ShapeDtypeStruct((local, hidden, part), F32)] * 3
        out_specs = [pl.BlockSpec((1, hidden, part), lambda i, c: (block, 0, 0))] * 3
        if not isinstance(outs[0], int):
            in_specs += [pl.BlockSpec(memory_space=pl.ANY)] * 3
            aliases = {len(args) + 1 + k: k for k in range(3)}
            args += list(outs)
    else:
        out_shape = [jax.ShapeDtypeStruct((groups, 3, part // groups, padded), BF16)]
        out_specs = [pl.BlockSpec(out_shape[0].shape, lambda i, c: (0, 0, 0, 0))]
    return pl.pallas_call(
        functools.partial(weight_kernel, block, hidden),
        grid_spec=pltpu.PrefetchScalarGridSpec(
            num_scalar_prefetch=1,
            grid=((planes - 1) * steps,),
            in_specs=in_specs,
            out_specs=out_specs,
            scratch_shapes=[pltpu.VMEM((part, padded), F32)] * 3,
        ),
        out_shape=out_shape,
        input_output_aliases=aliases,
        compiler_params=pltpu.CompilerParams(vmem_limit_bytes=62 * 2**20),
        cost_estimate=pl.CostEstimate(
            flops=6 * (total - count) * (model_width + part) * padded,
            bytes_accessed=6 * model_width * padded + 4 * total * model_width,
            transcendentals=total * padded,
        ),
        name="weight_grads",
    )(plane, *args)


def per_device(
    tokens,
    segments,
    routes,
    attn_gain,
    query_weight,
    query_bias,
    key_weight,
    key_bias,
    value_weight,
    value_bias,
    out_weight,
    mlp_gain,
    router_weight,
    shared_router,
    shared_gate,
    shared_up,
    shared_down,
    expert_gate,
    expert_up,
    expert_down,
    grad_out,
):
    tok_rows, model_width = tokens.shape
    groups, cores = lax.axis_size("expert"), lax.axis_size("tensor")
    planes = lax.axis_size("dp")
    mine, core, plane = lax.axis_index("expert"), lax.axis_index("tensor"), lax.axis_index("dp")
    rows = tok_rows // cores
    plane_rows = tok_rows * groups
    heads_here = query_weight.shape[1] // HD
    width = query_weight.shape[1] // groups
    heads = width // HD
    local_experts, _, hidden = expert_gate.shape
    expert_count = local_experts * groups
    blocks = local_experts + 1
    gathered = planes <= GATHERED_PLANES
    padded = -(-hidden // LANE) * LANE
    part_rows = model_width // planes

    first_unit = mine * hidden // LANE
    window = jnp.stack([first_unit, mine * hidden - first_unit * LANE]).astype(jnp.int32)
    weight_gu, weight_down = pack_weights(
        window, expert_gate, expert_up, expert_down, shared_gate, shared_up, shared_down, padded
    )

    half = plane_rows // 2
    slot = jnp.arange(plane_rows, dtype=jnp.int32)
    half_core = (core + slot // half) % 2
    row_index = plane * plane_rows + slot % half // rows * tok_rows + half_core * rows + slot % rows
    places = (row_index % SEQ_LEN).astype(F32)
    frequency = THETA ** (-2.0 * jnp.arange(HD // 2, dtype=F32) / HD)
    angles = places[:, None] * jnp.concatenate([frequency, frequency])[None, :]
    cosine = jnp.cos(angles)
    sines = jnp.sin(angles) * jnp.where(jnp.arange(HD) < HD // 2, -1.0, 1.0)[None, :]

    own_tokens = lax.dynamic_slice(tokens, (core * rows, 0), (rows, model_width))
    inputs = own_tokens.astype(F32)
    gain_one = attn_gain.astype(F32)
    scale_one = lax.rsqrt(jnp.mean(inputs * inputs, axis=-1, keepdims=True) + EPS)
    normed_one = gather_halves((inputs * scale_one * gain_one).astype(BF16), (weight_gu, weight_down, cosine, sines))
    grad_top_own = lax.dynamic_slice(grad_out, (core * rows, 0), (rows, model_width))
    top_axes = ("dp", "tensor", "expert") if gathered else ("tensor", "expert")
    grad_top_all = lax.all_gather(grad_top_own, top_axes, axis=0, tiled=True)

    picks = jnp.sum(1 << routes, axis=1)
    facts_own = jnp.zeros((FACT_ROWS, tok_rows), BF16)
    facts_own = facts_own.at[0].set(segments.astype(BF16)).at[1].set(picks.astype(BF16))
    facts = jnp.zeros((groups, FACT_ROWS, tok_rows), BF16)
    facts = lax.dynamic_update_slice(facts, facts_own[None], (mine, 0, 0))
    for step in range(1, groups):
        came = lax.ppermute(facts_own, "expert", shift_pairs(groups, step))
        facts = lax.dynamic_update_slice(facts, came[None], (source(mine, groups, step), 0, 0))
    facts = facts.transpose(1, 0, 2).reshape(FACT_ROWS, plane_rows)
    upward = [(i, i + 1) for i in range(planes - 1)]
    seg_own = facts[:1].astype(F32)
    seg_before = jnp.where(plane > 0, lax.ppermute(facts, "dp", upward)[:1].astype(F32), -1.0)
    seg_rows = seg_own.reshape(plane_rows, 1)
    bits = jnp.concatenate(half_order(facts[1].reshape(plane_rows, 1), groups), axis=0).astype(jnp.int32)

    place = jnp.stack([mine, core]).astype(jnp.int32)
    weights_in = (query_weight, key_weight, value_weight)
    bias_in = jnp.stack([bias.reshape(-1) for bias in (query_bias, key_bias, value_bias)])
    query_rot, own_kv = project(place, normed_one, weights_in, bias_in, cosine, sines, groups)
    before_kv = lax.ppermute(own_kv, "dp", upward)
    attended = half_order(attend(query_rot, before_kv, own_kv, seg_rows, seg_before, seg_own), groups)
    out_rows = lax.dynamic_slice(out_weight, (mine * width, 0), (width, model_width))
    after_attn = inputs + scatter_halves(*(dot(half, out_rows) for half in attended))

    gain_two = mlp_gain.astype(F32)
    scale_two = lax.rsqrt(jnp.mean(after_attn * after_attn, axis=-1, keepdims=True) + EPS)
    normed_own = (after_attn * scale_two * gain_two).astype(BF16)
    normed_two = gather_halves(normed_own)
    if gathered:
        normed_all = lax.all_gather(after(normed_own, normed_two[0]), ("dp", "tensor", "expert"), axis=0, tiled=True)
    gate_columns = jnp.concatenate([router_weight, shared_router[:, None]], axis=1)
    first_tile = 2 * plane if gathered else jnp.zeros_like(plane)
    top_tiles = jnp.stack([first_tile + (core + k) % 2 for k in range(2)]).astype(jnp.int32)
    half_gates, half_probs = [], []
    for index in range(2):
        logits = dot(normed_two[index], gate_columns)
        chosen = (
            (bits[index * half : (index + 1) * half] >> jnp.arange(expert_count, dtype=jnp.int32)[None, :]) & 1
        ).astype(F32)
        probs = jax.nn.softmax(logits[:, :expert_count], axis=-1)
        named = lax.dynamic_slice(probs * chosen, (0, mine * local_experts), (half, local_experts))
        half_gates.append(jnp.concatenate([named, jax.nn.sigmoid(logits[:, expert_count:])], axis=1))
        half_probs.append((probs, chosen))
    gates = jnp.concatenate(half_gates, axis=0)
    gated, grad_hidden, slopes = feed(
        top_tiles, normed_two, grad_top_all, gates, weight_gu, weight_down, blocks
    )
    router_probs, chosen = (jnp.concatenate(parts, axis=0) for parts in zip(*half_probs, strict=True))

    shared_mix = gates[:, local_experts:]
    own_slopes = jnp.concatenate([slopes[e] for e in range(local_experts)], axis=1)
    all_slopes = lax.dynamic_update_slice(
        jnp.zeros((plane_rows, expert_count), F32), own_slopes, (0, mine * local_experts)
    ) * chosen
    grad_logits = router_probs * (all_slopes - jnp.sum(router_probs * all_slopes, axis=-1, keepdims=True))
    grad_shared_logit = slopes[local_experts] * shared_mix * (1.0 - shared_mix)
    grad_small = jnp.concatenate([grad_logits, grad_shared_logit], axis=1).astype(BF16)
    grad_normed_part = (dot(grad_hidden, weight_gu) + dot_nt(grad_small, gate_columns)).astype(BF16)
    own_part = jnp.concatenate(
        [lax.dynamic_slice(part, (0, plane * part_rows), (half, part_rows)) for part in normed_two], axis=0
    )

    def mix_meanwhile(token):
        values, grads = after((gated, grad_hidden), token)
        in_order = [lax.dynamic_slice(values, ((core + k) % 2 * half, 0), (half, values.shape[1])) for k in range(2)]
        mixed_part = dot(jnp.concatenate(in_order, axis=0), weight_down).astype(BF16)
        first_sums = [dot_tn(own_part, block_grads(grads, b)) for b in range(1, blocks)] if gathered else []
        return mixed_part, first_sums

    def block_grads(grads, block):
        return grads[:, 2 * block * padded : 2 * (block + 1) * padded]

    grad_normed_two, (mixed_part, first_sums) = scatter_halves(
        grad_normed_part[:half], grad_normed_part[half:], mix_meanwhile
    )
    mixed = lax.psum_scatter(
        after(mixed_part, grad_normed_two), ("tensor", "expert"), scatter_dimension=0, tiled=True
    )
    out = both_cores((after_attn + mixed.astype(F32)).astype(BF16))
    grad_columns = functools.reduce(
        jnp.add, [dot_tn(normed_two[k], grad_small[k * half : (k + 1) * half]) for k in range(2)]
    )

    grad_mlp_gain = jnp.sum(grad_normed_two * after_attn * scale_two, axis=0)
    grad_after = grad_top_own.astype(F32) + norm_back(after_attn, scale_two, gain_two, grad_normed_two)

    plane_number = jnp.stack([plane, core]).astype(jnp.int32)
    grad_sent = grad_after.astype(BF16)
    values, grads, top_all = after((gated, grad_hidden, grad_top_all), grad_sent)
    own_sums = []
    if gathered:
        top_t = turn(plane_number, top_all, part_rows)
        own_top_t = jnp.concatenate(
            [
                lax.dynamic_slice(top_t, (0, (2 * plane + (core + k) % 2) * half), (part_rows, half))
                for k in range(2)
            ],
            axis=1,
        )
        first_sums = [dot_tn(own_part, block_grads(grads, 0)), *first_sums]
        own_sums = [
            (first_sums[b], dot(own_top_t, values[:, b * padded : (b + 1) * padded])) for b in range(blocks)
        ]
    grad_attended = gather_halves(grad_sent, tuple(own_sums))
    grad_heads = token_order(*(dot_nt(part, out_rows).astype(BF16) for part in grad_attended), groups)
    grad_query_rot, back_kv, own_kv_grad = attend_back(
        query_rot, before_kv, own_kv, seg_rows, seg_before, seg_own, grad_heads
    )

    small_rows = part_rows // groups

    def to_owners(values):
        return lax.all_to_all(values, "expert", 0, 0)

    def placed(pieces):
        total = None
        for j in range(groups):
            at = j * hidden // LANE * LANE
            piece = jnp.pad(pieces[j].astype(F32), [(0, 0), (at, groups * hidden - at - padded)])
            total = piece if total is None else total + piece
        return total

    if gathered:
        gates_sent = after(
            jnp.pad(gates.T, [(0, -gates.shape[1] % 8), (0, 0)]), back_kv
        )
        gates_came = lax.all_to_all(jnp.broadcast_to(gates_sent[None], (planes, *gates_sent.shape)), "dp", 0, 0)
        normed_all = after(normed_all, back_kv)
        rows_t = turn(plane_number, normed_all, part_rows)
        gates_all = gates_came.transpose(0, 2, 1).reshape(planes * plane_rows, -1)

        def weight_sums(block, outs, *tokens):
            return weight_grads(
                plane_number,
                planes,
                block,
                after(normed_all, *tokens),
                grad_top_all,
                rows_t,
                top_t,
                gates_all,
                (weight_gu, weight_down),
                own_sums[block],
                outs,
                groups,
                hidden,
            )

        shared_grads = weight_sums(local_experts, (local_experts,), back_kv)[0]
        shared_grads_token = shared_grads
    else:
        top_half = grad_top_all.reshape(2, half, model_width)
        top_here = jnp.concatenate(
            [lax.dynamic_slice(top_half, ((core + k) % 2, 0, 0), (1, half, model_width))[0] for k in range(2)], axis=0
        )
        gu_part = lax.psum_scatter(
            dot_tn(jnp.concatenate(normed_two, axis=0), grad_hidden).astype(BF16),
            "dp",
            scatter_dimension=0,
            tiled=True,
        )
        down_part = lax.psum_scatter(dot_tn(top_here, gated).astype(BF16), "dp", scatter_dimension=0, tiled=True)

        def block_of(values, index, size):
            return values[:, index * padded : index * padded + size]

        shared_grads = jnp.stack(
            [
                block_of(values, index, padded).reshape(groups, small_rows, padded)
                for values, index in (
                    (gu_part, 2 * local_experts),
                    (gu_part, 2 * local_experts + 1),
                    (down_part, local_experts),
                )
            ],
            axis=1,
        )
    shared_grads = to_owners(shared_grads)
    came_kv = lax.ppermute(back_kv, "dp", [(i + 1, i) for i in range(planes - 1)])
    if gathered:
        came_kv = after(came_kv, shared_grads_token)
    *grad_qkv, own_one_part, other_one_part, bias_sums = project_back(
        place, grad_query_rot, own_kv_grad, came_kv, weights_in, cosine, sines, groups
    )
    grad_part = projection_grads(normed_one, grad_attended, grad_qkv, attended)
    def attn_gain_of(grads):
        return jnp.sum(grads * inputs * scale_one, axis=0)

    weight_sum = lax.psum_scatter(grad_part, "dp", scatter_dimension=0, tiled=True)
    weight_sum = weight_sum.reshape(groups, small_rows, 4, width)
    if gathered:
        expert_grads = (local_experts,)
        for e in range(local_experts - 2):
            expert_grads = weight_sums(e, expert_grads, grad_part)
        grad_normed_one, expert_grads = scatter_halves(
            own_one_part,
            other_one_part,
            lambda token: weight_sums(local_experts - 2, expert_grads, token, grad_part),
        )
        shared_grads, grad_attn_gain = after((shared_grads, attn_gain_of(grad_normed_one)), expert_grads)
    else:
        grad_normed_one = scatter_halves(own_one_part, other_one_part)
        grad_attn_gain = attn_gain_of(grad_normed_one)
    grad_shared_gate = placed(shared_grads[:, 0])
    grad_shared_up = placed(shared_grads[:, 1])
    grad_shared_down = placed(shared_grads[:, 2]).T
    grad_own = grad_after + norm_back(inputs, scale_one, gain_one, grad_normed_one)
    if gathered:
        expert_grads = weight_sums(local_experts - 1, expert_grads, grad_own, weight_sum)
    else:
        expert_grads = [
            jnp.stack([block_of(values, first + stride * e, hidden).T for e in range(local_experts)]).astype(F32)
            for values, first, stride in ((gu_part, 0, 2), (gu_part, 1, 2), (down_part, 0, 1))
        ]
    grad_expert_gate, grad_expert_up = (jnp.swapaxes(grad, 1, 2) for grad in expert_grads[:2])
    grad_expert_down = expert_grads[2]
    grad_tokens = both_cores(grad_own)

    weight_rows = (
        to_owners(weight_sum).transpose(2, 1, 0, 3).reshape(4, small_rows, groups * width).astype(F32)
    )
    qkv_rows = weight_rows[:3]
    grad_out_weight = weight_rows[3].T

    bias_sums = bias_sums[0].reshape(1, 3, heads, HD)
    bias_table = lax.dynamic_update_slice(
        jnp.zeros((cores, 3, heads_here, HD), F32), bias_sums, (core, 0, mine * heads, 0)
    )
    devices = planes * groups
    spread = jnp.concatenate(
        [
            grad_attn_gain.reshape(devices, -1),
            grad_mlp_gain.reshape(devices, -1),
            grad_columns.reshape(devices, -1),
            bias_table.reshape(cores * 3 * heads_here, devices, HD // devices).transpose(1, 0, 2).reshape(devices, -1),
        ],
        axis=1,
    )
    sums = jnp.sum(lax.all_to_all(spread, ("dp", "expert"), 0, 0, tiled=True), axis=0, keepdims=True)
    sums = lax.psum(sums, "tensor")[0] if cores != 2 else (sums + lax.ppermute(sums, "tensor", [(0, 1), (1, 0)]))[0]
    gain_part = model_width // devices
    grad_attn_gain, grad_mlp_gain = sums[:gain_part], sums[gain_part : 2 * gain_part]
    table = sums[2 * gain_part :]
    column_size = gain_part * (expert_count + 1)
    column_sums = table[:column_size].reshape(gain_part, expert_count + 1)
    bias_sums = table[column_size:].reshape(cores, 3, heads_here, HD // devices)
    bias_sums = lax.dynamic_slice(bias_sums, (core, 0, 0, 0), (1, 3, heads_here, HD // devices))[0]
    return (
        out,
        grad_tokens,
        grad_attn_gain,
        qkv_rows[0],
        bias_sums[0],
        qkv_rows[1],
        bias_sums[1],
        qkv_rows[2],
        bias_sums[2],
        grad_out_weight,
        grad_mlp_gain,
        column_sums[:, :expert_count],
        column_sums[:, expert_count],
        grad_shared_gate,
        grad_shared_up,
        grad_shared_down,
        grad_expert_gate,
        grad_expert_up,
        grad_expert_down,
    )


def solution(mesh):
    tokens = ("dp", "expert")
    return jax.shard_map(
        per_device,
        mesh=mesh,
        in_specs=(
            P(tokens, None),
            P(tokens),
            P(tokens, None),
            P(),
            P(None, "tensor"),
            P("tensor", None),
            P(None, "tensor"),
            P("tensor", None),
            P(None, "tensor"),
            P("tensor", None),
            P("tensor", None),
            P(),
            P(),
            P(),
            P(None, "tensor"),
            P(None, "tensor"),
            P("tensor", None),
            P("expert", None, "tensor"),
            P("expert", None, "tensor"),
            P("expert", "tensor", None),
            P(tokens, None),
        ),
        out_specs=(
            P(tokens, None),
            P(tokens, None),
            P(tokens),
            P(tokens, "tensor"),
            P("tensor", tokens),
            P(tokens, "tensor"),
            P("tensor", tokens),
            P(tokens, "tensor"),
            P("tensor", tokens),
            P("tensor", tokens),
            P(tokens),
            P(tokens, None),
            P(tokens),
            P(tokens, "tensor"),
            P(tokens, "tensor"),
            P("tensor", tokens),
            P("expert", "dp", "tensor"),
            P("expert", "dp", "tensor"),
            P("expert", "tensor", "dp"),
        ),
        check_vma=False,
    )
```
